32 devices in a mesh: dp: 4 (over x, core), seq: 4 (over z), rep: 2 (over y).
Axes of the slice: x: 2, y: 2, z: 4, core: 2. Of those that a mesh axis runs over, the one named last changes fastest.
Arguments:
- tokens: bfloat16 [4, 1024, 2048], P('dp', ('seq', 'rep')), may hold values from -6 to 6
- segments: int32 [4, 1024], P('dp'), may hold values from 0 to 20, as said below
- routes: int32 [4, 1024, 8], P('dp', ('seq', 'rep')), may hold values from 0 to 31, all different within a row
- priority: int32 [4, 1024], P('dp', ('seq', 'rep')), may hold values from 0 to 127, as said below
- w_query: bfloat16 [2048, 4096], P(('dp', 'seq', 'rep')), may hold values from -0.125 to 0.125
- key_matrix: bfloat16 [2048, 512], P(('dp', 'seq', 'rep')), may hold values from -0.125 to 0.125
- value_matrix: bfloat16 [2048, 512], P(('dp', 'seq', 'rep')), may hold values from -0.125 to 0.125
- w_out: bfloat16 [4096, 2048], P(('dp', 'seq', 'rep')), may hold values from -1.5 to 1.5
- w_router: bfloat16 [2048, 32], P(('dp', 'seq', 'rep')), may hold values from -0.0625 to 0.0625
- attn_gain: bfloat16 [2048], P(('dp', 'seq', 'rep')), may hold values from 0.5 to 1.5
- moe_gain: bfloat16 [2048], P(('dp', 'seq', 'rep')), may hold values from 0.5 to 1.5
- query_gain: bfloat16 [128], P(('dp', 'seq', 'rep')), may hold values from 0.5 to 1.5
- key_norm_weight: bfloat16 [128], P(('dp', 'seq', 'rep')), may hold values from 0.5 to 1.5
- w_gate_up: bfloat16 [32, 2048, 1536], P(('dp', 'seq', 'rep')), may hold values from -0.125 to 0.125
- w_down: bfloat16 [32, 768, 2048], P(('dp', 'seq', 'rep')), may hold values from -0.875 to 0.875
- cotangent: bfloat16 [4, 1024, 2048], P('dp', ('seq', 'rep')), may hold values from -6 to 6
Outputs:
- mixed: bfloat16 [4, 1024, 2048], P('dp', ('seq', 'rep'))
- input_grad: float32 [4, 1024, 2048], P('dp', ('seq', 'rep'))
- grad_query: float32 [2048, 4096], P(('dp', 'seq', 'rep'))
- grad_key: float32 [2048, 512], P(('dp', 'seq', 'rep'))
- grad_value: float32 [2048, 512], P(('dp', 'seq', 'rep'))
- grad_out: float32 [4096, 2048], P(('dp', 'seq', 'rep'))
- grad_router: float32 [2048, 32], P(('dp', 'seq', 'rep'))
- grad_attn_gain: float32 [2048], P(('dp', 'seq', 'rep'))
- grad_moe_gain: float32 [2048], P(('dp', 'seq', 'rep'))
- grad_query_gain: float32 [128], P(('dp', 'seq', 'rep'))
- grad_key_gain: float32 [128], P(('dp', 'seq', 'rep'))
- grad_gate_up: float32 [32, 2048, 1536], P(('dp', 'seq', 'rep'))
- grad_down: float32 [32, 768, 2048], P(('dp', 'seq', 'rep'))
The draws below stay inside these ranges and needn't reach their ends.
Inputs may be any that keep to these rules, and one draw needn't show every extreme that they name: `segments`: along each sequence the document numbers start at 0 and never fall; documents hold 1024 * 200 / 4096 (rounded up) to 500 tokens, except that one sequence is a single document and a sequence's last document may be shorter. `priority`: within each aligned block of 128 tokens the values are a permutation.
All inputs are finite; a program needn't handle non-finite values.
Results may differ from the reference program's by a relative error of at most 0.02.
Values may be sent and summed in bfloat16 or wider, within the bound.
No kernel may reach another device: no remote copies, remote signals or barrier semaphores. Data moves between devices by JAX's collectives and lax.ppermute only.
A program may use at most 320 MiB of HBM per device.

```python
import jax
import jax.numpy as jnp
from jax import lax

MODEL_DIM = 2048
QUERY_HEADS = 32
KEY_VALUE_HEADS = 4
HEAD_DIM = 128
FFE = 768
TOPK = 8
TOK_DEV = 128
SEQUENCE_COUNT = 4
SEQUENCE_LENGTH = 1024
TOKENS = 4096
EXPERTS = 32
CAP = 32


def draw_segments(key, part):
    key = jax.random.fold_in(key, 11)
    length_key, pick_key = jax.random.split(key)
    other_key = jax.random.fold_in(key, 5)
    shortest = (SEQUENCE_LENGTH * 200 + 4095) // 4096
    longest = SEQUENCE_LENGTH * 2000 // 4096
    pieces = SEQUENCE_LENGTH // shortest + 1
    doc_lengths = jax.random.randint(length_key, (SEQUENCE_COUNT, pieces), shortest, longest + 1)
    boundaries = jnp.cumsum(doc_lengths, axis=1)
    places = jnp.arange(SEQUENCE_LENGTH, dtype=jnp.int32)
    numbers = jnp.sum((places[None, :, None] >= boundaries[:, None, :]).astype(jnp.int32), axis=-1)
    single = jax.random.randint(pick_key, (), 0, SEQUENCE_COUNT)
    finest = (single + jax.random.randint(other_key, (), 1, SEQUENCE_COUNT)) % SEQUENCE_COUNT
    sequence_ids = jnp.arange(SEQUENCE_COUNT, dtype=jnp.int32)
    short_numbers = jnp.broadcast_to((places // shortest)[None, :], (SEQUENCE_COUNT, SEQUENCE_LENGTH))
    numbers = jnp.where(sequence_ids[:, None] == finest, short_numbers, numbers)
    return jnp.where(sequence_ids[:, None] == single, 0, numbers).astype(jnp.int32)


def draw_priority(key, part):
    key = jax.random.fold_in(key, 23)
    block_keys = jax.random.split(key, SEQUENCE_COUNT * SEQUENCE_LENGTH // TOK_DEV)
    orders = jax.vmap(lambda block_key: jax.random.permutation(block_key, TOK_DEV))(block_keys)
    return orders.reshape(SEQUENCE_COUNT, SEQUENCE_LENGTH).astype(jnp.int32)


def steps_of(stream_key, dims, cuts, low, high):
    loudness, own = 1.0, jax.random.fold_in(stream_key, 6)
    for position, parts in cuts:
        steps = jnp.exp(jax.random.uniform(jax.random.fold_in(own, position), (parts,), jnp.float32, low / len(cuts), high / len(cuts)))
        loudness = loudness * jnp.repeat(steps, dims[position] // parts).reshape([-1 if axis == position else 1 for axis in range(len(dims))])
    return loudness


def distinct(key, rows, count, top, lift):
    sequence = jax.random.permutation(jax.random.fold_in(key, 1), count)
    pull = sequence
    for power in range(3):
        pull = pull * pull // count
    pull = pull * lift // count
    lots = jax.random.randint(jax.random.fold_in(key, 2), (rows, count), 0, 4096) + pull
    holders = jax.random.permutation(jax.random.fold_in(key, 3), rows)[jnp.arange(count) % rows]
    lots = jnp.where(jnp.arange(rows)[:, None] == holders[None, :], 1 << 14, lots)
    score = lots * count + jnp.arange(count)
    return lax.top_k(score.astype(jnp.int32), top)[1].astype(jnp.int32)


def gaussian(own_key, shape, width, most, cuts=(), kind=jnp.bfloat16):
    entries = jax.random.normal(own_key, shape, jnp.float32) * width
    if len(cuts) > 0:
        entries = steps_of(own_key, shape, cuts, -0.22, 0.18) * entries
    return jnp.clip(entries, min=-most, max=most).astype(kind)


def setup_inputs(seed: int = 0) -> dict:
    streams_of = jax.random.split(jax.random.key(seed), 17)
    return {
        "tokens": gaussian(streams_of[0], (SEQUENCE_COUNT, SEQUENCE_LENGTH, MODEL_DIM), 1.0, 6.0, ((0, 4), (1, 8))),
        "segments": draw_segments(jax.random.fold_in(streams_of[16], 71), 0),
        "routes": distinct(streams_of[2], SEQUENCE_COUNT * SEQUENCE_LENGTH, EXPERTS, TOPK, 2048).reshape((SEQUENCE_COUNT, SEQUENCE_LENGTH, TOPK)),
        "priority": draw_priority(jax.random.fold_in(streams_of[16], 71), 0),
        "w_query": gaussian(streams_of[4], (MODEL_DIM, QUERY_HEADS * HEAD_DIM), MODEL_DIM ** -0.5, 0.125, ((0, 32),)),
        "key_matrix": gaussian(streams_of[5], (MODEL_DIM, KEY_VALUE_HEADS * HEAD_DIM), MODEL_DIM ** -0.5, 0.125, ((0, 32),)),
        "value_matrix": gaussian(streams_of[6], (MODEL_DIM, KEY_VALUE_HEADS * HEAD_DIM), MODEL_DIM ** -0.5, 0.125, ((0, 32),)),
        "w_out": gaussian(streams_of[7], (QUERY_HEADS * HEAD_DIM, MODEL_DIM), (QUERY_HEADS * HEAD_DIM // 256) ** -0.5, 1.5, ((0, 32),)),
        "w_router": gaussian(streams_of[8], (MODEL_DIM, EXPERTS), (4 * MODEL_DIM) ** -0.5, 0.0625, ((0, 32),)),
        "attn_gain": jnp.clip(1.0 + 0.1 * jax.random.normal(streams_of[9], (MODEL_DIM,), jnp.float32), 0.5, 1.5).astype(jnp.bfloat16),
        "moe_gain": jnp.clip(1.0 + 0.1 * jax.random.normal(streams_of[10], (MODEL_DIM,), jnp.float32), 0.5, 1.5).astype(jnp.bfloat16),
        "query_gain": jnp.clip(1.0 + 0.1 * jax.random.normal(streams_of[11], (HEAD_DIM,), jnp.float32), 0.5, 1.5).astype(jnp.bfloat16),
        "key_norm_weight": jnp.clip(1.0 + 0.1 * jax.random.normal(streams_of[12], (HEAD_DIM,), jnp.float32), 0.5, 1.5).astype(jnp.bfloat16),
        "w_gate_up": gaussian(streams_of[13], (EXPERTS, MODEL_DIM, 2 * FFE), MODEL_DIM ** -0.5, 0.125, ((0, 32),)),
        "w_down": gaussian(streams_of[14], (EXPERTS, FFE, MODEL_DIM), (FFE // 16) ** -0.5, 0.875, ((0, 32),)),
        "cotangent": gaussian(streams_of[15], (SEQUENCE_COUNT, SEQUENCE_LENGTH, MODEL_DIM), 1.0, 6.0, ((0, 4), (1, 8))),
    }


@jax.custom_vjp
def lower_bound(v):
    return lax.optimization_barrier(v.astype(jnp.bfloat16)).astype(jnp.float32)

@jax.custom_vjp
def low_back(v):
    return v

def low_keep(v):
    return (lower_bound(v), None)

def low_pass(kept, grad):
    return (grad,)

def back_keep(v):
    return (v, None)

def back_low(kept, grad):
    return (lower_bound(grad),)
lower_bound.defvjp(low_keep, low_pass)
low_back.defvjp(back_keep, back_low)
EPS = 1e-06
THETA = 1000000.0
BIG_NEG = -1e+30
HIGH = lax.Precision.HIGHEST

def norm_rows(values, gain_vector):
    return values * lax.rsqrt(lax.optimization_barrier(jnp.mean(values * values, axis=-1, keepdims=True)) + EPS) * gain_vector

def rotary_angles(positions):
    half_width = HEAD_DIM // 2
    frequency = THETA ** (-2.0 * jnp.arange(half_width, dtype=jnp.float32) / HEAD_DIM)
    angles = positions.astype(jnp.float32)[:, None] * frequency[None, :]
    return (jnp.cos(angles), jnp.sin(angles))

def rotate_heads(values, cosine_table, sine_values):
    half_width = HEAD_DIM // 2
    first_half = values[..., :half_width]
    second_half = values[..., half_width:]
    cosine_table = cosine_table[:, None, :]
    sine_values = sine_values[:, None, :]
    return jnp.concatenate([first_half * cosine_table - second_half * sine_values, second_half * cosine_table + first_half * sine_values], axis=-1)

def build_head_tensors(projected, gain_vector, head_count, cosine_table, sine_values):
    shaped = projected.reshape(projected.shape[0], head_count, HEAD_DIM)
    return rotate_heads(norm_rows(shaped, gain_vector), cosine_table, sine_values)

def attend_sequence(operands):
    queries, key_head_rows, value_head_rows, documents = operands
    rows_per_block = min(512, SEQUENCE_LENGTH)
    count_of_blocks = SEQUENCE_LENGTH // rows_per_block
    heads_per_group = QUERY_HEADS // KEY_VALUE_HEADS
    places = jnp.arange(SEQUENCE_LENGTH, dtype=jnp.int32)

    def one_block(block_input):
        query_tile_rows, query_pos = block_input
        query_doc = documents[query_pos]
        grouped_queries = query_tile_rows.reshape(rows_per_block, KEY_VALUE_HEADS, heads_per_group, HEAD_DIM)
        scores = low_back(jnp.einsum('rhgd,lhd->hgrl', grouped_queries, key_head_rows, precision=HIGH) * HEAD_DIM ** (-0.5))
        allowed = (query_doc[:, None] == documents[None, :]) & (places[None, :] <= query_pos[:, None])
        masked = jnp.where(allowed, scores, BIG_NEG)
        highest = lax.optimization_barrier(jnp.max(masked, axis=-1, keepdims=True))
        exponent = jnp.where(allowed, jnp.exp(masked - highest), 0.0)
        attend_probs = lower_bound(exponent / lax.optimization_barrier(jnp.sum(exponent, axis=-1, keepdims=True)))
        output = jnp.einsum('hgrl,lhd->rhgd', attend_probs, value_head_rows, precision=HIGH)
        return output.reshape(rows_per_block, QUERY_HEADS * HEAD_DIM)
    blocks_out = lax.map(jax.checkpoint(one_block), (queries.reshape(count_of_blocks, rows_per_block, QUERY_HEADS, HEAD_DIM), places.reshape(count_of_blocks, rows_per_block)))
    return blocks_out.reshape(SEQUENCE_LENGTH, QUERY_HEADS * HEAD_DIM)

def expert_apply(operands):
    inputs, gate_up_weights, down_weights = operands
    gate_up = low_back(jnp.dot(inputs, gate_up_weights, precision=HIGH))
    hidden = lower_bound(jax.nn.silu(gate_up[:, :FFE]) * gate_up[:, FFE:])
    return lower_bound(low_back(jnp.dot(hidden, down_weights, precision=HIGH)))

def capacity_targets(routes, priority):
    count_of_blocks = TOKENS // TOK_DEV
    choice_ids = routes.reshape(count_of_blocks, TOK_DEV, TOPK)
    priority_rank = priority.reshape(count_of_blocks, TOK_DEV)
    pick_table = (choice_ids[..., None] == jnp.arange(EXPERTS, dtype=jnp.int32)).astype(jnp.int32)
    counts = lax.optimization_barrier(jnp.sum(pick_table, axis=2))
    earlier = (priority_rank[:, None, :] < priority_rank[:, :, None]).astype(jnp.int32)
    rank_table = jnp.einsum('bts,bse->bte', earlier, counts)
    slot_index = lax.optimization_barrier(jnp.sum(pick_table * rank_table[:, :, None, :], axis=-1))
    block_ids = jnp.arange(count_of_blocks, dtype=jnp.int32)[:, None, None]
    targets = choice_ids * (count_of_blocks * CAP) + block_ids * CAP + slot_index
    return jnp.where(slot_index < CAP, targets, EXPERTS * count_of_blocks * CAP).reshape(-1)

def layer_forward(tokens, w_query, key_matrix, value_matrix, w_out, w_router, attn_gain, moe_gain, query_gain, key_norm_weight, w_gate_up, w_down, segments, routes, priority):
    expert_rows = TOKENS // TOK_DEV * CAP
    flat = tokens.reshape(TOKENS, MODEL_DIM)
    normed = lower_bound(norm_rows(flat, attn_gain))
    query_proj = low_back(jnp.dot(normed, w_query, precision=HIGH))
    projected_keys = low_back(jnp.dot(normed, key_matrix, precision=HIGH))
    projected_values = lower_bound(low_back(jnp.dot(normed, value_matrix, precision=HIGH)))
    positions = jnp.tile(jnp.arange(SEQUENCE_LENGTH, dtype=jnp.int32), SEQUENCE_COUNT)
    cosine_table, sine_values = rotary_angles(positions)
    queries = lower_bound(build_head_tensors(query_proj, query_gain, QUERY_HEADS, cosine_table, sine_values)).reshape(SEQUENCE_COUNT, SEQUENCE_LENGTH, QUERY_HEADS, HEAD_DIM)
    key_head_rows = lower_bound(build_head_tensors(projected_keys, key_norm_weight, KEY_VALUE_HEADS, cosine_table, sine_values)).reshape(SEQUENCE_COUNT, SEQUENCE_LENGTH, KEY_VALUE_HEADS, HEAD_DIM)
    value_head_rows = projected_values.reshape(SEQUENCE_COUNT, SEQUENCE_LENGTH, KEY_VALUE_HEADS, HEAD_DIM)
    attended = lax.map(attend_sequence, (queries, key_head_rows, value_head_rows, segments))
    attended = lower_bound(low_back(attended.reshape(TOKENS, QUERY_HEADS * HEAD_DIM)))
    middle = flat + low_back(jnp.dot(attended, w_out, precision=HIGH))
    routed = lower_bound(norm_rows(middle, moe_gain))
    logits = low_back(jnp.dot(routed, w_router, precision=HIGH))
    choice_ids = routes.reshape(TOKENS, TOPK)
    gate_values = jax.nn.softmax(jnp.take_along_axis(logits, choice_ids, axis=1), axis=-1)
    targets = capacity_targets(routes, priority)
    sources = jnp.full((EXPERTS * expert_rows,), TOKENS * TOPK, jnp.int32).at[targets].set(jnp.arange(TOKENS * TOPK, dtype=jnp.int32), mode='drop')
    token_of_slot = sources // TOPK
    padded = jnp.concatenate([routed, jnp.zeros((1, MODEL_DIM), jnp.float32)], axis=0)
    buffers = low_back(padded[token_of_slot]).reshape(EXPERTS, expert_rows, MODEL_DIM)
    results = lax.map(jax.checkpoint(expert_apply), (buffers, w_gate_up, w_down)).reshape(EXPERTS * expert_rows, MODEL_DIM)
    slot_gates = jnp.concatenate([gate_values.reshape(-1), jnp.zeros((1,), jnp.float32)])[sources]
    combined = jnp.zeros((TOKENS + 1, MODEL_DIM), jnp.float32).at[token_of_slot].add(results * slot_gates[:, None])
    return (middle + combined[:TOKENS]).reshape(SEQUENCE_COUNT, SEQUENCE_LENGTH, MODEL_DIM)

def reference(tokens, segments, routes, priority, w_query, key_matrix, value_matrix, w_out, w_router, attn_gain, moe_gain, query_gain, key_norm_weight, w_gate_up, w_down, cotangent):
    float_args = tuple((operand.astype(jnp.float32) for operand in (tokens, w_query, key_matrix, value_matrix, w_out, w_router, attn_gain, moe_gain, query_gain, key_norm_weight, w_gate_up, w_down)))

    def forward_fn(*operands):
        return layer_forward(*operands, segments, routes, priority)
    result, pullback = jax.vjp(forward_fn, *float_args)
    grads = pullback(cotangent.astype(jnp.float32))
    return (result.astype(jnp.bfloat16), grads[0], grads[1], grads[2], grads[3], grads[4], grads[5], grads[6], grads[7], grads[8], grads[9], grads[10], grads[11])
```

```python
import functools

import jax
import jax.numpy as jnp
from jax import lax
from jax.experimental import pallas as pl
from jax.experimental.pallas import tpu as pltpu
from jax.sharding import PartitionSpec as P

QUERY_HEADS = 32
KEY_VALUE_HEADS = 4
HEAD_DIM = 128
FFE = 768
TOPK = 8

EPS = 1e-06
THETA = 1000000.0
BIG_NEG = -1e30
ALL = ("dp", "seq", "rep")
PLANE = ("dp", "rep")
F32 = jnp.float32
BF16 = jnp.bfloat16
LOG2E = 1.4426950408889634
VMEM_LIMIT = 52 * 1024 * 1024


def norm_rows(values, gain_vector):
    return values * lax.rsqrt(jnp.mean(values * values, axis=-1, keepdims=True) + EPS) * gain_vector


def swap(blocks, axes):
    return lax.all_to_all(blocks, axes, split_axis=0, concat_axis=0, tiled=True)


def gather(shard, axes, count):
    return swap(jnp.broadcast_to(shard[None], (count,) + shard.shape), axes)


def dot(a, b):
    return jnp.dot(a, b, preferred_element_type=F32)


def dot_nt(a, b):
    return lax.dot_general(a, b, (((1,), (1,)), ((), ())), preferred_element_type=F32)


def dot_tn(a, b):
    return lax.dot_general(a, b, (((0,), (0,)), ((), ())), preferred_element_type=F32)


def rotary_tables(positions):
    half_width = HEAD_DIM // 2
    frequency = THETA ** (-2.0 * jnp.arange(half_width, dtype=F32) / HEAD_DIM)
    angles = positions.astype(F32)[:, None] * frequency[None, :]
    cosine, sine = jnp.cos(angles), jnp.sin(angles)
    return (
        jnp.concatenate([cosine, cosine], axis=-1),
        jnp.concatenate([-sine, sine], axis=-1),
    )


def write_bias(bias, query_doc, query_pos, key_doc):
    key_pos = lax.broadcasted_iota(jnp.int32, bias.shape, 1)
    allowed = (query_doc == key_doc) & (key_pos <= query_pos)
    bias[...] = jnp.where(allowed, 0.0, BIG_NEG)


def rotated(projected, gain, cosine, sine):
    scale = lax.rsqrt(jnp.mean(projected * projected, axis=-1, keepdims=True) + EPS)
    unit = projected * scale
    gained = unit * gain
    return scale, unit, gained * cosine + pltpu.roll(gained, HEAD_DIM // 2, 1) * sine


def forward_kernel(
    q_ref, k_ref, v_ref, qdoc_ref, kdoc_ref, qpos_ref, cos_ref, sin_ref, gain_ref, out_ref, total_ref, bias
):
    @pl.when(pl.program_id(1) == 0)
    def _():
        write_bias(bias, qdoc_ref[0], qpos_ref[...], kdoc_ref[0])

    _, _, turned = rotated(q_ref[...], gain_ref[...], cos_ref[...], sin_ref[...])
    factor = HEAD_DIM ** (-0.5) * LOG2E
    scores = dot_nt(turned.astype(BF16), k_ref[0]) * factor + bias[...]
    highest = jnp.max(scores, axis=-1, keepdims=True)
    exponent = jnp.exp2(scores - highest)
    total = jnp.sum(exponent, axis=-1, keepdims=True)
    probs = (exponent * (1.0 / total)).astype(BF16)
    out_ref[...] = dot(probs, v_ref[0]).astype(BF16)
    total_ref[0, 0] = highest + jnp.log2(total)


def backward_kernel(
    q_ref,
    k_ref,
    v_ref,
    qdoc_ref,
    kdoc_ref,
    qpos_ref,
    cos_ref,
    sin_ref,
    gain_ref,
    total_ref,
    grad_ref,
    dq_ref,
    dkv_ref,
    dgain_ref,
    bias,
    dk_sum,
    dv_sum,
):
    seq, head = pl.program_id(0), pl.program_id(1)

    @pl.when(head == 0)
    def _():
        write_bias(bias, qdoc_ref[0], qpos_ref[...], kdoc_ref[0])
        dk_sum[...] = jnp.zeros_like(dk_sum)
        dv_sum[...] = jnp.zeros_like(dv_sum)

    @pl.when((head == 0) & (seq == 0))
    def _():
        dgain_ref[...] = jnp.zeros_like(dgain_ref)

    gain, cosine, sine = gain_ref[...], cos_ref[...], sin_ref[...]
    scale, unit, turned = rotated(q_ref[...], gain, cosine, sine)
    turned = turned.astype(BF16)
    attention_scale = HEAD_DIM ** (-0.5)
    scores = dot_nt(turned, k_ref[0]) * (attention_scale * LOG2E) + bias[...]
    probs = jnp.exp2(scores - total_ref[0, 0])
    grad = grad_ref[...]
    grad_probs = dot_nt(grad, v_ref[0])
    delta = jnp.sum(probs * grad_probs, axis=-1, keepdims=True)
    grad_scores = (probs * (grad_probs - delta)).astype(BF16)
    dv_sum[...] += dot_tn(probs.astype(BF16), grad)
    dk_sum[...] += dot_tn(grad_scores, turned)
    grad_turned = dot(grad_scores, k_ref[0]) * attention_scale
    grad_gained = grad_turned * cosine - pltpu.roll(grad_turned, HEAD_DIM // 2, 1) * sine
    dgain_ref[...] += jnp.sum(grad_gained * unit, axis=0, keepdims=True)
    weighted = grad_gained * gain
    dq_ref[...] = (
        scale * (weighted - unit * jnp.mean(weighted * unit, axis=-1, keepdims=True))
    ).astype(BF16)

    @pl.when(head == pl.num_programs(1) - 1)
    def _():
        shape = dkv_ref.shape[:1] + dkv_ref.shape[2:3] + (HEAD_DIM,)
        dkv_ref[:, 0, :, :HEAD_DIM] = (dk_sum[...] * attention_scale).astype(BF16).reshape(shape)
        dkv_ref[:, 0, :, HEAD_DIM:] = dv_sum[...].astype(BF16).reshape(shape)


def attention_specs(rows, length):
    return [
        pl.BlockSpec((rows, HEAD_DIM), lambda s, h: (s, h)),
        pl.BlockSpec((1, length, HEAD_DIM), lambda s, h: (s, 0, 0)),
        pl.BlockSpec((1, length, HEAD_DIM), lambda s, h: (s, 0, 1)),
        pl.BlockSpec((1, rows, 1), lambda s, h: (s, 0, 0)),
        pl.BlockSpec((1, 1, length), lambda s, h: (s, 0, 0)),
        pl.BlockSpec((rows, 1), lambda s, h: (0, 0)),
        pl.BlockSpec((rows, HEAD_DIM), lambda s, h: (0, 0)),
        pl.BlockSpec((rows, HEAD_DIM), lambda s, h: (0, 0)),
        pl.BlockSpec((1, HEAD_DIM), lambda s, h: (0, 0)),
    ]


def attention_forward(operands, sequences, heads, rows, length):
    pairs = sequences * heads * rows * length
    return pl.pallas_call(
        forward_kernel,
        grid=(sequences, heads),
        in_specs=attention_specs(rows, length),
        out_specs=[
            pl.BlockSpec((rows, HEAD_DIM), lambda s, h: (s, h)),
            pl.BlockSpec((1, 1, rows, 1), lambda s, h: (s, h, 0, 0)),
        ],
        out_shape=[
            jax.ShapeDtypeStruct((sequences * rows, heads * HEAD_DIM), BF16),
            jax.ShapeDtypeStruct((sequences, heads, rows, 1), F32),
        ],
        scratch_shapes=[pltpu.VMEM((rows, length), F32)],
        compiler_params=pltpu.CompilerParams(vmem_limit_bytes=VMEM_LIMIT),
        cost_estimate=pl.CostEstimate(
            flops=4 * pairs * HEAD_DIM, bytes_accessed=8 << 20, transcendentals=pairs
        ),
    )(*operands)


def attention_backward(operands, sequences, heads, rows, length):
    pairs = sequences * heads * rows * length
    parts = length // rows
    return pl.pallas_call(
        backward_kernel,
        grid=(sequences, heads),
        in_specs=attention_specs(rows, length)
        + [
            pl.BlockSpec((1, 1, rows, 1), lambda s, h: (s, h, 0, 0)),
            pl.BlockSpec((rows, HEAD_DIM), lambda s, h: (s, h)),
        ],
        out_specs=[
            pl.BlockSpec((rows, HEAD_DIM), lambda s, h: (s, h)),
            pl.BlockSpec((parts, 1, rows, 2 * HEAD_DIM), lambda s, h: (0, s, 0, 0)),
            pl.BlockSpec((1, HEAD_DIM), lambda s, h: (0, 0)),
        ],
        out_shape=[
            jax.ShapeDtypeStruct((sequences * rows, heads * HEAD_DIM), BF16),
            jax.ShapeDtypeStruct((parts, sequences, rows, 2 * HEAD_DIM), BF16),
            jax.ShapeDtypeStruct((1, HEAD_DIM), F32),
        ],
        scratch_shapes=[
            pltpu.VMEM((rows, length), F32),
            pltpu.VMEM((length, HEAD_DIM), F32),
            pltpu.VMEM((length, HEAD_DIM), F32),
        ],
        compiler_params=pltpu.CompilerParams(vmem_limit_bytes=VMEM_LIMIT),
        cost_estimate=pl.CostEstimate(
            flops=10 * pairs * HEAD_DIM, bytes_accessed=12 << 20, transcendentals=pairs
        ),
    )(*operands)


def body(
    tokens,
    segments,
    routes,
    priority,
    w_query,
    key_matrix,
    value_matrix,
    w_out,
    w_router,
    attn_gain,
    moe_gain,
    query_gain,
    key_norm_weight,
    w_gate_up,
    w_down,
    cotangent,
):
    own_rows, width = tokens.shape[1], tokens.shape[2]
    length = segments.shape[1]
    dp_size, seq_size, rep_size = (lax.axis_size(name) for name in ALL)
    devices = dp_size * seq_size * rep_size
    members = dp_size * rep_size
    seq_at, rep_at = lax.axis_index("seq"), lax.axis_index("rep")
    experts = devices * w_gate_up.shape[0]
    capacity = own_rows * TOPK // experts
    slots = experts * capacity
    depth = w_router.shape[0]
    heads = QUERY_HEADS // members
    head_width = heads * HEAD_DIM
    rows = rep_size * own_rows
    plane_rows = members * own_rows

    choice_ids = routes[0]
    expert_ids = jnp.arange(experts, dtype=jnp.int32)
    picked = jnp.any(choice_ids[:, :, None] == expert_ids[None, None, :], axis=1)
    earlier = (priority[0][None, :] < priority[0][:, None]).astype(BF16)
    slot_index = dot(earlier, picked.astype(BF16)).astype(jnp.int32)
    slot_ids = jnp.arange(capacity, dtype=jnp.int32)
    table = picked[:, :, None] & (slot_index[:, :, None] == slot_ids[None, None, :])
    placing = table.astype(BF16).reshape(own_rows, slots)

    packed = jnp.concatenate(
        [w_router.reshape(-1), attn_gain, moe_gain, query_gain, key_norm_weight]
    )
    unpacked = gather(packed, ALL, devices)
    bounds = [0]
    for part in (w_router.size, depth, depth, query_gain.size, key_norm_weight.size):
        bounds.append(bounds[-1] + part)
    small = [unpacked[:, a:b] for a, b in zip(bounds[:-1], bounds[1:])]
    router = small[0].reshape(width, experts)
    first_gain, second_gain, query_norm_gain, key_norm_gain = (
        piece.reshape(-1).astype(F32) for piece in small[1:]
    )

    plane_tokens = gather(tokens[0], PLANE, members).reshape(plane_rows, width).astype(F32)
    query_part = w_query.reshape(depth, dp_size, heads, rep_size, HEAD_DIM).transpose(1, 3, 0, 2, 4)
    query_part = query_part.reshape(members, depth, head_width)

    def spread(matrix):
        split = matrix.reshape(depth, dp_size, HEAD_DIM).transpose(1, 0, 2)[:, None]
        return jnp.broadcast_to(split, (dp_size, rep_size, depth, HEAD_DIM)).reshape(
            members, depth, HEAD_DIM
        )

    leaving = jnp.concatenate([query_part, spread(key_matrix), spread(value_matrix)], axis=-1)
    columns = leaving.shape[-1]
    weights = gather(swap(leaving, PLANE), "seq", seq_size)
    weights = (
        weights.reshape(seq_size, dp_size, rep_size * depth, columns)
        .transpose(1, 0, 2, 3)
        .reshape(width, columns)
    )
    whole_heads = w_out.shape[0] == HEAD_DIM
    if whole_heads:
        out_weights = gather(w_out, "seq", seq_size).reshape(head_width, width)
    else:
        group = lax.all_gather(w_out, ("seq", "rep"), axis=0, tiled=True)
        group = group.reshape(heads, rep_size, HEAD_DIM, width)
        out_weights = lax.dynamic_index_in_dim(group, rep_at, 1, keepdims=False).reshape(
            head_width, width
        )

    dy_and_picks = jnp.concatenate([cotangent[0], picked.astype(BF16)], axis=-1)
    dy_sent = dot_tn(placing, dy_and_picks).astype(BF16).reshape(experts, capacity, width + experts)
    dy_arrived = swap(dy_sent, ALL).reshape(slots, width + experts)
    dy_rows, pick_rows = dy_arrived[:, :width], dy_arrived[:, width:].astype(F32)

    scale_first = lax.rsqrt(jnp.mean(plane_tokens * plane_tokens, axis=-1, keepdims=True) + EPS)
    unit_first = plane_tokens * scale_first
    normed = (unit_first * first_gain).astype(BF16)
    projected = dot(normed, weights)
    query_proj = projected[:, :head_width]
    key_proj = projected[:, head_width : head_width + HEAD_DIM]
    value_rows = projected[:, head_width + HEAD_DIM :].astype(BF16)
    positions = seq_at * rows + jnp.arange(rows, dtype=jnp.int32)
    cosine, sine = rotary_tables(positions)

    def make_keys(key_in, gain_in):
        gained = norm_rows(key_in, gain_in).reshape(dp_size, rows, HEAD_DIM)
        rolled = jnp.roll(gained, HEAD_DIM // 2, axis=-1)
        return (gained * cosine[None] + rolled * sine[None]).reshape(plane_rows, HEAD_DIM)

    key_rows, key_pull = jax.vjp(make_keys, key_proj, key_norm_gain)
    key_value = jnp.concatenate([key_rows.astype(BF16), value_rows], axis=-1)
    key_value = gather(key_value.reshape(dp_size, rows, 2 * HEAD_DIM), "seq", seq_size)
    key_value = key_value.transpose(1, 0, 2, 3).reshape(dp_size, length, 2 * HEAD_DIM)

    documents = gather(segments[0], "dp", dp_size)
    query_doc = lax.dynamic_slice_in_dim(documents, seq_at * rows, rows, axis=1)
    operands = (
        query_proj,
        key_value,
        key_value,
        query_doc[:, :, None],
        documents[:, None, :],
        positions[:, None],
        cosine,
        sine,
        query_norm_gain[None],
    )
    attended, totals = attention_forward(operands, dp_size, heads, rows, length)
    out_parts = dot(attended, out_weights).astype(BF16).reshape(members, own_rows, width)
    middle = tokens[0].astype(F32) + jnp.sum(swap(out_parts, PLANE).astype(F32), axis=0)

    scale_second = lax.rsqrt(jnp.mean(middle * middle, axis=-1, keepdims=True) + EPS)
    unit_second = middle * scale_second
    routed = (unit_second * second_gain).astype(BF16)
    sent = dot_tn(placing, routed).astype(BF16).reshape(experts, capacity, width)
    routed_rows = swap(sent, ALL).reshape(slots, width)

    def gates_of(token_rows, choices):
        logits = jnp.where(choices, dot(token_rows, router), BIG_NEG)
        exponent = jnp.where(
            choices, jnp.exp(logits - jnp.max(logits, axis=-1, keepdims=True)), 0.0
        )
        return exponent / jnp.maximum(jnp.sum(exponent, axis=-1, keepdims=True), 1e-30)

    gates = gates_of(routed, picked)
    own_expert = lax.axis_index(ALL)
    gate_rows = lax.dynamic_slice_in_dim(
        gates_of(routed_rows, pick_rows > 0.5), own_expert, 1, axis=1
    )
    gate_up_weights, down_weights = w_gate_up[0], w_down[0]
    grad_hidden = dot_nt(dy_rows, down_weights)
    gate_up = dot(routed_rows, gate_up_weights)
    gate_in, up_in = gate_up[:, :FFE], gate_up[:, FFE:]
    sigmoid = jax.nn.sigmoid(gate_in)
    silu = gate_in * sigmoid
    hidden_f = silu * up_in
    hidden = hidden_f.astype(BF16)
    grad_gates_sent = jnp.sum(hidden_f * grad_hidden, axis=-1)
    scaled = grad_hidden * gate_rows
    grad_act = jnp.concatenate(
        [scaled * up_in * (sigmoid * (1.0 + gate_in * (1.0 - sigmoid))), scaled * silu], axis=-1
    ).astype(BF16)
    grad_pairs = dot_nt(grad_act, gate_up_weights).astype(BF16)
    grad_gates_back = swap(grad_gates_sent.reshape(devices, capacity), ALL)
    grad_back = swap(grad_pairs.reshape(devices, capacity, width), ALL).reshape(slots, width)
    results = (dot(hidden, down_weights) * gate_rows).astype(BF16)
    returned = swap(results.reshape(devices, capacity, width), ALL).reshape(slots, width)
    grad_gate_up = dot_tn(routed_rows, grad_act)
    grad_down = dot_tn((hidden_f * gate_rows).astype(BF16), dy_rows)

    mixed = (middle + dot(placing, returned)).astype(BF16)
    grad_gates = jnp.sum(jnp.where(table, grad_gates_back[None], 0.0), axis=-1)
    grad_logits = (
        gates * (grad_gates - jnp.sum(gates * grad_gates, axis=-1, keepdims=True))
    ).astype(BF16)
    grad_router = dot_tn(routed, grad_logits)
    grad_routed = dot(placing, grad_back) + dot_nt(grad_logits, router)
    grad_moe_gain = jnp.sum(grad_routed * unit_second, axis=0)
    weighted = grad_routed * second_gain
    grad_middle = cotangent[0].astype(F32) + scale_second * (
        weighted - unit_second * jnp.mean(weighted * unit_second, axis=-1, keepdims=True)
    )

    grad_branch = gather(grad_middle.astype(BF16), PLANE, members).reshape(plane_rows, width)
    grad_attended = dot_nt(grad_branch, out_weights).astype(BF16)
    grad_out = dot_tn(attended, grad_branch)
    if whole_heads:
        grad_out = grad_out.astype(BF16).reshape(seq_size, HEAD_DIM, width)
        grad_out = jnp.sum(swap(grad_out, "seq").astype(F32), axis=0)
    else:
        group = jnp.zeros((heads, rep_size, HEAD_DIM, width), BF16)
        group = lax.dynamic_update_index_in_dim(
            group, grad_out.astype(BF16).reshape(heads, HEAD_DIM, width), rep_at, 1
        )
        grad_out = lax.psum_scatter(
            group.reshape(heads * rep_size * HEAD_DIM, width).astype(F32),
            ("seq", "rep"),
            scatter_dimension=0,
            tiled=True,
        )
    grad_query_proj, grad_key_value, grad_query_gain = attention_backward(
        operands + (totals, grad_attended), dp_size, heads, rows, length
    )
    grad_key_value = jnp.sum(swap(grad_key_value, "seq").astype(F32), axis=0)
    grad_key_value = grad_key_value.reshape(plane_rows, 2 * HEAD_DIM)
    grad_key_proj, grad_key_gain = key_pull(grad_key_value[:, :HEAD_DIM])
    grad_projected = jnp.concatenate(
        [
            grad_query_proj,
            grad_key_proj.astype(BF16),
            grad_key_value[:, HEAD_DIM:].astype(BF16),
        ],
        axis=-1,
    )
    grad_normed = dot_nt(grad_projected, weights)
    grad_weights = dot_tn(normed, grad_projected).astype(BF16)
    grad_weights = grad_weights.reshape(dp_size, seq_size, rep_size * depth, columns)
    grad_weights = swap(grad_weights.transpose(1, 0, 2, 3), "seq")
    grad_weights = jnp.sum(grad_weights.astype(F32), axis=0).astype(BF16)
    grad_weights = swap(grad_weights.reshape(members, depth, columns), PLANE)
    grad_query = (
        grad_weights[:, :, :head_width]
        .reshape(dp_size, rep_size, depth, heads, HEAD_DIM)
        .transpose(2, 0, 3, 1, 4)
        .reshape(depth, QUERY_HEADS * HEAD_DIM)
        .astype(F32)
    )

    def joined(piece):
        summed = jnp.sum(
            piece.reshape(dp_size, rep_size, depth, HEAD_DIM).astype(F32), axis=1
        )
        return summed.transpose(1, 0, 2).reshape(depth, KEY_VALUE_HEADS * HEAD_DIM)

    grad_key = joined(grad_weights[:, :, head_width : head_width + HEAD_DIM])
    grad_value = joined(grad_weights[:, :, head_width + HEAD_DIM :])
    grad_attn_gain = jnp.sum(grad_normed * unit_first, axis=0)
    normed_parts = grad_normed.astype(BF16).reshape(members, own_rows, width)
    own_grad_normed = jnp.sum(swap(normed_parts, PLANE).astype(F32), axis=0)
    own_tokens = tokens[0].astype(F32)
    own_scale = lax.rsqrt(jnp.mean(own_tokens * own_tokens, axis=-1, keepdims=True) + EPS)
    own_unit = own_tokens * own_scale
    weighted = own_grad_normed * first_gain
    input_grad = grad_middle + own_scale * (
        weighted - own_unit * jnp.mean(weighted * own_unit, axis=-1, keepdims=True)
    )

    packed = jnp.concatenate(
        [
            piece.reshape(devices, -1)
            for piece in (grad_router, grad_attn_gain, grad_moe_gain, grad_query_gain, grad_key_gain)
        ],
        axis=-1,
    )
    owned = jnp.sum(swap(packed, ALL), axis=0)
    small = [owned[a:b] for a, b in zip(bounds[:-1], bounds[1:])]
    return (
        mixed[None],
        input_grad[None],
        grad_query,
        grad_key,
        grad_value,
        grad_out,
        small[0].reshape(depth, experts),
        small[1],
        small[2],
        small[3],
        small[4],
        grad_gate_up[None],
        grad_down[None],
    )


def solution(mesh):
    tokens_spec = P("dp", ("seq", "rep"), None)
    rows_spec = P(ALL, None)
    vector_spec = P(ALL)
    expert_spec = P(ALL, None, None)
    return jax.shard_map(
        body,
        mesh=mesh,
        in_specs=(
            tokens_spec,
            P("dp", None),
            tokens_spec,
            P("dp", ("seq", "rep")),
            rows_spec,
            rows_spec,
            rows_spec,
            rows_spec,
            rows_spec,
            vector_spec,
            vector_spec,
            vector_spec,
            vector_spec,
            expert_spec,
            expert_spec,
            tokens_spec,
        ),
        out_specs=(
            tokens_spec,
            tokens_spec,
            rows_spec,
            rows_spec,
            rows_spec,
            rows_spec,
            rows_spec,
            vector_spec,
            vector_spec,
            vector_spec,
            vector_spec,
            expert_spec,
            expert_spec,
        ),
        check_vma=False,
    )
```

```python
import functools

import jax
import jax.numpy as jnp
from jax import lax
from jax.experimental import pallas as pl
from jax.experimental.pallas import tpu as pltpu
from jax.sharding import PartitionSpec as P

QUERY_HEADS = 32
KEY_VALUE_HEADS = 4
HEAD_DIM = 128
FFE = 768
TOPK = 8

EPS = 1e-06
THETA = 1000000.0
BIG_NEG = -1e30
LOG2E = 1.4426950408889634
ALL = ("dp", "seq", "rep")
PLANE = ("dp", "rep")
F32 = jnp.float32
BF16 = jnp.bfloat16
VMEM_LIMIT = 56 * 1024 * 1024
SCALE = HEAD_DIM ** (-0.5)
SIDE, CORE, CROSS = 1, 2, 4
FLIPS = (CROSS | SIDE, CROSS, SIDE, 0)
LANES = 128
PRIORITY_ROW, DOCUMENT_ROW, MOE_GAIN_ROW, QUERY_GAIN_ROW, KEY_GAIN_ROW, ATTN_GAIN_ROW, PACKET_ROWS = 8, 9, 10, 11, 12, 13, 16


def dot(a, b):
    return jnp.dot(a, b, preferred_element_type=F32)


def dot_nt(a, b):
    return lax.dot_general(a, b, (((1,), (1,)), ((), ())), preferred_element_type=F32)


def dot_tn(a, b):
    return lax.dot_general(a, b, (((0,), (0,)), ((), ())), preferred_element_type=F32)


def after(value, *earlier):
    return lax.optimization_barrier((value,) + earlier)[0]


def swap(blocks, axes):
    return lax.all_to_all(blocks, axes, split_axis=0, concat_axis=0, tiled=True)


def spread(shard, axes, count):
    return swap(jnp.broadcast_to(shard[None], (count,) + shard.shape), axes)


def shape_of(shape, dtype):
    return jax.ShapeDtypeStruct(shape, dtype)


def run(kernel, outs, *operands, scratch=(), flops=0, transcendentals=0):
    in_specs = [pl.BlockSpec(memory_space=pltpu.SMEM)]
    in_specs += [pl.BlockSpec(memory_space=pltpu.VMEM)] * (len(operands) - 1)
    touched = sum(o.size * o.dtype.itemsize for o in operands[1:])
    touched += sum(o.size * o.dtype.itemsize for o in outs)
    return pl.pallas_call(
        kernel,
        in_specs=in_specs,
        out_specs=[pl.BlockSpec(memory_space=pltpu.VMEM)] * len(outs),
        out_shape=outs,
        scratch_shapes=scratch,
        compiler_params=pltpu.CompilerParams(vmem_limit_bytes=VMEM_LIMIT),
        cost_estimate=pl.CostEstimate(
            flops=int(flops), bytes_accessed=int(touched), transcendentals=int(transcendentals)
        ),
    )(*operands)


def plane_move(block, bits):
    return lax.ppermute(block, PLANE, [(index, index ^ bits) for index in range(8)])


def plane_gather(block):
    half = block.shape[0] // 2
    across, aside, core = (plane_move(block, bits) for bits in (CROSS, SIDE, CORE))
    far = [plane_move(across[:half], SIDE), plane_move(aside[half:], CROSS)]
    across_core, aside_core = plane_move(across, CORE), plane_move(aside, CORE)
    far_core = [plane_move(piece, CORE) for piece in far]
    return [block, aside, core, aside_core, across] + far + [across_core] + far_core


def place_plane(refs, member, write):
    rows = refs[0].shape[0]
    offsets = [(0, 0), (1, 0), (2, 0), (3, 0), (4, 0), (5, 0), (5, rows // 2), (6, 0), (7, 0), (7, rows // 2)]
    for ref, (bits, start) in zip(refs, offsets):
        write(pl.multiple_of((member ^ bits) * rows + start, rows // 2), ref)


def first_sums(_, arrived, kept, far_low, far_high, across, aside, own):
    half = far_low.shape[0]
    sums = [arrived[i].astype(F32) + kept[i].astype(F32) for i in range(4)]
    far_low[...] = sums[0][:half].astype(BF16)
    far_high[...] = sums[0][half:].astype(BF16)
    across[...] = sums[1].astype(BF16)
    aside[...] = sums[2].astype(BF16)
    own[...] = sums[3]


def second_sums(_, across, aside, from_across, from_aside, across_out, aside_out):
    half = from_across.shape[0]
    across_out[:half] = across[:half]
    across_out[half:] = (across[half:].astype(F32) + from_aside[...].astype(F32)).astype(BF16)
    aside_out[:half] = (aside[:half].astype(F32) + from_across[...].astype(F32)).astype(BF16)
    aside_out[half:] = aside[half:]


def plane_reduce(info, sent, kept):
    _, rows, width = sent.shape
    piece, whole = shape_of((rows // 2, width), BF16), shape_of((rows, width), BF16)
    arrived = plane_move(sent, CORE)
    far_low, far_high, across, aside, own = run(
        first_sums, [piece, piece, whole, whole, shape_of((rows, width), F32)], info, arrived, kept
    )
    from_across, from_aside = plane_move(far_low, CROSS), plane_move(far_high, SIDE)
    across, aside = run(
        second_sums, [whole, whole], info, across, aside, from_across, from_aside
    )
    return own, plane_move(across, CROSS), plane_move(aside, SIDE)


UP, DOWN = ((0, 1), (1, 2), (2, 3)), ((3, 2), (2, 1), (1, 0))
ORDER = ((0, 1, 2, 3), (1, 2, 0, 3), (2, 1, 3, 0), (3, 2, 1, 0))
OFFSETS = (0, -1, 1, -2, 2, -3, 3)


def line_move(block, pairs):
    return lax.ppermute(block, "seq", list(pairs))


def line_gather(block, count):
    if count != 4:
        return [spread(block, "seq", count)]
    up1, down1 = line_move(block, UP), line_move(block, DOWN)
    up2, down2 = line_move(up1, UP[1:]), line_move(down1, DOWN[1:])
    up3, down3 = line_move(up2, UP[2:]), line_move(down2, DOWN[2:])
    return [block, up1, down1, up2, down2, up3, down3]


def place_line(refs, place, count, write):
    if len(refs) == 1:
        for index in range(count):
            write(index, refs[0].at[index])
        return
    for offset, ref in zip(OFFSETS, refs):
        index = place + offset

        @pl.when((index >= 0) & (index < count))
        def _(index=index, ref=ref):
            write(index, ref)


def needed_offsets(steps):
    return [o for o in OFFSETS if any(ORDER[z][step] - z == o for z in range(4) for step in steps)]


def needed(sources, steps):
    if len(sources) == 1:
        return sources
    return [dict(zip(OFFSETS, sources))[o] for o in needed_offsets(steps)]


def block_of_step(refs, info, steps, step):
    if len(refs) == 1:
        return refs[0][info[4 + step]]
    by_offset = dict(zip(needed_offsets(steps), refs))
    offsets = [ORDER[z][step] - z for z in range(4)]
    block = by_offset[offsets[3]][...]
    for z in range(3):
        if offsets[z] != offsets[3]:
            block = jnp.where(info[0] == z, by_offset[offsets[z]][...], block)
    return block


def line_steps(blocks, place):
    if len(blocks) == 1:
        return [blocks[0][step] for step in range(blocks[0].shape[0])]
    block, up1, down1, up2, down2, up3, down3 = blocks
    low = place < 2
    return [
        block,
        jnp.where(low, down1, up1),
        jnp.where(low, jnp.where(place == 0, down2, up1), jnp.where(place == 3, up2, down1)),
        jnp.where(low, jnp.where(place == 0, down3, down2), jnp.where(place == 3, up3, up2)),
    ]


def line_reduce(parts, place, count):
    if count != 4:
        total = jnp.sum(swap(jnp.stack(parts).astype(BF16), "seq").astype(F32), axis=0)
        return total, None, None
    own, first, second, third = parts
    edge = (place == 0) | (place == 3)
    inward = line_move(third.astype(BF16), [(0, 1), (3, 2)])
    middle = jnp.where(edge, second, third + inward).astype(BF16)
    up, down = line_move(middle, UP[:2]), line_move(middle, DOWN[:2])
    up = (jnp.where(place == 2, second, first) + up).astype(BF16)
    down = (jnp.where(place == 1, second, first) + down).astype(BF16)
    return own, line_move(up, UP), line_move(down, DOWN)


def total_of(terms):
    return sum(term.astype(F32) for term in terms if term is not None)


def pick(blocks, index, axis=0):
    return lax.dynamic_index_in_dim(blocks, index, axis, keepdims=False)


def pack_weights_kernel(*refs):
    *query_refs, key_ref, value_ref, query_out, key_value_out = refs
    for j, ref in enumerate(query_refs):
        query_out[0, :, j * HEAD_DIM : (j + 1) * HEAD_DIM] = ref[...]
    takes_keys = lax.rem(pl.program_id(0), 2) == 0
    key_value_out[0] = jnp.where(takes_keys, key_ref[...], value_ref[...])


def pack_weights(w_query, key_matrix, value_matrix, members, rep_size, heads):
    depth = w_query.shape[0]
    group = heads * rep_size

    def head_spec(j):
        return pl.BlockSpec(
            (depth, HEAD_DIM), lambda m: (0, (m // rep_size) * group + j * rep_size + m % rep_size)
        )

    group_spec = pl.BlockSpec((depth, HEAD_DIM), lambda m: (0, m // rep_size))
    return pl.pallas_call(
        pack_weights_kernel,
        grid=(members,),
        in_specs=[head_spec(j) for j in range(heads)]
        + [group_spec, group_spec],
        out_specs=[
            pl.BlockSpec((1, depth, heads * HEAD_DIM), lambda m: (m, 0, 0)),
            pl.BlockSpec((1, depth, HEAD_DIM), lambda m: (m, 0, 0)),
        ],
        out_shape=[
            shape_of((members, depth, heads * HEAD_DIM), BF16),
            shape_of((members, depth, HEAD_DIM), BF16),
        ],
        cost_estimate=pl.CostEstimate(flops=1 << 20, bytes_accessed=2 << 20, transcendentals=0),
    )(*([w_query] * heads), key_matrix, value_matrix)


def packet_kernel(info, routes, priority, documents, moe_gain, query_gain, key_gain, attn_gain, out):
    own = info[2]
    eye = lax.broadcasted_iota(jnp.int32, (LANES, LANES), 0) == lax.broadcasted_iota(
        jnp.int32, (LANES, LANES), 1
    )
    rows = [dot_tn(routes[...].astype(BF16), eye.astype(BF16)), priority[...].astype(F32)]
    rows.append(documents[...].astype(F32))
    for ref, at in ((moe_gain, 0), (query_gain, own), (key_gain, own), (attn_gain, 0)):
        size = ref.shape[1]
        lane = lax.broadcasted_iota(jnp.int32, (size, LANES), 1)
        value = lax.broadcasted_iota(jnp.int32, (size, LANES), 0)
        rows.append(dot(ref[...], (lane == at * size + value).astype(BF16)))
    packet = jnp.concatenate(rows + [jnp.zeros((PACKET_ROWS - 14, LANES), F32)], axis=0).astype(BF16)
    for index in range(out.shape[0]):
        out[index] = packet


def normalize_kernel(info, gain, *refs):
    out = refs[-1]

    def write(row, ref):
        values = ref[...].astype(F32)
        scale = lax.rsqrt(jnp.mean(values * values, axis=-1, keepdims=True) + EPS)
        out[pl.ds(row, ref.shape[0]), :] = (values * scale * gain[...]).astype(BF16)

    place_plane(refs[:-1], info[1], write)


def place_weights(refs, info, count, out, groups):
    rows = out.shape[0] // (groups * count)

    def write(index, ref):
        for group in range(groups):
            start = pl.multiple_of((group * count + index) * rows, rows)
            out[pl.ds(start, rows), :] = ref[pl.ds(group * rows, rows), :]

    place_line(refs, info[0], count, write)


def turn(values, cosine, sine):
    return values * cosine + pltpu.roll(values, HEAD_DIM // 2, 1) * sine


def key_value_kernel(count, groups, info, units, cosine, sine, gain, *refs):
    *sources, weights, key_proj, out = refs
    place_weights(sources, info, count, weights, groups)
    projected = dot(units[...], weights[...])
    key_proj[...] = projected
    scale = lax.rsqrt(jnp.mean(projected * projected, axis=-1, keepdims=True) + EPS)
    keys = projected * scale * gain[...]
    rows = out.shape[1]
    for group in range(groups):
        part = slice(group * rows, (group + 1) * rows)
        turned = turn(keys[part], cosine[...], sine[...])
        out[group] = jnp.where(info[3] == 0, turned, projected[part]).astype(BF16)


def query_kernel(count, groups, info, units, *refs):
    *sources, weights, out = refs
    place_weights(sources, info, count, weights, groups)
    out[...] = dot(units[...], weights[...])


def attention_setup(info, sources, qdoc_ref, kdoc_ref, qpos_ref, bias, keys, values):
    key_pos = lax.broadcasted_iota(jnp.int32, bias.shape, 1)
    allowed = (qdoc_ref[0] == kdoc_ref[0]) & (key_pos <= qpos_ref[...])
    bias[...] = jnp.where(allowed, 0.0, BIG_NEG)
    rows, count = bias.shape[0], len(sources) // 2
    for step in range(count):
        part = pl.ds(pl.multiple_of(info[4 + step] * rows, rows), rows)
        mine, other = sources[step][0], sources[count + step][0]
        keys[part, :] = jnp.where(info[3] == 0, mine, other)
        values[part, :] = jnp.where(info[3] == 0, other, mine)


def rotated(projected, gain, cosine, sine):
    scale = lax.rsqrt(jnp.mean(projected * projected, axis=-1, keepdims=True) + EPS)
    unit = projected * scale
    return scale, unit, turn(unit * gain, cosine, sine)


def forward_kernel(info, q_ref, qdoc_ref, kdoc_ref, qpos_ref, cos_ref, sin_ref, gain_ref, *refs):
    *sources, out_ref, total_ref, bias, keys, values = refs

    @pl.when(pl.program_id(1) == 0)
    def _():
        attention_setup(info, sources, qdoc_ref, kdoc_ref, qpos_ref, bias, keys, values)

    _, _, turned = rotated(q_ref[...], gain_ref[...], cos_ref[...], sin_ref[...])
    scores = dot_nt(turned.astype(BF16), keys[...]) * (SCALE * LOG2E) + bias[...]
    highest = jnp.max(scores, axis=-1, keepdims=True)
    exponent = jnp.exp2(scores - highest)
    total = jnp.sum(exponent, axis=-1, keepdims=True)
    probs = (exponent * (1.0 / total)).astype(BF16)
    out_ref[...] = dot(probs, values[...]).astype(BF16)
    total_ref[0, 0] = highest + jnp.log2(total)


def backward_kernel(info, q_ref, qdoc_ref, kdoc_ref, qpos_ref, cos_ref, sin_ref, gain_ref, *refs):
    *sources, total_ref, grad_ref, dq_ref, kept_ref, sent_ref, dgain_ref, bias, key_rows, value_rows, dk_sum, dv_sum = refs
    seq, head = pl.program_id(0), pl.program_id(1)

    @pl.when(head == 0)
    def _():
        attention_setup(info, sources, qdoc_ref, kdoc_ref, qpos_ref, bias, key_rows, value_rows)
        dk_sum[...] = jnp.zeros_like(dk_sum)
        dv_sum[...] = jnp.zeros_like(dv_sum)

    @pl.when((head == 0) & (seq == 0))
    def _():
        dgain_ref[...] = jnp.zeros_like(dgain_ref)

    gain, cosine, sine = gain_ref[...], cos_ref[...], sin_ref[...]
    scale, unit, turned = rotated(q_ref[...], gain, cosine, sine)
    turned = turned.astype(BF16)
    keys, values = key_rows[...], value_rows[...]
    scores = dot_nt(turned, keys) * (SCALE * LOG2E) + bias[...]
    probs = jnp.exp2(scores - total_ref[0, 0])
    grad = grad_ref[...]
    grad_probs = dot_nt(grad, values)
    delta = jnp.sum(probs * grad_probs, axis=-1, keepdims=True)
    grad_scores = (probs * (grad_probs - delta)).astype(BF16)
    dv_sum[...] += dot_tn(probs.astype(BF16), grad)
    dk_sum[...] += dot_tn(grad_scores, turned)
    grad_turned = dot(grad_scores, keys) * SCALE
    grad_gained = turn(grad_turned, cosine, -sine)
    dgain_ref[...] += jnp.sum(grad_gained * unit, axis=0, keepdims=True)
    weighted = grad_gained * gain
    dq_ref[...] = (
        scale * (weighted - unit * jnp.mean(weighted * unit, axis=-1, keepdims=True))
    ).astype(BF16)

    @pl.when(head == pl.num_programs(1) - 1)
    def _():
        shape = kept_ref.shape[:1] + kept_ref.shape[2:]
        dk, dv = dk_sum[...] * SCALE, dv_sum[...]
        kept_ref[:, 0] = jnp.where(info[3] == 0, dk, dv).astype(BF16).reshape(shape)
        sent_ref[:, 0] = jnp.where(info[3] == 0, dv, dk).astype(BF16).reshape(shape)


def attention_specs(rows, length, sources, first=0):
    specs = [
        pl.BlockSpec(memory_space=pltpu.SMEM),
        pl.BlockSpec((rows, HEAD_DIM), lambda s, h: (first + s, h)),
        pl.BlockSpec((1, rows, 1), lambda s, h: (first + s, 0, 0)),
        pl.BlockSpec((1, 1, length), lambda s, h: (first + s, 0, 0)),
        pl.BlockSpec((rows, 1), lambda s, h: (0, 0)),
        pl.BlockSpec((rows, HEAD_DIM), lambda s, h: (0, 0)),
        pl.BlockSpec((rows, HEAD_DIM), lambda s, h: (0, 0)),
        pl.BlockSpec((1, HEAD_DIM), lambda s, h: (0, 0)),
    ]
    return specs + [
        pl.BlockSpec((1, rows, HEAD_DIM), lambda s, h: (first + s, 0, 0)) for _ in sources
    ]


def attention_forward(operands, sources, sequences, heads, rows, length):
    pairs = sequences * heads * rows * length
    return pl.pallas_call(
        forward_kernel,
        grid=(sequences, heads),
        in_specs=attention_specs(rows, length, sources),
        out_specs=[
            pl.BlockSpec((rows, HEAD_DIM), lambda s, h: (s, h)),
            pl.BlockSpec((1, 1, rows, 1), lambda s, h: (s, h, 0, 0)),
        ],
        out_shape=[
            shape_of((sequences * rows, heads * HEAD_DIM), BF16),
            shape_of((sequences, heads, rows, 1), F32),
        ],
        scratch_shapes=[
            pltpu.VMEM((rows, length), F32),
            pltpu.VMEM((length, HEAD_DIM), BF16),
            pltpu.VMEM((length, HEAD_DIM), BF16),
        ],
        compiler_params=pltpu.CompilerParams(vmem_limit_bytes=VMEM_LIMIT),
        cost_estimate=pl.CostEstimate(
            flops=4 * pairs * HEAD_DIM, bytes_accessed=8 << 20, transcendentals=pairs
        ),
    )(*operands, *sources)


def attention_backward(operands, sources, totals, grads, first, sequences, heads, rows, length):
    pairs = sequences * heads * rows * length
    parts = length // rows
    key_value_spec = pl.BlockSpec((parts, 1, rows, HEAD_DIM), lambda s, h: (0, s, 0, 0))
    key_value_shape = shape_of((parts, sequences, rows, HEAD_DIM), BF16)
    return pl.pallas_call(
        backward_kernel,
        grid=(sequences, heads),
        in_specs=attention_specs(rows, length, sources, first)
        + [
            pl.BlockSpec((1, 1, rows, 1), lambda s, h: (first + s, h, 0, 0)),
            pl.BlockSpec((rows, HEAD_DIM), lambda s, h: (first + s, h)),
        ],
        out_specs=[
            pl.BlockSpec((rows, HEAD_DIM), lambda s, h: (s, h)),
            key_value_spec,
            key_value_spec,
            pl.BlockSpec((1, HEAD_DIM), lambda s, h: (0, 0)),
        ],
        out_shape=[
            shape_of((sequences * rows, heads * HEAD_DIM), BF16),
            key_value_shape,
            key_value_shape,
            shape_of((1, HEAD_DIM), F32),
        ],
        scratch_shapes=[
            pltpu.VMEM((rows, length), F32),
            pltpu.VMEM((length, HEAD_DIM), BF16),
            pltpu.VMEM((length, HEAD_DIM), BF16),
            pltpu.VMEM((length, HEAD_DIM), F32),
            pltpu.VMEM((length, HEAD_DIM), F32),
        ],
        compiler_params=pltpu.CompilerParams(vmem_limit_bytes=VMEM_LIMIT),
        cost_estimate=pl.CostEstimate(
            flops=10 * pairs * HEAD_DIM, bytes_accessed=8 << 20, transcendentals=pairs
        ),
    )(*operands, *sources, totals, grads)


def key_value_back_kernel(groups, info, own, up, down, key_proj, cosine, sine, gain, out, dgain):
    rows = own.shape[1]
    total = jnp.zeros_like(dgain)
    for group in range(groups):
        grad = own[group].astype(F32) + up[group].astype(F32) + down[group].astype(F32)
        part = slice(group * rows, (group + 1) * rows)
        values_grad = grad
        grad = turn(grad, cosine[...], -sine[...])
        keys = key_proj[part]
        scale = lax.rsqrt(jnp.mean(keys * keys, axis=-1, keepdims=True) + EPS)
        unit = keys * scale
        total = total + jnp.sum(grad * unit, axis=0, keepdims=True)
        weighted = grad * gain[...]
        keys_grad = scale * (weighted - unit * jnp.mean(weighted * unit, axis=-1, keepdims=True))
        out[part, :] = jnp.where(info[3] == 0, keys_grad, values_grad).astype(BF16)
    dgain[...] = jnp.where(info[3] == 0, total, 0.0)


def out_sent_kernel(count, info, attended, *refs):
    *sources, sent, weights = refs

    def write(index, ref):
        start = pl.multiple_of(index * HEAD_DIM, HEAD_DIM)
        weights[pl.ds(start, HEAD_DIM), :] = ref[...]

    place_line(sources, info[0], count, write)
    out_parts(info, CORE, attended, weights, sent)


def out_kept_kernel(info, attended, weights, kept):
    out_parts(info, 0, attended, weights, kept)


def rows_for(info, flip, ref, rows):
    return [
        ref[pl.ds(pl.multiple_of((info[1] ^ (bits | flip)) * rows, rows), rows), :] for bits in FLIPS
    ]


def out_parts(info, flip, attended, weights, out):
    rows, width = out.shape[1:]
    left = jnp.concatenate(rows_for(info, flip, attended, rows), axis=0)
    for start in range(0, width, 512):
        part = slice(start, start + 512)
        out[:, :, part] = dot(left, weights[:, part]).astype(BF16).reshape(4, rows, 512)


def normed_grad_kernel(flip, info, query_grad, key_value_grad, query_weights, key_value_weights, units, out, sums):
    rows, width = out.shape[1:]
    left = jnp.concatenate(rows_for(info, flip, query_grad, rows), axis=0)
    other = jnp.concatenate(rows_for(info, flip, key_value_grad, rows), axis=0)
    unit = jnp.concatenate(rows_for(info, flip, units, rows), axis=0)
    for start in range(0, width, 512):
        part = slice(start, start + 512)
        grad = dot_nt(left, query_weights[part]) + dot_nt(other, key_value_weights[part])
        out[:, :, part] = grad.astype(BF16).reshape(4, rows, 512)
        sums[:, part] = jnp.sum(grad * unit[:, part].astype(F32), axis=0, keepdims=True)


def middle_kernel(info, own, across, aside, tokens, gain, middle, routed, scale_out):
    values = own[...] + across[...].astype(F32) + aside[...].astype(F32) + tokens[...].astype(F32)
    scale = lax.rsqrt(jnp.mean(values * values, axis=-1, keepdims=True) + EPS)
    middle[...] = values
    routed[...] = (values * scale * gain[...]).astype(BF16)
    scale_out[...] = scale


def gradient_spread_kernel(info, weights, *refs):
    *blocks, gathered, attended_grad = refs

    def write(row, ref):
        gathered[pl.ds(row, ref.shape[0]), :] = ref[...]

    place_plane(blocks, info[1], write)
    attended_grad[...] = dot_nt(gathered[...], weights[...]).astype(BF16)


def gates_of(token_rows, router, choices):
    logits = jnp.where(choices, dot(token_rows, router), BIG_NEG)
    exponent = jnp.where(choices, jnp.exp(logits - jnp.max(logits, axis=-1, keepdims=True)), 0.0)
    return exponent / jnp.maximum(jnp.sum(exponent, axis=-1, keepdims=True), 1e-30)


def gates_kernel(info, routed, router, picked, gates):
    gates[...] = gates_of(routed[...], router[...], picked[...][:, : gates.shape[1]] > 0.5)


def dispatch_kernel(steps, info, table, *refs):
    *blocks, out = refs
    members = out.shape[0]
    slots = table.shape[2] // members
    for at, step in enumerate(steps):
        block = block_of_step(blocks, info, steps, step)
        rows = dot_tn(table[info[4 + step]], block).astype(BF16)
        out[:, at * slots : (at + 1) * slots, :] = rows.reshape(members, slots, out.shape[2])


def dispatch_with_choices_kernel(steps, info, table, picked, *refs):
    *blocks, out = refs
    members, _, width = out.shape
    slots = table.shape[2] // members
    for at, step in enumerate(steps):
        place = table[info[4 + step]]
        part = slice(at * slots, (at + 1) * slots)
        rows = dot_tn(place, block_of_step(blocks, info, steps, step)).astype(BF16)
        choices = dot_tn(place, picked[info[4 + step]]).astype(BF16)
        model = rows.shape[1]
        out[:, part, :model] = rows.reshape(members, slots, model)
        out[:, part, model:] = choices.reshape(members, slots, width - model)


def combine_kernel(steps, info, table, arrived, *outs):
    members, _, width = arrived.shape
    slots = table.shape[2] // members
    for at, (step, out) in enumerate(zip(steps, outs)):
        rows = arrived[:, at * slots : (at + 1) * slots, :].reshape(members * slots, width)
        out[...] = dot(table[info[4 + step]], rows).astype(out.dtype)


def combine_all_kernel(info, table, arrived, out):
    members, _, width = arrived.shape
    slots = table.shape[2] // members
    for step in range(out.shape[0]):
        rows = arrived[:, step * slots : (step + 1) * slots, :].reshape(members * slots, width)
        place = info[4 + step]
        out[place] = dot(table[place], rows).astype(BF16)


def expert_prepare_kernel(info, arrived, down, grad_hidden):
    members, slots, _ = arrived.shape
    model = down.shape[2]
    rows = arrived[:, :, :model].reshape(members * slots, model)
    for start in range(0, FFE, 256):
        grad = dot_nt(rows, down[0, start : start + 256, :])
        grad_hidden[:, :, start : start + 256] = grad.reshape(members, slots, 256)


def expert_kernel(first, experts, info, arrived, grad_hidden, dy_rows, router, weights, act, hidden_out, back):
    members, slots, width = arrived.shape
    rows = members * slots
    inputs = arrived[...].reshape(rows, width)
    part = slice(first, first + slots)
    chosen = dy_rows[:, part, width:].reshape(rows, -1)[:, :experts] > 0.5
    own = lax.broadcasted_iota(jnp.int32, (rows, experts), 1) == info[2]
    gate = jnp.sum(
        jnp.where(own, gates_of(inputs, router[...], chosen), 0.0), axis=-1, keepdims=True
    )
    grad_gate = jnp.zeros((rows, 1), F32)
    for start in range(0, FFE, 256):
        piece = slice(start, start + 256)
        lower = slice(FFE + start, FFE + start + 256)
        gate_in = dot(inputs, weights[0, :, piece])
        up_in = dot(inputs, weights[0, :, lower])
        grad_in = grad_hidden[:, part, piece].reshape(rows, 256)
        sigmoid = 1.0 / (1.0 + jnp.exp(-gate_in))
        silu = gate_in * sigmoid
        hidden = silu * up_in
        grad_gate = grad_gate + jnp.sum(hidden * grad_in, axis=-1, keepdims=True)
        scaled = grad_in * gate
        act[:, piece] = (scaled * up_in * (sigmoid + silu * (1.0 - sigmoid))).astype(BF16)
        act[:, lower] = (scaled * silu).astype(BF16)
        hidden_out[:, piece] = (hidden * gate).astype(BF16)
    for start in range(0, width, 512):
        piece = slice(start, start + 512)
        grad = dot_nt(act[...], weights[0, piece, :]).astype(BF16)
        back[:, :, piece] = grad.reshape(members, slots, 512)
    extra = back.shape[2] - width
    high = grad_gate.astype(BF16).astype(F32)
    lane = lax.broadcasted_iota(jnp.int32, (rows, extra), 1)
    columns = jnp.where(lane == info[2], high, 0.0)
    columns = columns + jnp.where(lane == info[2] + experts, grad_gate - high, 0.0)
    back[:, :, width:] = columns.astype(BF16).reshape(members, slots, extra)


def results_kernel(info, down, *refs):
    *hiddens, out = refs
    members, _, width = out.shape
    slots = out.shape[1] // len(hiddens)
    for at, hidden in enumerate(hiddens):
        for start in range(0, width, 512):
            piece = slice(start, start + 512)
            rows = dot(hidden[...], down[0, :, piece]).astype(BF16)
            out[:, at * slots : (at + 1) * slots, piece] = rows.reshape(members, slots, 512)


def gate_up_grad(rows, acts):
    count, groups = rows[0].shape[0], len(rows)
    width, columns = rows[0].shape[1], acts[0].shape[1]
    tile = 512

    def kernel(*refs):
        out = refs[-1]
        total = dot_tn(refs[0][...], refs[groups][...])
        for group in range(1, groups):
            total = total + dot_tn(refs[group][...], refs[groups + group][...])
        out[0] = total

    return pl.pallas_call(
        kernel,
        grid=(width // tile,),
        in_specs=[pl.BlockSpec((count, tile), lambda i: (0, i))] * groups
        + [pl.BlockSpec((count, columns), lambda i: (0, 0))] * groups,
        out_specs=pl.BlockSpec((1, tile, columns), lambda i: (0, i, 0)),
        out_shape=shape_of((1, width, columns), F32),
        compiler_params=pltpu.CompilerParams(vmem_limit_bytes=VMEM_LIMIT),
        cost_estimate=pl.CostEstimate(
            flops=2 * groups * count * width * columns, bytes_accessed=24 << 20, transcendentals=0
        ),
    )(*rows, *acts)


def down_grad(hiddens, arrived, model):
    groups, tile = len(hiddens), 256
    count = hiddens[0].shape[0]
    slots = arrived.shape[1] // groups

    def kernel(*refs):
        *lefts, right, out = refs
        total = 0.0
        for group, left in enumerate(lefts):
            rows = right[:, group * slots : (group + 1) * slots, :model].reshape(count, model)
            total = total + dot_tn(left[...], rows)
        out[0] = total

    return pl.pallas_call(
        kernel,
        grid=(FFE // tile,),
        in_specs=[pl.BlockSpec((count, tile), lambda i: (0, i))] * groups
        + [pl.BlockSpec(arrived.shape, lambda i: (0, 0, 0))],
        out_specs=pl.BlockSpec((1, tile, model), lambda i: (0, i, 0)),
        out_shape=shape_of((1, FFE, model), F32),
        compiler_params=pltpu.CompilerParams(vmem_limit_bytes=VMEM_LIMIT),
        cost_estimate=pl.CostEstimate(
            flops=2 * groups * count * FFE * model, bytes_accessed=16 << 20, transcendentals=0
        ),
    )(*hiddens, arrived)


def token_back_kernel(info, own, up, down, gates, router, middle, scale, gain, cotangent, routed, grad_middle, grad_branch, grad_gain, grad_router):
    width = middle.shape[1]
    experts = gates.shape[1]
    total = own[...].astype(F32) + up[...].astype(F32) + down[...].astype(F32)
    extra = total[:, width:]
    grad_gates = extra[:, :experts] + extra[:, experts : 2 * experts]
    values = gates[...]
    grad_logits = values * (grad_gates - jnp.sum(values * grad_gates, axis=-1, keepdims=True))
    grad_logits = grad_logits.astype(BF16)
    grad_routed = total[:, :width] + dot_nt(grad_logits, router[...])
    unit = middle[...] * scale[...]
    grad_gain[...] = jnp.sum(grad_routed * unit, axis=0, keepdims=True)
    weighted = grad_routed * gain[...]
    grad = cotangent[...].astype(F32) + scale[...] * (
        weighted - unit * jnp.mean(weighted * unit, axis=-1, keepdims=True)
    )
    grad_middle[...] = grad
    grad_branch[...] = grad.astype(BF16)
    grad_router[...] = dot_tn(routed[...], grad_logits)


def input_grad_kernel(info, own, across, aside, tokens, gain, grad_middle, out):
    weighted = (own[...] + across[...].astype(F32) + aside[...].astype(F32)) * gain[...]
    values = tokens[...].astype(F32)
    scale = lax.rsqrt(jnp.mean(values * values, axis=-1, keepdims=True) + EPS)
    unit = values * scale
    out[...] = grad_middle[...] + scale * (
        weighted - unit * jnp.mean(weighted * unit, axis=-1, keepdims=True)
    )


def unpack_query_kernel(rep_size, info, arrived, out):
    members, _, columns = arrived.shape
    heads = columns // HEAD_DIM
    for member in range(members):
        for j in range(heads):
            head = (member // rep_size) * heads * rep_size + j * rep_size + member % rep_size
            out[:, head * HEAD_DIM : (head + 1) * HEAD_DIM] = (
                arrived[member, :, j * HEAD_DIM : (j + 1) * HEAD_DIM].astype(F32)
            )


def unpack_key_value_kernel(rep_size, info, arrived, keys, values):
    for group in range(arrived.shape[0] // rep_size):
        part = slice(group * HEAD_DIM, (group + 1) * HEAD_DIM)
        keys[:, part] = arrived[group * rep_size].astype(F32)
        values[:, part] = arrived[group * rep_size + 1].astype(F32)


def body(
    tokens,
    segments,
    routes,
    priority,
    w_query,
    key_matrix,
    value_matrix,
    w_out,
    w_router,
    attn_gain,
    moe_gain,
    query_gain,
    key_norm_weight,
    w_gate_up,
    w_down,
    cotangent,
):
    own_rows, width = tokens.shape[1], tokens.shape[2]
    length = segments.shape[1]
    dp_size, seq_size, rep_size = (lax.axis_size(name) for name in ALL)
    devices = dp_size * seq_size * rep_size
    members = dp_size * rep_size
    dp_at, seq_at, rep_at = (lax.axis_index(name) for name in ALL)
    experts = devices * w_gate_up.shape[0]
    capacity = own_rows * TOPK // experts
    plane_slots = members * capacity
    depth = w_router.shape[0]
    heads = QUERY_HEADS // members
    head_width = heads * HEAD_DIM
    rows = rep_size * own_rows
    plane_rows = members * own_rows
    chunk = members * depth
    extra = -(-2 * experts // LANES) * LANES
    if seq_size == 4:
        order = [jnp.array(ORDER, jnp.int32)[seq_at, step] for step in range(4)]
    else:
        order = [jnp.int32(step) for step in range(seq_size)]
    info = jnp.stack([seq_at, lax.axis_index(PLANE), lax.axis_index(ALL), rep_at] + order)
    own_tokens, own_cotangent = tokens[0], cotangent[0]

    token_blocks = plane_gather(own_tokens)
    query_part, key_value_part = pack_weights(
        w_query, key_matrix, value_matrix, members, rep_size, heads
    )
    key_value_part = swap(key_value_part, PLANE)
    own_documents = lax.dynamic_slice_in_dim(segments, (seq_at * rep_size + rep_at) * own_rows, own_rows, 1)
    packet = run(
        packet_kernel,
        [shape_of((devices, PACKET_ROWS, LANES), BF16)],
        info,
        routes[0],
        priority,
        own_documents,
        moe_gain[None],
        query_gain[None],
        key_norm_weight[None],
        attn_gain[None],
    )[0]
    packet = swap(after(packet, key_value_part), ALL)
    query_part = swap(after(query_part, packet), PLANE)
    key_value_sources = line_gather(key_value_part.reshape(chunk, HEAD_DIM), seq_size)
    query_sources = line_gather(query_part.reshape(chunk, head_width), seq_size)
    router = spread(after(w_router, query_part), ALL, devices).reshape(width, experts)

    packet = packet.astype(F32)
    documents = packet[:, DOCUMENT_ROW].reshape(dp_size, length).astype(jnp.int32)
    first_gain = packet[:, ATTN_GAIN_ROW, :depth].reshape(1, width)
    second_gain = packet[:, MOE_GAIN_ROW, :depth].reshape(1, width)
    query_norm_gain = jnp.sum(packet[:, QUERY_GAIN_ROW], axis=0, keepdims=True)
    key_norm_gain = jnp.sum(packet[:, KEY_GAIN_ROW], axis=0, keepdims=True)
    meta = packet.reshape(dp_size, seq_size, rep_size, PACKET_ROWS, LANES)
    meta = pick(pick(meta, dp_at), rep_at, 1).astype(jnp.int32)
    choice_ids, priority_rank = meta[:, :TOPK], meta[:, PRIORITY_ROW]
    expert_lanes = -(-experts // LANES) * LANES
    expert_ids = jnp.arange(expert_lanes, dtype=jnp.int32)
    picked = jnp.any(choice_ids[:, :, :, None] == expert_ids, axis=1)
    earlier = (priority_rank[:, None, :] < priority_rank[:, :, None]).astype(BF16)
    plane_picked = pick(
        picked[:, :, :experts].reshape(seq_size, own_rows, dp_size, seq_size, rep_size), seq_at, 3
    ).reshape(seq_size, own_rows, members)
    slot_index = jnp.einsum(
        "bts,bse->bte", earlier, plane_picked.astype(BF16), preferred_element_type=F32
    ).astype(jnp.int32)
    slot_ids = jnp.arange(capacity, dtype=jnp.int32)
    table = plane_picked[..., None] & (slot_index[..., None] == slot_ids)
    table = table.reshape(seq_size, own_rows, plane_slots).astype(BF16)
    picked = picked.astype(BF16)

    units = run(
        normalize_kernel, [shape_of((plane_rows, width), BF16)], info, first_gain, *token_blocks
    )[0]
    positions = seq_at * rows + jnp.arange(rows, dtype=jnp.int32)
    frequency = THETA ** (-2.0 * jnp.arange(HEAD_DIM // 2, dtype=F32) / HEAD_DIM)
    angles = positions.astype(F32)[:, None] * jnp.concatenate([frequency, frequency])[None, :]
    sign = jnp.where(jnp.arange(HEAD_DIM) < HEAD_DIM // 2, -1.0, 1.0)
    cosine, sine = jnp.cos(angles), jnp.sin(angles) * sign[None, :]
    key_value_weights, key_proj, key_value_rows = run(
        functools.partial(key_value_kernel, seq_size, dp_size),
        [
            shape_of((width, HEAD_DIM), BF16),
            shape_of((plane_rows, HEAD_DIM), F32),
            shape_of((dp_size, rows, HEAD_DIM), BF16),
        ],
        info,
        units,
        cosine,
        sine,
        key_norm_gain,
        *key_value_sources,
        flops=2 * plane_rows * width * HEAD_DIM,
    )
    mine = line_steps(line_gather(key_value_rows, seq_size), seq_at)
    key_values = mine + [plane_move(block, SIDE) for block in mine]
    query_weights, query_proj = run(
        functools.partial(query_kernel, seq_size, dp_size),
        [shape_of((width, head_width), BF16), shape_of((plane_rows, head_width), F32)],
        info,
        units,
        *query_sources,
        flops=2 * plane_rows * width * head_width,
    )

    steps = list(range(seq_size))
    groups = [steps[: seq_size // 2], steps[seq_size // 2 :]]
    group_slots = len(groups[0]) * capacity
    group_rows = members * group_slots
    cotangent_sources = [lax.all_gather(after(own_cotangent, key_values[0]), "seq")]

    whole_heads = w_out.shape[0] == HEAD_DIM
    if whole_heads:
        out_sources = [lax.all_gather(w_out, "seq")]
    else:
        group = lax.all_gather(w_out, ("seq", "rep"), axis=0, tiled=True)
        group = group.reshape(heads, rep_size, HEAD_DIM, width)
        out_sources = [pick(group, rep_at, 1)]

    query_proj = after(query_proj, router)
    query_doc = lax.dynamic_slice_in_dim(documents, seq_at * rows, rows, axis=1)
    operands = (
        info,
        query_proj,
        query_doc[:, :, None],
        documents[:, None, :],
        positions[:, None],
        cosine,
        sine,
        query_norm_gain,
    )
    attended, totals = attention_forward(operands, key_values, dp_size, heads, rows, length)
    parts_shape = shape_of((4, own_rows, width), BF16)
    part_flops = 8 * own_rows * head_width * width
    sent, out_weights = run(
        functools.partial(out_sent_kernel, heads),
        [parts_shape, shape_of((head_width, width), BF16)],
        info,
        attended,
        *out_sources,
        flops=part_flops,
    )
    kept = run(out_kept_kernel, [parts_shape], info, attended, out_weights, flops=part_flops)[0]
    row_f32, row_bf16 = shape_of((own_rows, width), F32), shape_of((own_rows, width), BF16)
    middle, routed, scale_second = run(
        middle_kernel,
        [row_f32, row_bf16, shape_of((own_rows, 1), F32)],
        info,
        *plane_reduce(info, sent, kept),
        own_tokens,
        second_gain,
    )

    routed_sources = line_gather(routed, seq_size)
    own_picked = pick(picked, seq_at)
    gates = run(
        gates_kernel, [shape_of((own_rows, experts), F32)], info, routed, router, own_picked
    )[0]
    dy_rows = run(
        functools.partial(dispatch_with_choices_kernel, steps),
        [shape_of((members, seq_size * capacity, width + expert_lanes), BF16)],
        info,
        table,
        picked,
        *cotangent_sources,
        flops=2 * own_rows * seq_size * plane_slots * width,
    )[0]
    dy_rows = swap(after(dy_rows, routed), PLANE)
    grad_hidden = run(
        expert_prepare_kernel,
        [shape_of((members, seq_size * capacity, FFE), F32)],
        info,
        dy_rows,
        w_down,
        flops=2 * seq_size * plane_slots * width * FFE,
    )[0]
    arrived, acts, hiddens, backs = [], [], [], []
    token = dy_rows
    for group in groups:
        outgoing = run(
            functools.partial(dispatch_kernel, group),
            [shape_of((members, group_slots, width), BF16)],
            info,
            table,
            *needed(routed_sources, group),
            flops=2 * own_rows * len(group) * plane_slots * width,
        )[0]
        arrived.append(swap(after(outgoing, token), PLANE))
        token = arrived[-1]
    for at in range(2):
        act, hidden, back = run(
            functools.partial(expert_kernel, at * group_slots, experts),
            [
                shape_of((group_rows, 2 * FFE), BF16),
                shape_of((group_rows, FFE), BF16),
                shape_of((members, group_slots, width + extra), BF16),
            ],
            info,
            arrived[at],
            grad_hidden,
            dy_rows,
            router,
            w_gate_up,
            flops=8 * group_rows * width * FFE,
        )
        acts.append(act)
        hiddens.append(hidden)
        backs.append(back)
    pair_parts = [None] * seq_size
    token = arrived[-1]
    for at in (1, 0):
        returned = swap(after(backs[at], token), PLANE)
        token = returned
        kinds = [F32 if step == 0 else BF16 for step in groups[at]]
        combined = run(
            functools.partial(combine_kernel, groups[at]),
            [shape_of((own_rows, width + extra), kind) for kind in kinds],
            info,
            table,
            returned,
            flops=2 * own_rows * len(groups[at]) * plane_slots * (width + extra),
        )
        for step, part in zip(groups[at], combined):
            pair_parts[step] = part
    results = run(
        results_kernel,
        [shape_of((members, seq_size * capacity, width), BF16)],
        info,
        w_down,
        *hiddens,
        flops=4 * group_rows * width * FFE,
    )[0]
    results = swap(after(results, token), PLANE)
    pair_terms = line_reduce(pair_parts, seq_at, seq_size)
    pair_terms = [jnp.zeros(pair_parts[0].shape, BF16) if t is None else t for t in pair_terms]
    grad_gate_up = gate_up_grad([rows_.reshape(group_rows, width) for rows_ in arrived], acts)
    grad_down = down_grad(hiddens, dy_rows, width)
    pair_terms[2] = after(pair_terms[2], grad_gate_up, grad_down)
    grad_middle, grad_branch, grad_moe_gain, grad_router = run(
        token_back_kernel,
        [row_f32, row_bf16, shape_of((1, width), F32), shape_of((width, experts), F32)],
        info,
        *pair_terms,
        gates,
        router,
        middle,
        scale_second,
        second_gain,
        own_cotangent,
        routed,
    )
    result_parts = run(
        combine_all_kernel,
        [shape_of((seq_size, own_rows, width), BF16)],
        info,
        table,
        results,
        flops=2 * own_rows * seq_size * plane_slots * width,
    )[0]
    result_sum = lax.psum_scatter(result_parts, "seq", scatter_dimension=0, tiled=False)
    mixed = (middle + result_sum.astype(F32)).astype(BF16)

    branch_blocks = plane_gather(grad_branch)
    grad_branch, grad_attended = run(
        gradient_spread_kernel,
        [shape_of((plane_rows, width), BF16), shape_of((plane_rows, head_width), BF16)],
        info,
        out_weights,
        *branch_blocks,
        flops=2 * plane_rows * head_width * width,
    )
    grad_out = dot_tn(attended, grad_branch).astype(BF16)
    grad_attended = after(grad_attended, grad_out)
    if whole_heads:
        grad_out = grad_out.reshape(heads, HEAD_DIM, width)
        grad_out = lax.psum_scatter(grad_out, "seq", scatter_dimension=0, tiled=False).astype(F32)
    else:
        group = jnp.zeros((heads, rep_size, HEAD_DIM, width), F32)
        group = lax.dynamic_update_index_in_dim(
            group, grad_out.reshape(heads, HEAD_DIM, width).astype(F32), rep_at, 1
        )
        grad_out = lax.psum_scatter(
            group.reshape(heads * rep_size * HEAD_DIM, width),
            ("seq", "rep"),
            scatter_dimension=0,
            tiled=True,
        )
    half = dp_size // 2
    query_grads, kept_grads, sent_grads, gain_grads = zip(
        *(
            attention_backward(
                operands, key_values, totals, grad_attended, first, half, heads, rows, length
            )
            for first in (0, half)
        )
    )
    grad_query_proj = jnp.concatenate(query_grads)
    grad_query_gain = gain_grads[0] + gain_grads[1]
    kept_grads = [
        kept.astype(F32) + plane_move(sent, SIDE).astype(F32)
        for kept, sent in zip(kept_grads, sent_grads)
    ]
    grad_key_value = jnp.concatenate(kept_grads, axis=1).astype(BF16)
    key_value_terms = line_reduce(
        [pick(grad_key_value, index) for index in order], seq_at, seq_size
    )
    key_value_terms = [
        jnp.zeros((dp_size, rows, HEAD_DIM), BF16) if t is None else t for t in key_value_terms
    ]
    grad_key_value, grad_key_gain = run(
        functools.partial(key_value_back_kernel, dp_size),
        [shape_of((plane_rows, HEAD_DIM), BF16), shape_of((1, HEAD_DIM), F32)],
        info,
        *key_value_terms,
        key_proj,
        cosine,
        sine,
        key_norm_gain,
    )

    def weight_grad(grad, token):
        parts = dot_tn(units, grad).astype(BF16)
        parts = parts.reshape(dp_size, seq_size, rep_size * depth, grad.shape[1])
        parts = [pick(parts, index, 1) for index in order]
        total = total_of(line_reduce(parts, seq_at, seq_size)).astype(BF16)
        return swap(after(total.reshape(members, depth, grad.shape[1]), token), PLANE)

    query_arrived = weight_grad(grad_query_proj, results)
    grad_query = run(
        functools.partial(unpack_query_kernel, rep_size),
        [shape_of(w_query.shape, F32)],
        info,
        query_arrived,
    )[0]
    key_value_arrived = weight_grad(grad_key_value, query_arrived)
    grad_key, grad_value = run(
        functools.partial(unpack_key_value_kernel, rep_size),
        [shape_of(key_matrix.shape, F32)] * 2,
        info,
        key_value_arrived,
    )

    sums = []
    parts = []
    for flip in (CORE, 0):
        part, column_sums = run(
            functools.partial(normed_grad_kernel, flip),
            [parts_shape, shape_of((1, width), F32)],
            info,
            grad_query_proj,
            grad_key_value,
            query_weights,
            key_value_weights,
            units,
            flops=8 * own_rows * (head_width + HEAD_DIM) * width,
        )
        parts.append(part)
        sums.append(column_sums)
    input_grad = run(
        input_grad_kernel,
        [row_f32],
        info,
        *plane_reduce(info, *parts),
        own_tokens,
        first_gain,
        grad_middle,
    )[0]

    pieces = (grad_router, sums[0] + sums[1], grad_moe_gain, grad_query_gain, grad_key_gain)
    small = jnp.concatenate([piece.reshape(devices, -1) for piece in pieces], axis=-1)
    small = jnp.sum(swap(after(small, key_value_arrived), ALL), axis=0)
    bounds = [0]
    for piece in pieces:
        bounds.append(bounds[-1] + piece.size // devices)
    small = [small[a:b] for a, b in zip(bounds[:-1], bounds[1:])]
    return (
        mixed[None],
        input_grad[None],
        grad_query,
        grad_key,
        grad_value,
        grad_out,
        small[0].reshape(depth, experts),
        small[1] / attn_gain.astype(F32),
        small[2],
        small[3],
        small[4],
        grad_gate_up,
        grad_down,
    )


def solution(mesh):
    tokens_spec = P("dp", ("seq", "rep"), None)
    rows_spec = P(ALL, None)
    vector_spec = P(ALL)
    expert_spec = P(ALL, None, None)
    return jax.shard_map(
        body,
        mesh=mesh,
        in_specs=(
            (tokens_spec, P("dp", None), tokens_spec, P("dp", ("seq", "rep")))
            + (rows_spec,) * 5
            + (vector_spec,) * 4
            + (expert_spec, expert_spec, tokens_spec)
        ),
        out_specs=(
            (tokens_spec, tokens_spec)
            + (rows_spec,) * 5
            + (vector_spec,) * 4
            + (expert_spec, expert_spec)
        ),
        check_vma=False,
    )
```

```python
import functools

import jax
import jax.numpy as jnp
from jax import lax
from jax.experimental import pallas as pl
from jax.experimental.pallas import tpu as pltpu
from jax.sharding import PartitionSpec as P

QUERY_HEADS = 32
KEY_VALUE_HEADS = 4
HEAD_DIM = 128
FFE = 768
TOPK = 8

EPS = 1e-06
THETA = 1000000.0
BIG_NEG = -1e30
LOG2E = 1.4426950408889634
ALL = ("dp", "seq", "rep")
PLANE = ("dp", "rep")
F32 = jnp.float32
BF16 = jnp.bfloat16
VMEM_LIMIT = 56 * 1024 * 1024
SCALE = HEAD_DIM ** (-0.5)
SIDE, CORE, CROSS = 1, 2, 4
FLIPS = (CROSS | SIDE, CROSS, SIDE, 0)
LANES = 128
PRIORITY_ROW, DOCUMENT_ROW, MOE_GAIN_ROW, QUERY_GAIN_ROW, KEY_GAIN_ROW, ATTN_GAIN_ROW, PACKET_ROWS = 8, 9, 10, 11, 12, 13, 16


def dot(a, b):
    return jnp.dot(a, b, preferred_element_type=F32)


def dot_nt(a, b):
    return lax.dot_general(a, b, (((1,), (1,)), ((), ())), preferred_element_type=F32)


def dot_tn(a, b):
    return lax.dot_general(a, b, (((0,), (0,)), ((), ())), preferred_element_type=F32)


def after(value, *earlier):
    return pl.pallas_call(
        lambda *refs: None,
        in_specs=[pl.BlockSpec(memory_space=pl.ANY)] * (1 + len(earlier)),
        out_specs=pl.BlockSpec(memory_space=pl.ANY),
        out_shape=jax.ShapeDtypeStruct(value.shape, value.dtype),
        input_output_aliases={0: 0},
        cost_estimate=pl.CostEstimate(flops=1000, bytes_accessed=1000, transcendentals=0),
    )(value, *earlier)


def swap(blocks, axes):
    return lax.all_to_all(blocks, axes, split_axis=0, concat_axis=0, tiled=True)


def spread(shard, axes, count):
    return swap(jnp.broadcast_to(shard[None], (count,) + shard.shape), axes)


def shape_of(shape, dtype):
    return jax.ShapeDtypeStruct(shape, dtype)


def run(kernel, outs, *operands, tokens=(), flops=0, filler=False):
    in_specs = [pl.BlockSpec(memory_space=pltpu.SMEM)]
    in_specs += [pl.BlockSpec(memory_space=pltpu.VMEM)] * (len(operands) - 1)
    in_specs += [pl.BlockSpec(memory_space=pl.ANY)] * len(tokens)
    touched = sum(o.size * o.dtype.itemsize for o in operands[1:])
    touched += sum(o.size * o.dtype.itemsize for o in outs)
    if filler:
        flops, touched = 1000, 1000

    def body(*refs):
        kernel(*refs[: len(operands)], *refs[len(operands) + len(tokens) :])

    return pl.pallas_call(
        body,
        in_specs=in_specs,
        out_specs=[pl.BlockSpec(memory_space=pltpu.VMEM)] * len(outs),
        out_shape=outs,
        compiler_params=pltpu.CompilerParams(vmem_limit_bytes=VMEM_LIMIT),
        cost_estimate=pl.CostEstimate(
            flops=int(flops), bytes_accessed=int(touched), transcendentals=0
        ),
    )(*operands, *tokens)


def plane_move(block, bits):
    return lax.ppermute(block, PLANE, [(index, index ^ bits) for index in range(8)])


def plane_gather(block):
    half = block.shape[0] // 2
    across, aside, core = (plane_move(block, bits) for bits in (CROSS, SIDE, CORE))
    far = [plane_move(across[:half], SIDE), plane_move(aside[half:], CROSS)]
    across_core, aside_core = plane_move(across, CORE), plane_move(aside, CORE)
    far_core = [plane_move(piece, CORE) for piece in far]
    return [block, aside, core, aside_core, across] + far + [across_core] + far_core


def place_plane(refs, member, write):
    rows = refs[0].shape[0]
    offsets = [(0, 0), (1, 0), (2, 0), (3, 0), (4, 0), (5, 0), (5, rows // 2), (6, 0), (7, 0), (7, rows // 2)]
    for ref, (bits, start) in zip(refs, offsets):
        write(pl.multiple_of((member ^ bits) * rows + start, rows // 2), ref)


def first_sums(_, arrived, kept, far_low, far_high, across, aside, own):
    half = far_low.shape[0]
    sums = [arrived[i].astype(F32) + kept[i].astype(F32) for i in range(4)]
    far_low[...] = sums[0][:half].astype(BF16)
    far_high[...] = sums[0][half:].astype(BF16)
    across[...] = sums[1].astype(BF16)
    aside[...] = sums[2].astype(BF16)
    own[...] = sums[3]


def second_sums(_, across, aside, from_across, from_aside, across_out, aside_out):
    half = from_across.shape[0]
    across_out[:half] = across[:half]
    across_out[half:] = (across[half:].astype(F32) + from_aside[...].astype(F32)).astype(BF16)
    aside_out[:half] = (aside[:half].astype(F32) + from_across[...].astype(F32)).astype(BF16)
    aside_out[half:] = aside[half:]


def plane_reduce(info, sent, kept):
    _, rows, width = sent.shape
    piece, whole = shape_of((rows // 2, width), BF16), shape_of((rows, width), BF16)
    arrived = plane_move(sent, CORE)
    far_low, far_high, across, aside, own = run(
        first_sums, [piece, piece, whole, whole, shape_of((rows, width), F32)], info, arrived, kept
    )
    from_across, from_aside = plane_move(far_low, CROSS), plane_move(far_high, SIDE)
    across, aside = run(
        second_sums, [whole, whole], info, across, aside, from_across, from_aside
    )
    return own, plane_move(across, CROSS), plane_move(aside, SIDE), across


def line_move(block, bits):
    return lax.ppermute(block, "seq", [(place, place ^ bits) for place in range(4)])


def line_gather(block, count):
    if count != 4:
        return [spread(block, "seq", count)]
    near, second = line_move(block, 1), line_move(block, 2)
    return [block, near, second, line_move(after(second, near), 1)]


def line_gather_near(block, count):
    return [block, line_move(block, 1)] if count == 4 else [block]


def place_line(refs, place, count, write):
    for at in range(count):
        if len(refs) == 1:
            write(at, refs[0].at[at])
        else:
            write(place ^ at, refs[at])


def needed(sources, steps):
    return sources if len(sources) == 1 else [sources[step] for step in steps]


def block_of_step(refs, info, steps, step):
    if len(refs) == 1:
        return refs[0][info[4 + step]]
    pieces = len(refs) // len(steps)
    at = steps.index(step) * pieces
    return jnp.concatenate([ref[...] for ref in refs[at : at + pieces]], axis=0)


def line_steps(blocks):
    if len(blocks) == 1:
        return [blocks[0][step] for step in range(blocks[0].shape[0])]
    return blocks


def line_forward(part, crossing):
    return (part.astype(F32) + line_move(crossing, 1).astype(F32)).astype(BF16)


def line_reduce(parts, place, count):
    if count != 4:
        return [jnp.sum(swap(parts, "seq").astype(F32), axis=0)]
    own, near, second, crossing = (pick(parts, place ^ bits) for bits in range(4))
    return [own, line_move(line_forward(second, crossing), 2), line_move(near, 1)]


def total_of(terms):
    return sum(term.astype(F32) for term in terms)


def pick(blocks, index, axis=0):
    return lax.dynamic_index_in_dim(blocks, index, axis, keepdims=False)


def pack_weights_kernel(*refs):
    *query_refs, key_ref, value_ref, query_out, key_value_out = refs
    for j, ref in enumerate(query_refs):
        query_out[0, :, j * HEAD_DIM : (j + 1) * HEAD_DIM] = ref[...]
    takes_keys = lax.rem(pl.program_id(0), 2) == 0
    key_value_out[0] = jnp.where(takes_keys, key_ref[...], value_ref[...])


def pack_weights(w_query, key_matrix, value_matrix, members, rep_size, heads):
    depth = w_query.shape[0]
    group = heads * rep_size

    def head_spec(j):
        return pl.BlockSpec(
            (depth, HEAD_DIM), lambda m: (0, (m // rep_size) * group + j * rep_size + m % rep_size)
        )

    group_spec = pl.BlockSpec((depth, HEAD_DIM), lambda m: (0, m // rep_size))
    return pl.pallas_call(
        pack_weights_kernel,
        grid=(members,),
        in_specs=[head_spec(j) for j in range(heads)]
        + [group_spec, group_spec],
        out_specs=[
            pl.BlockSpec((1, depth, heads * HEAD_DIM), lambda m: (m, 0, 0)),
            pl.BlockSpec((1, depth, HEAD_DIM), lambda m: (m, 0, 0)),
        ],
        out_shape=[
            shape_of((members, depth, heads * HEAD_DIM), BF16),
            shape_of((members, depth, HEAD_DIM), BF16),
        ],
        cost_estimate=pl.CostEstimate(flops=1 << 20, bytes_accessed=2 << 20, transcendentals=0),
    )(*([w_query] * heads), key_matrix, value_matrix)


def packet_kernel(rep_size, info, weights, router, routes, priority, documents, moe_gain, query_gain, key_gain, attn_gain, out):
    own = info[2]
    eye = lax.broadcasted_iota(jnp.int32, (LANES, LANES), 0) == lax.broadcasted_iota(
        jnp.int32, (LANES, LANES), 1
    )
    rows = [dot_tn(routes[...].astype(BF16), eye.astype(BF16)), priority[...].astype(F32)]
    rows.append(documents[...].astype(F32))
    for ref, at in ((moe_gain, 0), (query_gain, own), (key_gain, own), (attn_gain, 0)):
        size = ref.shape[1]
        lane = lax.broadcasted_iota(jnp.int32, (size, LANES), 1)
        value = lax.broadcasted_iota(jnp.int32, (size, LANES), 0)
        rows.append(dot(ref[...], (lane == at * size + value).astype(BF16)))
    packet = jnp.concatenate(rows + [jnp.zeros((PACKET_ROWS - 14, LANES), F32)], axis=0).astype(BF16)
    depth, count = weights.shape[1], out.shape[0]
    line = count // weights.shape[0]
    for index in range(count):
        member = index // (line * rep_size) * rep_size + index % rep_size
        out[index, :depth] = weights[member]
        out[index, depth : depth + PACKET_ROWS] = packet
        out[index, depth + PACKET_ROWS :] = router[...]


def gain_row(packet, depth, out):
    for index in range(packet.shape[0]):
        row = packet[index, depth + ATTN_GAIN_ROW : depth + ATTN_GAIN_ROW + 1, :depth]
        out[:, index * depth : (index + 1) * depth] = row.astype(F32)


def normalize_kernel(depth, info, packet, *refs):
    *refs, out, gain = refs
    gain_row(packet, depth, gain)

    def write(row, ref):
        values = ref[...].astype(F32)
        scale = lax.rsqrt(jnp.mean(values * values, axis=-1, keepdims=True) + EPS)
        out[pl.ds(row, ref.shape[0]), :] = (values * scale * gain[...]).astype(BF16)

    place_plane(refs, info[1], write)


def place_weights(refs, info, count, out, groups):
    rows = out.shape[0] // (groups * count)

    def write(index, ref):
        for group in range(groups):
            start = pl.multiple_of((group * count + index) * rows, rows)
            out[pl.ds(start, rows), :] = ref[pl.ds(group * rows, rows), :]

    place_line(refs, info[0], count, write)


def turn(values, cosine, sine):
    return values * cosine + pltpu.roll(values, HEAD_DIM // 2, 1) * sine


def key_value_kernel(info, units, packet, cosine, sine, key_proj, out, weights, gain):
    depth = units.shape[1] // packet.shape[0]
    total = jnp.zeros(gain.shape, F32)
    for index in range(packet.shape[0]):
        weights[index * depth : (index + 1) * depth] = packet[index, :depth]
        row = depth + KEY_GAIN_ROW
        total = total + packet[index, row : row + 1, :].astype(F32)
    gain[...] = total
    projected = dot(units[...], weights[...])
    key_proj[...] = projected
    scale = lax.rsqrt(jnp.mean(projected * projected, axis=-1, keepdims=True) + EPS)
    keys = projected * scale * total
    groups, rows, _ = out.shape
    for group in range(groups):
        part = slice(group * rows, (group + 1) * rows)
        turned = turn(keys[part], cosine[...], sine[...])
        out[group] = jnp.where(info[3] == 0, turned, projected[part]).astype(BF16)


def query_kernel(count, groups, info, units, *refs):
    *sources, weights, out = refs
    place_weights(sources, info, count, weights, groups)
    out[...] = dot(units[...], weights[...])


def attention_setup(info, sources, qdoc_ref, kdoc_ref, qpos_ref, bias, keys, values):
    key_pos = lax.broadcasted_iota(jnp.int32, bias.shape, 1)
    allowed = (qdoc_ref[0] == kdoc_ref[0]) & (key_pos <= qpos_ref[...])
    bias[...] = jnp.where(allowed, 0.0, BIG_NEG)
    rows, count = bias.shape[0], len(sources) // 2
    for step in range(count):
        part = pl.ds(pl.multiple_of(info[4 + step] * rows, rows), rows)
        mine, other = sources[step][0], sources[count + step][0]
        keys[part, :] = jnp.where(info[3] == 0, mine, other)
        values[part, :] = jnp.where(info[3] == 0, other, mine)


def rotated(projected, gain, cosine, sine):
    scale = lax.rsqrt(jnp.mean(projected * projected, axis=-1, keepdims=True) + EPS)
    unit = projected * scale
    return scale, unit, turn(unit * gain, cosine, sine)


def forward_kernel(info, q_ref, qdoc_ref, kdoc_ref, qpos_ref, cos_ref, sin_ref, gain_ref, *refs):
    *sources, out_ref, total_ref, bias, keys, values = refs

    @pl.when(pl.program_id(1) == 0)
    def _():
        attention_setup(info, sources, qdoc_ref, kdoc_ref, qpos_ref, bias, keys, values)

    _, _, turned = rotated(q_ref[...], gain_ref[...], cos_ref[...], sin_ref[...])
    scores = dot_nt(turned.astype(BF16), keys[...]) * (SCALE * LOG2E) + bias[...]
    highest = jnp.max(scores, axis=-1, keepdims=True)
    exponent = jnp.exp2(scores - highest)
    total = jnp.sum(exponent, axis=-1, keepdims=True)
    probs = (exponent * (1.0 / total)).astype(BF16)
    out_ref[...] = dot(probs, values[...]).astype(BF16)
    total_ref[0, 0] = highest + jnp.log2(total)


def backward_kernel(info, q_ref, qdoc_ref, kdoc_ref, qpos_ref, cos_ref, sin_ref, gain_ref, *refs):
    *sources, total_ref, grad_ref, dq_ref, kept_ref, sent_ref, dgain_ref, bias, key_rows, value_rows, dk_sum, dv_sum = refs
    seq, head = pl.program_id(0), pl.program_id(1)

    @pl.when(head == 0)
    def _():
        attention_setup(info, sources, qdoc_ref, kdoc_ref, qpos_ref, bias, key_rows, value_rows)
        dk_sum[...] = jnp.zeros_like(dk_sum)
        dv_sum[...] = jnp.zeros_like(dv_sum)

    @pl.when((head == 0) & (seq == 0))
    def _():
        dgain_ref[...] = jnp.zeros_like(dgain_ref)

    gain, cosine, sine = gain_ref[...], cos_ref[...], sin_ref[...]
    scale, unit, turned = rotated(q_ref[...], gain, cosine, sine)
    turned = turned.astype(BF16)
    keys, values = key_rows[...], value_rows[...]
    scores = dot_nt(turned, keys) * (SCALE * LOG2E) + bias[...]
    probs = jnp.exp2(scores - total_ref[0, 0])
    grad = grad_ref[...]
    grad_probs = dot_nt(grad, values)
    delta = jnp.sum(probs * grad_probs, axis=-1, keepdims=True)
    grad_scores = (probs * (grad_probs - delta)).astype(BF16)
    dv_sum[...] += dot_tn(probs.astype(BF16), grad)
    dk_sum[...] += dot_tn(grad_scores, turned)
    grad_turned = dot(grad_scores, keys) * SCALE
    grad_gained = turn(grad_turned, cosine, -sine)
    dgain_ref[...] += jnp.sum(grad_gained * unit, axis=0, keepdims=True)
    weighted = grad_gained * gain
    dq_ref[...] = (
        scale * (weighted - unit * jnp.mean(weighted * unit, axis=-1, keepdims=True))
    ).astype(BF16)

    @pl.when(head == pl.num_programs(1) - 1)
    def _():
        shape = kept_ref.shape[:1] + kept_ref.shape[2:]
        dk, dv = dk_sum[...] * SCALE, dv_sum[...]
        kept_ref[:, 0] = jnp.where(info[3] == 0, dk, dv).astype(BF16).reshape(shape)
        sent_ref[:, 0] = jnp.where(info[3] == 0, dv, dk).astype(BF16).reshape(shape)


def attention_specs(rows, length, sources, first=0):
    specs = [
        pl.BlockSpec(memory_space=pltpu.SMEM),
        pl.BlockSpec((rows, HEAD_DIM), lambda s, h: (first + s, h)),
        pl.BlockSpec((1, rows, 1), lambda s, h: (first + s, 0, 0)),
        pl.BlockSpec((1, 1, length), lambda s, h: (first + s, 0, 0)),
        pl.BlockSpec((rows, 1), lambda s, h: (0, 0)),
        pl.BlockSpec((rows, HEAD_DIM), lambda s, h: (0, 0)),
        pl.BlockSpec((rows, HEAD_DIM), lambda s, h: (0, 0)),
        pl.BlockSpec((1, HEAD_DIM), lambda s, h: (0, 0)),
    ]
    return specs + [
        pl.BlockSpec((1, rows, HEAD_DIM), lambda s, h: (first + s, 0, 0)) for _ in sources
    ]


def attention_forward(operands, sources, sequences, heads, rows, length):
    pairs = sequences * heads * rows * length
    return pl.pallas_call(
        forward_kernel,
        grid=(sequences, heads),
        in_specs=attention_specs(rows, length, sources),
        out_specs=[
            pl.BlockSpec((rows, HEAD_DIM), lambda s, h: (s, h)),
            pl.BlockSpec((1, 1, rows, 1), lambda s, h: (s, h, 0, 0)),
        ],
        out_shape=[
            shape_of((sequences * rows, heads * HEAD_DIM), BF16),
            shape_of((sequences, heads, rows, 1), F32),
        ],
        scratch_shapes=[
            pltpu.VMEM((rows, length), F32),
            pltpu.VMEM((length, HEAD_DIM), BF16),
            pltpu.VMEM((length, HEAD_DIM), BF16),
        ],
        compiler_params=pltpu.CompilerParams(vmem_limit_bytes=VMEM_LIMIT),
        cost_estimate=pl.CostEstimate(
            flops=1000, bytes_accessed=1000, transcendentals=0
        ),
    )(*operands, *sources)


def attention_backward(
    operands, sources, totals, grads, first, sequences, heads, rows, length, tokens=()
):
    pairs = sequences * heads * rows * length
    parts = length // rows
    key_value_spec = pl.BlockSpec((parts, 1, rows, HEAD_DIM), lambda s, h: (0, s, 0, 0))
    key_value_shape = shape_of((parts, sequences, rows, HEAD_DIM), BF16)
    count = len(operands) + len(sources) + 2

    def kernel(*refs):
        backward_kernel(*refs[:count], *refs[count + len(tokens) :])

    return pl.pallas_call(
        kernel,
        grid=(sequences, heads),
        in_specs=attention_specs(rows, length, sources, first)
        + [
            pl.BlockSpec((1, 1, rows, 1), lambda s, h: (first + s, h, 0, 0)),
            pl.BlockSpec((rows, HEAD_DIM), lambda s, h: (first + s, h)),
        ]
        + [pl.BlockSpec(memory_space=pl.ANY)] * len(tokens),
        out_specs=[
            pl.BlockSpec((rows, HEAD_DIM), lambda s, h: (s, h)),
            key_value_spec,
            key_value_spec,
            pl.BlockSpec((1, HEAD_DIM), lambda s, h: (0, 0)),
        ],
        out_shape=[
            shape_of((sequences * rows, heads * HEAD_DIM), BF16),
            key_value_shape,
            key_value_shape,
            shape_of((1, HEAD_DIM), F32),
        ],
        scratch_shapes=[
            pltpu.VMEM((rows, length), F32),
            pltpu.VMEM((length, HEAD_DIM), BF16),
            pltpu.VMEM((length, HEAD_DIM), BF16),
            pltpu.VMEM((length, HEAD_DIM), F32),
            pltpu.VMEM((length, HEAD_DIM), F32),
        ],
        compiler_params=pltpu.CompilerParams(vmem_limit_bytes=VMEM_LIMIT),
        cost_estimate=pl.CostEstimate(
            flops=1000, bytes_accessed=1000, transcendentals=0
        ),
    )(*operands, *sources, totals, grads, *tokens)


def key_value_back_kernel(groups, info, key_proj, cosine, sine, gain, *refs):
    *terms, out, dgain = refs
    rows = terms[0].shape[1]
    total = jnp.zeros_like(dgain)
    for group in range(groups):
        grad = total_of([term[group] for term in terms])
        part = slice(group * rows, (group + 1) * rows)
        values_grad = grad
        grad = turn(grad, cosine[...], -sine[...])
        keys = key_proj[part]
        scale = lax.rsqrt(jnp.mean(keys * keys, axis=-1, keepdims=True) + EPS)
        unit = keys * scale
        total = total + jnp.sum(grad * unit, axis=0, keepdims=True)
        weighted = grad * gain[...]
        keys_grad = scale * (weighted - unit * jnp.mean(weighted * unit, axis=-1, keepdims=True))
        out[part, :] = jnp.where(info[3] == 0, keys_grad, values_grad).astype(BF16)
    dgain[...] = jnp.where(info[3] == 0, total, 0.0)


def out_sent_kernel(count, info, attended, *refs):
    *sources, sent, weights = refs

    def write(index, ref):
        start = pl.multiple_of(index * HEAD_DIM, HEAD_DIM)
        weights[pl.ds(start, HEAD_DIM), :] = ref[...]

    place_line(sources, info[0], count, write)
    out_parts(info, CORE, attended, weights, sent)


def out_kept_kernel(info, attended, weights, kept):
    out_parts(info, 0, attended, weights, kept)


def rows_for(info, flip, ref, rows):
    return [
        ref[pl.ds(pl.multiple_of((info[1] ^ (bits | flip)) * rows, rows), rows), :] for bits in FLIPS
    ]


def out_parts(info, flip, attended, weights, out):
    rows, width = out.shape[1:]
    left = jnp.concatenate(rows_for(info, flip, attended, rows), axis=0)
    for start in range(0, width, 512):
        part = slice(start, start + 512)
        out[:, :, part] = dot(left, weights[:, part]).astype(BF16).reshape(4, rows, 512)


def normed_grad_kernel(flip, info, query_grad, key_value_grad, query_weights, key_value_weights, units, out, sums):
    rows, width = out.shape[1:]
    left = jnp.concatenate(rows_for(info, flip, query_grad, rows), axis=0)
    other = jnp.concatenate(rows_for(info, flip, key_value_grad, rows), axis=0)
    unit = jnp.concatenate(rows_for(info, flip, units, rows), axis=0)
    for start in range(0, width, 512):
        part = slice(start, start + 512)
        grad = dot_nt(left, query_weights[part]) + dot_nt(other, key_value_weights[part])
        out[:, :, part] = grad.astype(BF16).reshape(4, rows, 512)
        sums[:, part] = jnp.sum(grad * unit[:, part].astype(F32), axis=0, keepdims=True)


def middle_kernel(info, own, across, aside, tokens, gain, middle, routed, scale_out):
    values = own[...] + across[...].astype(F32) + aside[...].astype(F32) + tokens[...].astype(F32)
    scale = lax.rsqrt(jnp.mean(values * values, axis=-1, keepdims=True) + EPS)
    middle[...] = values
    routed[...] = (values * scale * gain[...]).astype(BF16)
    scale_out[...] = scale


def gradient_spread_kernel(info, weights, *refs):
    *blocks, gathered, attended_grad = refs

    def write(row, ref):
        gathered[pl.ds(row, ref.shape[0]), :] = ref[...]

    place_plane(blocks, info[1], write)
    attended_grad[...] = dot_nt(gathered[...], weights[...]).astype(BF16)


def gates_of(token_rows, router, choices):
    logits = jnp.where(choices, dot(token_rows, router), BIG_NEG)
    exponent = jnp.where(choices, jnp.exp(logits - jnp.max(logits, axis=-1, keepdims=True)), 0.0)
    return exponent / jnp.maximum(jnp.sum(exponent, axis=-1, keepdims=True), 1e-30)


def gates_kernel(info, routed, router, picked, gates):
    gates[...] = gates_of(routed[...], router[...], picked[...][:, : gates.shape[1]] > 0.5)


def dispatch_kernel(steps, info, table, *refs):
    *blocks, out = refs
    members = out.shape[0]
    slots = table.shape[2] // members
    for at, step in enumerate(steps):
        block = block_of_step(blocks, info, steps, step)
        rows = dot_tn(table[info[4 + step]], block).astype(BF16)
        out[:, at * slots : (at + 1) * slots, :] = rows.reshape(members, slots, out.shape[2])


def dispatch_with_choices_kernel(steps, info, table, picked, *refs):
    *blocks, out = refs
    members, _, width = out.shape
    slots = table.shape[2] // members
    for at, step in enumerate(steps):
        place = table[info[4 + step]]
        part = slice(at * slots, (at + 1) * slots)
        rows = dot_tn(place, block_of_step(blocks, info, steps, step)).astype(BF16)
        choices = dot_tn(place, picked[info[4 + step]]).astype(BF16)
        model = rows.shape[1]
        out[:, part, :model] = rows.reshape(members, slots, model)
        out[:, part, model:] = choices.reshape(members, slots, width - model)


def combined(table, place, arrived, at):
    members, _, width = arrived.shape
    slots = table.shape[2] // members
    rows = arrived[:, at * slots : (at + 1) * slots, :].reshape(members * slots, width)
    return dot(table[place], rows)


def combine_kernel(first, info, table, arrived, *outs):
    for at, out in enumerate(outs):
        out[...] = combined(table, info[4 + first + at], arrived, at).astype(out.dtype)


def forward_kernel_of_parts(info, part, arrived, out):
    out[...] = (part[...].astype(F32) + arrived[...].astype(F32)).astype(BF16)


def combine_stacked_kernel(first, info, table, arrived, out):
    slots = table.shape[2] // arrived.shape[0]
    steps = arrived.shape[1] // slots
    for step in range(out.shape[0]):
        place = info[4 + step]
        if first <= step < first + steps:
            out[place] = combined(table, place, arrived, step - first).astype(BF16)
        else:
            out[place] = jnp.zeros(out.shape[1:], BF16)


def copy_kernel(info, value, out):
    out[...] = value[...]


def expert_prepare_kernel(info, arrived, down, grad_hidden):
    members, model = arrived.shape[0], down.shape[2]
    slots = grad_hidden.shape[0] // members
    rows = arrived[:, :, :model].reshape(members * slots, model)
    for start in range(0, FFE, 256):
        grad = dot_nt(rows, down[0, start : start + 256, :])
        grad_hidden[:, start : start + 256] = grad


def expert_kernel(experts, info, arrived, grad_hidden, dy_rows, router, weights, act, hidden_out, back):
    members, slots, width = arrived.shape
    rows = members * slots
    inputs = arrived[...].reshape(rows, width)
    chosen = dy_rows[:, :, width:].reshape(rows, -1)[:, :experts] > 0.5
    own = lax.broadcasted_iota(jnp.int32, (rows, experts), 1) == info[2]
    gate = jnp.sum(
        jnp.where(own, gates_of(inputs, router[...], chosen), 0.0), axis=-1, keepdims=True
    )
    grad_gate = jnp.zeros((rows, 1), F32)
    for start in range(0, FFE, 256):
        piece = slice(start, start + 256)
        lower = slice(FFE + start, FFE + start + 256)
        gate_in = dot(inputs, weights[0, :, piece])
        up_in = dot(inputs, weights[0, :, lower])
        grad_in = grad_hidden[:, piece]
        sigmoid = 1.0 / (1.0 + jnp.exp(-gate_in))
        silu = gate_in * sigmoid
        hidden = silu * up_in
        grad_gate = grad_gate + jnp.sum(hidden * grad_in, axis=-1, keepdims=True)
        scaled = grad_in * gate
        act[:, piece] = (scaled * up_in * (sigmoid + silu * (1.0 - sigmoid))).astype(BF16)
        act[:, lower] = (scaled * silu).astype(BF16)
        hidden_out[:, piece] = (hidden * gate).astype(BF16)
    for start in range(0, width, 512):
        piece = slice(start, start + 512)
        grad = dot_nt(act[...], weights[0, piece, :]).astype(BF16)
        back[:, :, piece] = grad.reshape(members, slots, 512)
    extra = back.shape[2] - width
    high = grad_gate.astype(BF16).astype(F32)
    lane = lax.broadcasted_iota(jnp.int32, (rows, extra), 1)
    columns = jnp.where(lane == info[2], high, 0.0)
    columns = columns + jnp.where(lane == info[2] + experts, grad_gate - high, 0.0)
    back[:, :, width:] = columns.astype(BF16).reshape(members, slots, extra)


def results_kernel(info, down, hidden, out):
    members, slots, width = out.shape
    for start in range(0, width, 512):
        piece = slice(start, start + 512)
        rows = dot(hidden[...], down[0, :, piece]).astype(BF16)
        out[:, :, piece] = rows.reshape(members, slots, 512)


def gate_up_grad(rows, acts, tokens):
    count, groups = rows[0].shape[0], len(rows)
    width, columns = rows[0].shape[1], acts[0].shape[1]
    tile = 512

    def kernel(*refs):
        out = refs[-1]
        total = dot_tn(refs[0][...], refs[groups][...])
        for group in range(1, groups):
            total = total + dot_tn(refs[group][...], refs[groups + group][...])
        out[0] = total

    return pl.pallas_call(
        kernel,
        grid=(width // tile,),
        in_specs=[pl.BlockSpec((count, tile), lambda i: (0, i))] * groups
        + [pl.BlockSpec((count, columns), lambda i: (0, 0))] * groups
        + [pl.BlockSpec(memory_space=pl.ANY)] * len(tokens),
        out_specs=pl.BlockSpec((1, tile, columns), lambda i: (0, i, 0)),
        out_shape=shape_of((1, width, columns), F32),
        compiler_params=pltpu.CompilerParams(vmem_limit_bytes=VMEM_LIMIT),
        cost_estimate=pl.CostEstimate(
            flops=1000, bytes_accessed=1000, transcendentals=0
        ),
    )(*rows, *acts, *tokens)


def down_grad(hiddens, arrived, model, tokens):
    groups, tile = len(hiddens), 256
    count = hiddens[0].shape[0]

    def kernel(*refs):
        total = 0.0
        for left, right in zip(refs[:groups], refs[groups : 2 * groups]):
            total = total + dot_tn(left[...], right[:, :, :model].reshape(count, model))
        refs[-1][0] = total

    return pl.pallas_call(
        kernel,
        grid=(FFE // tile,),
        in_specs=[pl.BlockSpec((count, tile), lambda i: (0, i))] * groups
        + [pl.BlockSpec(arrived[0].shape, lambda i: (0, 0, 0))] * groups
        + [pl.BlockSpec(memory_space=pl.ANY)] * len(tokens),
        out_specs=pl.BlockSpec((1, tile, model), lambda i: (0, i, 0)),
        out_shape=shape_of((1, FFE, model), F32),
        compiler_params=pltpu.CompilerParams(vmem_limit_bytes=VMEM_LIMIT),
        cost_estimate=pl.CostEstimate(flops=1000, bytes_accessed=1000, transcendentals=0),
    )(*hiddens, *arrived, *tokens)


def token_back_kernel(info, gates, router, middle, scale, gain, cotangent, routed, *refs):
    *terms, grad_middle, grad_branch, grad_gain, grad_router = refs
    width = middle.shape[1]
    experts = gates.shape[1]
    total = total_of([term[...] for term in terms])
    extra = total[:, width:]
    grad_gates = extra[:, :experts] + extra[:, experts : 2 * experts]
    values = gates[...]
    grad_logits = values * (grad_gates - jnp.sum(values * grad_gates, axis=-1, keepdims=True))
    grad_logits = grad_logits.astype(BF16)
    grad_routed = total[:, :width] + dot_nt(grad_logits, router[...])
    unit = middle[...] * scale[...]
    grad_gain[...] = jnp.sum(grad_routed * unit, axis=0, keepdims=True)
    weighted = grad_routed * gain[...]
    grad = cotangent[...].astype(F32) + scale[...] * (
        weighted - unit * jnp.mean(weighted * unit, axis=-1, keepdims=True)
    )
    grad_middle[...] = grad
    grad_branch[...] = grad.astype(BF16)
    grad_router[...] = dot_tn(routed[...], grad_logits)


def input_grad_kernel(info, own, across, aside, tokens, gain, grad_middle, out):
    weighted = (own[...] + across[...].astype(F32) + aside[...].astype(F32)) * gain[...]
    values = tokens[...].astype(F32)
    scale = lax.rsqrt(jnp.mean(values * values, axis=-1, keepdims=True) + EPS)
    unit = values * scale
    out[...] = grad_middle[...] + scale * (
        weighted - unit * jnp.mean(weighted * unit, axis=-1, keepdims=True)
    )


def mixed_kernel(info, middle, *refs):
    *terms, out = refs
    out[...] = (middle[...] + total_of([term[...] for term in terms])).astype(BF16)


def unpack_weights_kernel(rep_size, info, arrived, queries, keys, values):
    members, _, columns = arrived.shape
    heads = columns // HEAD_DIM - 1
    for member in range(members):
        group, rep = member // rep_size, member % rep_size
        for j in range(heads):
            head = group * heads * rep_size + j * rep_size + rep
            queries[:, head * HEAD_DIM : (head + 1) * HEAD_DIM] = arrived[
                member, :, j * HEAD_DIM : (j + 1) * HEAD_DIM
            ].astype(F32)
        out = values if rep else keys
        out[:, group * HEAD_DIM : (group + 1) * HEAD_DIM] = arrived[
            member, :, heads * HEAD_DIM :
        ].astype(F32)


def body(
    tokens,
    segments,
    routes,
    priority,
    w_query,
    key_matrix,
    value_matrix,
    w_out,
    w_router,
    attn_gain,
    moe_gain,
    query_gain,
    key_norm_weight,
    w_gate_up,
    w_down,
    cotangent,
):
    own_rows, width = tokens.shape[1], tokens.shape[2]
    length = segments.shape[1]
    dp_size, seq_size, rep_size = (lax.axis_size(name) for name in ALL)
    devices = dp_size * seq_size * rep_size
    members = dp_size * rep_size
    dp_at, seq_at, rep_at = (lax.axis_index(name) for name in ALL)
    experts = devices * w_gate_up.shape[0]
    capacity = own_rows * TOPK // experts
    plane_slots = members * capacity
    depth = w_router.shape[0]
    heads = QUERY_HEADS // members
    head_width = heads * HEAD_DIM
    rows = rep_size * own_rows
    plane_rows = members * own_rows
    chunk = members * depth
    extra = -(-2 * experts // LANES) * LANES
    entry = jnp.arange(4 + seq_size, dtype=jnp.int32)
    info = (entry - 4) ^ seq_at if seq_size == 4 else entry - 4
    places = (seq_at, lax.axis_index(PLANE), lax.axis_index(ALL), rep_at)
    for index, place in enumerate(places):
        info = jnp.where(entry == index, place, info)
    own_tokens, own_cotangent = tokens[0], cotangent[0]

    token_blocks = plane_gather(own_tokens)
    query_part, key_value_part = pack_weights(
        w_query, key_matrix, value_matrix, members, rep_size, heads
    )
    cotangent_sources = [lax.all_gather(own_cotangent, "seq")]
    query_part = swap(after(query_part, token_blocks[1], token_blocks[4]), PLANE)
    router_rows = w_router.size // LANES
    own_documents = lax.dynamic_slice_in_dim(segments, (seq_at * rep_size + rep_at) * own_rows, own_rows, 1)
    packet = run(
        functools.partial(packet_kernel, rep_size),
        [shape_of((devices, depth + PACKET_ROWS + router_rows, LANES), BF16)],
        info,
        key_value_part,
        w_router.reshape(router_rows, LANES),
        routes[0],
        priority,
        own_documents,
        moe_gain[None],
        query_gain[None],
        key_norm_weight[None],
        attn_gain[None],
        tokens=(query_part, *token_blocks[5:7]),
    )[0]
    packet = swap(packet, ALL)
    arrival = packet
    router = packet[:, depth + PACKET_ROWS :].reshape(devices, depth, experts)
    router = router.reshape(width, experts)
    packet = packet[:, depth : depth + PACKET_ROWS]
    query_part = after(query_part.reshape(chunk, head_width), arrival, cotangent_sources[0])
    query_sources = [lax.all_gather(query_part, "seq")]

    packet = packet.astype(F32)
    documents = packet[:, DOCUMENT_ROW].reshape(dp_size, length).astype(jnp.int32)
    second_gain = packet[:, MOE_GAIN_ROW, :depth].reshape(1, width)
    query_norm_gain = jnp.sum(packet[:, QUERY_GAIN_ROW], axis=0, keepdims=True)
    meta = packet.reshape(dp_size, seq_size, rep_size, PACKET_ROWS, LANES)
    meta = pick(pick(meta, dp_at), rep_at, 1).astype(jnp.int32)
    choice_ids, priority_rank = meta[:, :TOPK], meta[:, PRIORITY_ROW]
    expert_lanes = -(-experts // LANES) * LANES
    expert_ids = jnp.arange(expert_lanes, dtype=jnp.int32)
    picked = jnp.any(choice_ids[:, :, :, None] == expert_ids, axis=1)
    earlier = (priority_rank[:, None, :] < priority_rank[:, :, None]).astype(BF16)
    plane_picked = pick(
        picked[:, :, :experts].reshape(seq_size, own_rows, dp_size, seq_size, rep_size), seq_at, 3
    ).reshape(seq_size, own_rows, members)
    slot_index = jnp.einsum(
        "bts,bse->bte", earlier, plane_picked.astype(BF16), preferred_element_type=F32
    ).astype(jnp.int32)
    slot_ids = jnp.arange(capacity, dtype=jnp.int32)
    table = plane_picked[..., None] & (slot_index[..., None] == slot_ids)
    table = table.reshape(seq_size, own_rows, plane_slots).astype(BF16)
    picked = picked.astype(BF16)

    units, first_gain = run(
        functools.partial(normalize_kernel, depth),
        [shape_of((plane_rows, width), BF16), shape_of((1, width), F32)],
        info,
        arrival,
        *token_blocks,
    )
    positions = seq_at * rows + jnp.arange(rows, dtype=jnp.int32)
    frequency = THETA ** (-2.0 * jnp.arange(HEAD_DIM // 2, dtype=F32) / HEAD_DIM)
    angles = positions.astype(F32)[:, None] * jnp.concatenate([frequency, frequency])[None, :]
    sign = jnp.where(jnp.arange(HEAD_DIM) < HEAD_DIM // 2, -1.0, 1.0)
    cosine, sine = jnp.cos(angles), jnp.sin(angles) * sign[None, :]
    key_proj, key_value_rows, key_value_weights, key_norm_gain = run(
        key_value_kernel,
        [
            shape_of((plane_rows, HEAD_DIM), F32),
            shape_of((dp_size, rows, HEAD_DIM), BF16),
            shape_of((width, HEAD_DIM), BF16),
            shape_of((1, HEAD_DIM), F32),
        ],
        info,
        units,
        arrival,
        cosine,
        sine,
        flops=2 * plane_rows * width * HEAD_DIM,
    )
    mine = line_steps(line_gather(key_value_rows, seq_size))
    other = [plane_move(block, SIDE) for block in mine[:-1]]
    query_weights, query_proj = run(
        functools.partial(query_kernel, seq_size, dp_size),
        [shape_of((width, head_width), BF16), shape_of((plane_rows, head_width), F32)],
        info,
        units,
        *query_sources,
        flops=2 * plane_rows * width * head_width,
    )
    key_values = mine + other + [plane_move(mine[-1], SIDE)]

    whole_heads = w_out.shape[0] == HEAD_DIM
    if whole_heads:
        held_w_out = run(
            copy_kernel, [shape_of(w_out.shape, BF16)], info, w_out, tokens=mine[-1:]
        )[0]
        out_sources = [lax.all_gather(held_w_out, "seq")]
    else:
        group = lax.all_gather(w_out, ("seq", "rep"), axis=0, tiled=True)
        group = group.reshape(heads, rep_size, HEAD_DIM, width)
        out_sources = [pick(group, rep_at, 1)]

    steps = list(range(seq_size))
    groups = [steps[: seq_size // 2], steps[seq_size // 2 :]]
    group_slots = len(groups[0]) * capacity
    group_rows = members * group_slots
    group_rows = members * group_slots
    def send_cotangent(group, held, *late):
        outgoing = run(
            functools.partial(dispatch_with_choices_kernel, group),
            [shape_of((members, group_slots, width + expert_lanes), BF16)],
            info,
            table,
            picked,
            *cotangent_sources,
            tokens=held,
            flops=2 * own_rows * len(group) * plane_slots * width,
        )[0]
        return swap(after(outgoing, *late) if late else outgoing, PLANE)

    dy_rows = [send_cotangent(groups[0], (key_value_rows,))]
    dy_rows.append(
        send_cotangent(groups[1], mine[2:3], dy_rows[0], query_proj, *key_values[seq_size:])
    )
    grad_hidden = [
        run(
            expert_prepare_kernel,
            [shape_of((group_rows, FFE), F32)],
            info,
            rows_,
            w_down,
            filler=True,
        )[0]
        for rows_ in dy_rows
    ]

    query_doc = lax.dynamic_slice_in_dim(documents, seq_at * rows, rows, axis=1)
    operands = (
        info,
        query_proj,
        query_doc[:, :, None],
        documents[:, None, :],
        positions[:, None],
        cosine,
        sine,
        query_norm_gain,
    )
    attended, totals = attention_forward(operands, key_values, dp_size, heads, rows, length)
    parts_shape = shape_of((4, own_rows, width), BF16)
    part_flops = 8 * own_rows * head_width * width
    sent, out_weights = run(
        functools.partial(out_sent_kernel, heads),
        [parts_shape, shape_of((head_width, width), BF16)],
        info,
        attended,
        *out_sources,
        tokens=(dy_rows[1],),
        flops=part_flops,
    )
    kept = run(out_kept_kernel, [parts_shape], info, attended, out_weights, flops=part_flops)[0]
    row_f32, row_bf16 = shape_of((own_rows, width), F32), shape_of((own_rows, width), BF16)
    *plane_terms, _ = plane_reduce(info, sent, kept)
    middle, routed, scale_second = run(
        middle_kernel,
        [row_f32, row_bf16, shape_of((own_rows, 1), F32)],
        info,
        *plane_terms,
        own_tokens,
        second_gain,
    )

    if seq_size == 4:
        half_rows = own_rows // 2
        second = [line_move(routed[:half_rows], 2), line_move(routed[half_rows:], 2)]
        routed_far = second + [line_move(piece, 1) for piece in second]
        routed_near = [routed, line_move(routed, 1)]
        token = second[:1]
    else:
        routed_near = routed_far = line_gather(routed, seq_size)
        token = ()
    own_picked = pick(picked, seq_at)
    gates = run(
        gates_kernel, [shape_of((own_rows, experts), F32)], info, routed, router, own_picked
    )[0]
    arrived = []
    for group, routed_sources in zip(groups, (routed_near, routed_far)):
        outgoing = run(
            functools.partial(dispatch_kernel, group),
            [shape_of((members, group_slots, width), BF16)],
            info,
            table,
            *routed_sources,
            tokens=token,
            flops=2 * own_rows * len(group) * plane_slots * width,
        )[0]
        arrived.append(swap(outgoing, PLANE))
        token = arrived[-1:]
    worked, token = {}, ()
    for at in (1, 0):
        worked[at] = run(
            functools.partial(expert_kernel, experts),
            [
                shape_of((group_rows, 2 * FFE), BF16),
                shape_of((group_rows, FFE), BF16),
                shape_of((members, group_slots, width + extra), BF16),
            ],
            info,
            arrived[at],
            grad_hidden[at],
            dy_rows[at],
            router,
            w_gate_up,
            tokens=token,
            flops=8 * group_rows * width * FFE,
        )
        token = (worked[at][2],)
    acts, hiddens, backs = zip(worked[0], worked[1])

    def combine(at, rows_, columns, held=()):
        group = groups[at]
        return run(
            functools.partial(combine_kernel, group[0]),
            [shape_of((own_rows, columns), BF16)] * len(group),
            info,
            table,
            rows_,
            tokens=held,
            flops=2 * own_rows * len(group) * plane_slots * columns,
        )

    def send_groups(near, far):
        if seq_size != 4:
            return line_reduce(jnp.stack(list(near) + list(far)), seq_at, seq_size)
        return [near[0], line_move(far[0], 2), line_move(near[1], 1)]

    pairs_far, pairs_near = swap(backs[1], PLANE), swap(backs[0], PLANE)
    far_parts = combine(1, pairs_far, width + extra)
    grad_down = down_grad(hiddens, dy_rows, width, far_parts[:1])
    if seq_size == 4:
        far_parts = run(
            forward_kernel_of_parts,
            [shape_of((own_rows, width + extra), BF16)],
            info,
            far_parts[0],
            line_move(far_parts[1], 1),
            tokens=(grad_down,),
        )
    results = [
        run(
            results_kernel,
            [shape_of((members, group_slots, width), BF16)],
            info,
            w_down,
            hidden,
            tokens=far_parts[:1],
            filler=True,
        )[0]
        for hidden in hiddens
    ]
    near_parts = combine(0, pairs_near, width + extra, far_parts[:1])
    pair_terms = send_groups(near_parts, far_parts)
    grad_gate_up = gate_up_grad(
        [rows_.reshape(group_rows, width) for rows_ in arrived], acts, near_parts[:1]
    )
    results_far = swap(results[1], PLANE)
    grad_middle, grad_branch, grad_moe_gain, grad_router = run(
        token_back_kernel,
        [row_f32, row_bf16, shape_of((1, width), F32), shape_of((width, experts), F32)],
        info,
        gates,
        router,
        middle,
        scale_second,
        second_gain,
        own_cotangent,
        routed,
        *pair_terms,
        tokens=(grad_gate_up, results_far, grad_down, results[0]),
    )
    branch_blocks = plane_gather(grad_branch)
    far_stacked = run(
        functools.partial(combine_stacked_kernel, groups[1][0]),
        [shape_of((seq_size, own_rows, width), BF16)],
        info,
        table,
        results_far,
        tokens=branch_blocks[5:7],
        flops=2 * own_rows * len(groups[1]) * plane_slots * width,
    )[0]
    grad_branch, grad_attended = run(
        gradient_spread_kernel,
        [shape_of((plane_rows, width), BF16), shape_of((plane_rows, head_width), BF16)],
        info,
        out_weights,
        *branch_blocks,
        tokens=(far_stacked,),
        flops=2 * plane_rows * head_width * width,
    )
    far_sum = lax.psum_scatter(far_stacked, "seq", scatter_dimension=0, tiled=False)
    results_near = swap(after(results[0], grad_attended), PLANE)
    half = dp_size // 2
    first_call = attention_backward(
        operands, key_values, totals, grad_attended, 0, half, heads, rows, length
    )
    grad_out = dot_tn(after(attended, first_call[0]), grad_branch).astype(BF16)
    second_call = attention_backward(
        operands,
        key_values,
        totals,
        grad_attended,
        half,
        half,
        heads,
        rows,
        length,
        (grad_out, far_sum),
    )
    query_grads, kept_grads, sent_grads, gain_grads = zip(first_call, second_call)
    if whole_heads:
        grad_out = grad_out.reshape(heads, HEAD_DIM, width)
        grad_out = lax.psum_scatter(grad_out, "seq", scatter_dimension=0, tiled=False)
    else:
        group = jnp.zeros((heads, rep_size, HEAD_DIM, width), F32)
        group = lax.dynamic_update_index_in_dim(
            group, grad_out.reshape(heads, HEAD_DIM, width).astype(F32), rep_at, 1
        )
        grad_out = lax.psum_scatter(
            group.reshape(heads * rep_size * HEAD_DIM, width),
            ("seq", "rep"),
            scatter_dimension=0,
            tiled=True,
        )
    if seq_size == 4:
        near_terms = near_parts = combine(0, results_near, width, second_call[:1])
        near_terms = [near_terms[0], line_move(near_terms[1], 1)]
    else:
        near_terms = [
            lax.psum_scatter(
                run(
                    functools.partial(combine_stacked_kernel, 0),
                    [shape_of((seq_size, own_rows, width), BF16)],
                    info,
                    table,
                    results_near,
                )[0],
                "seq",
                scatter_dimension=0,
                tiled=False,
            )
        ]
    result_terms = near_terms + [far_sum.reshape(own_rows, width)]
    grad_query_proj = jnp.concatenate(query_grads)
    grad_query_gain = gain_grads[0] + gain_grads[1]
    kept_grads = [
        kept.astype(F32) + plane_move(sent, SIDE).astype(F32)
        for kept, sent in zip(kept_grads, (sent_grads[0], after(sent_grads[1], results_near)))
    ]
    grad_key_value = jnp.concatenate(kept_grads, axis=1).astype(BF16)
    key_value_terms = line_reduce(grad_key_value, seq_at, seq_size)
    grad_key_value, grad_key_gain = run(
        functools.partial(key_value_back_kernel, dp_size),
        [shape_of((plane_rows, HEAD_DIM), BF16), shape_of((1, HEAD_DIM), F32)],
        info,
        key_proj,
        cosine,
        sine,
        key_norm_gain,
        *key_value_terms,
        tokens=near_parts[:1],
    )

    def weight_parts(left, grad):
        parts = dot_tn(left, grad).astype(BF16)
        parts = parts.reshape(dp_size, seq_size, rep_size * depth, grad.shape[1])
        return parts.transpose(1, 0, 2, 3)

    query_parts = weight_parts(units, grad_query_proj)

    def normed_grad(flip, held=()):
        return run(
            functools.partial(normed_grad_kernel, flip),
            [parts_shape, shape_of((1, width), F32)],
            info,
            grad_query_proj,
            grad_key_value,
            query_weights,
            key_value_weights,
            units,
            tokens=held,
            flops=8 * own_rows * (head_width + HEAD_DIM) * width,
        )

    sent, sent_sums = normed_grad(CORE, (grad_out,))
    kept, kept_sums = normed_grad(0)
    weights_total = lax.psum_scatter(
        jnp.concatenate([query_parts, weight_parts(units, grad_key_value)], axis=-1),
        "seq",
        scatter_dimension=0,
        tiled=False,
    ).reshape(members, depth, head_width + HEAD_DIM)
    *plane_terms, mark = plane_reduce(info, sent, kept)

    pieces = (grad_router, sent_sums + kept_sums, grad_moe_gain, grad_query_gain, grad_key_gain)
    small = jnp.concatenate([piece.reshape(devices, -1) for piece in pieces], axis=-1)
    small = jnp.sum(swap(small, ALL), axis=0)
    bounds = [0]
    for piece in pieces:
        bounds.append(bounds[-1] + piece.size // devices)
    small = [small[a:b] for a, b in zip(bounds[:-1], bounds[1:])]
    weights_arrived = swap(weights_total, PLANE)
    grad_query, grad_key, grad_value = run(
        functools.partial(unpack_weights_kernel, rep_size),
        [shape_of(w_query.shape, F32)] + [shape_of(key_matrix.shape, F32)] * 2,
        info,
        weights_arrived,
    )
    mixed = run(
        mixed_kernel, [row_bf16], info, middle, *result_terms, tokens=plane_terms[1:]
    )[0]
    input_grad = run(
        input_grad_kernel,
        [row_f32],
        info,
        *plane_terms,
        own_tokens,
        first_gain,
        grad_middle,
    )[0]

    return (
        mixed[None],
        input_grad[None],
        grad_query,
        grad_key,
        grad_value,
        grad_out.astype(F32),
        small[0].reshape(depth, experts),
        small[1] / attn_gain.astype(F32),
        small[2],
        small[3],
        small[4],
        grad_gate_up,
        grad_down,
    )


def solution(mesh):
    tokens_spec = P("dp", ("seq", "rep"), None)
    rows_spec = P(ALL, None)
    vector_spec = P(ALL)
    expert_spec = P(ALL, None, None)
    return jax.shard_map(
        body,
        mesh=mesh,
        in_specs=(
            (tokens_spec, P("dp", None), tokens_spec, P("dp", ("seq", "rep")))
            + (rows_spec,) * 5
            + (vector_spec,) * 4
            + (expert_spec, expert_spec, tokens_spec)
        ),
        out_specs=(
            (tokens_spec, tokens_spec)
            + (rows_spec,) * 5
            + (vector_spec,) * 4
            + (expert_spec, expert_spec)
        ),
        check_vma=False,
    )
```

```python
import functools

import jax
import jax.numpy as jnp
from jax import lax
from jax.experimental import pallas as pl
from jax.experimental.pallas import tpu as pltpu
from jax.sharding import PartitionSpec as P

QUERY_HEADS = 32
KEY_VALUE_HEADS = 4
HEAD_DIM = 128
FFE = 768
TOPK = 8

EPS = 1e-06
THETA = 1000000.0
BIG_NEG = -1e30
LOG2E = 1.4426950408889634
ALL = ("dp", "seq", "rep")
PLANE = ("dp", "rep")
F32 = jnp.float32
BF16 = jnp.bfloat16
VMEM_LIMIT = 56 * 1024 * 1024
SCALE = HEAD_DIM ** (-0.5)
SIDE, CORE, CROSS = 1, 2, 4
FLIPS = (CROSS | SIDE, CROSS, SIDE, 0)
LANES = 128
PRIORITY_ROW, DOCUMENT_ROW, MOE_GAIN_ROW, QUERY_GAIN_ROW, KEY_GAIN_ROW, ATTN_GAIN_ROW, PACKET_ROWS = 8, 9, 10, 11, 12, 13, 16


def dot(a, b):
    return jnp.dot(a, b, preferred_element_type=F32)


def dot_nt(a, b):
    return lax.dot_general(a, b, (((1,), (1,)), ((), ())), preferred_element_type=F32)


def dot_tn(a, b):
    return lax.dot_general(a, b, (((0,), (0,)), ((), ())), preferred_element_type=F32)


def after(value, *earlier):
    return pl.pallas_call(
        lambda *refs: None,
        in_specs=[pl.BlockSpec(memory_space=pl.ANY)] * (1 + len(earlier)),
        out_specs=pl.BlockSpec(memory_space=pl.ANY),
        out_shape=jax.ShapeDtypeStruct(value.shape, value.dtype),
        input_output_aliases={0: 0},
        cost_estimate=pl.CostEstimate(flops=1000, bytes_accessed=1000, transcendentals=0),
    )(value, *earlier)


def swap(blocks, axes):
    return lax.all_to_all(blocks, axes, split_axis=0, concat_axis=0, tiled=True)


def spread(shard, axes, count):
    return swap(jnp.broadcast_to(shard[None], (count,) + shard.shape), axes)


def shape_of(shape, dtype):
    return jax.ShapeDtypeStruct(shape, dtype)


def run(kernel, outs, *operands, tokens=(), flops=0, filler=False):
    in_specs = [pl.BlockSpec(memory_space=pltpu.SMEM)]
    in_specs += [pl.BlockSpec(memory_space=pltpu.VMEM)] * (len(operands) - 1)
    in_specs += [pl.BlockSpec(memory_space=pl.ANY)] * len(tokens)
    touched = sum(o.size * o.dtype.itemsize for o in operands[1:])
    touched += sum(o.size * o.dtype.itemsize for o in outs)
    if filler:
        flops, touched = 1000, 1000

    def body(*refs):
        kernel(*refs[: len(operands)], *refs[len(operands) + len(tokens) :])

    return pl.pallas_call(
        body,
        in_specs=in_specs,
        out_specs=[pl.BlockSpec(memory_space=pltpu.VMEM)] * len(outs),
        out_shape=outs,
        compiler_params=pltpu.CompilerParams(vmem_limit_bytes=VMEM_LIMIT),
        cost_estimate=pl.CostEstimate(
            flops=int(flops), bytes_accessed=int(touched), transcendentals=0
        ),
    )(*operands, *tokens)


def plane_move(block, bits):
    return lax.ppermute(block, PLANE, [(index, index ^ bits) for index in range(8)])


def plane_gather(block):
    half = block.shape[0] // 2
    across, aside, core = (plane_move(block, bits) for bits in (CROSS, SIDE, CORE))
    far = [plane_move(across[:half], SIDE), plane_move(aside[half:], CROSS)]
    across_core, aside_core = plane_move(across, CORE), plane_move(aside, CORE)
    far_core = [plane_move(piece, CORE) for piece in far]
    return [block, aside, core, aside_core, across] + far + [across_core] + far_core


def place_plane(refs, member, write):
    rows = refs[0].shape[0]
    offsets = [(0, 0), (1, 0), (2, 0), (3, 0), (4, 0), (5, 0), (5, rows // 2), (6, 0), (7, 0), (7, rows // 2)]
    for ref, (bits, start) in zip(refs, offsets):
        write(pl.multiple_of((member ^ bits) * rows + start, rows // 2), ref)


def first_sums(_, arrived, kept, far_low, far_high, across, aside, own):
    half = far_low.shape[0]
    sums = [arrived[i].astype(F32) + kept[i].astype(F32) for i in range(4)]
    far_low[...] = sums[0][:half].astype(BF16)
    far_high[...] = sums[0][half:].astype(BF16)
    across[...] = sums[1].astype(BF16)
    aside[...] = sums[2].astype(BF16)
    own[...] = sums[3]


def second_sums(_, across, aside, from_across, from_aside, across_out, aside_out):
    half = from_across.shape[0]
    across_out[:half] = across[:half]
    across_out[half:] = (across[half:].astype(F32) + from_aside[...].astype(F32)).astype(BF16)
    aside_out[:half] = (aside[:half].astype(F32) + from_across[...].astype(F32)).astype(BF16)
    aside_out[half:] = aside[half:]


def plane_reduce(info, sent, kept):
    _, rows, width = sent.shape
    piece, whole = shape_of((rows // 2, width), BF16), shape_of((rows, width), BF16)
    arrived = plane_move(sent, CORE)
    far_low, far_high, across, aside, own = run(
        first_sums, [piece, piece, whole, whole, shape_of((rows, width), F32)], info, arrived, kept
    )
    from_across, from_aside = plane_move(far_low, CROSS), plane_move(far_high, SIDE)
    across, aside = run(
        second_sums, [whole, whole], info, across, aside, from_across, from_aside
    )
    return own, plane_move(across, CROSS), plane_move(aside, SIDE), across


def line_move(block, bits):
    return lax.ppermute(block, "seq", [(place, place ^ bits) for place in range(4)])


def line_gather(block, count):
    if count != 4:
        return [spread(block, "seq", count)]
    near, second = line_move(block, 1), line_move(block, 2)
    return [block, near, second, line_move(after(second, near), 1)]


def line_gather_near(block, count):
    return [block, line_move(block, 1)] if count == 4 else [block]


def place_line(refs, place, count, write):
    for at in range(count):
        if len(refs) == 1:
            write(at, refs[0].at[at])
        else:
            write(place ^ at, refs[at])


def needed(sources, steps):
    return sources if len(sources) == 1 else [sources[step] for step in steps]


def block_of_step(refs, info, steps, step):
    if len(refs) == 1:
        return refs[0][info[4 + step]]
    pieces = len(refs) // len(steps)
    at = steps.index(step) * pieces
    return jnp.concatenate([ref[...] for ref in refs[at : at + pieces]], axis=0)


def line_steps(blocks):
    if len(blocks) == 1:
        return [blocks[0][step] for step in range(blocks[0].shape[0])]
    return blocks


def line_forward(part, crossing):
    return (part.astype(F32) + line_move(crossing, 1).astype(F32)).astype(BF16)


def line_reduce(parts, place, count):
    if count != 4:
        return [jnp.sum(swap(parts, "seq").astype(F32), axis=0)]
    own, near, second, crossing = (pick(parts, place ^ bits) for bits in range(4))
    return [own, line_move(line_forward(second, crossing), 2), line_move(near, 1)]


def total_of(terms):
    return sum(term.astype(F32) for term in terms)


def pick(blocks, index, axis=0):
    return lax.dynamic_index_in_dim(blocks, index, axis, keepdims=False)


def pack_weights_kernel(*refs):
    *query_refs, key_ref, value_ref, query_out, key_value_out = refs
    for j, ref in enumerate(query_refs):
        query_out[0, :, j * HEAD_DIM : (j + 1) * HEAD_DIM] = ref[...]
    takes_keys = lax.rem(pl.program_id(0), 2) == 0
    key_value_out[0] = jnp.where(takes_keys, key_ref[...], value_ref[...])


def pack_weights(w_query, key_matrix, value_matrix, members, rep_size, heads):
    depth = w_query.shape[0]
    group = heads * rep_size

    def head_spec(j):
        return pl.BlockSpec(
            (depth, HEAD_DIM), lambda m: (0, (m // rep_size) * group + j * rep_size + m % rep_size)
        )

    group_spec = pl.BlockSpec((depth, HEAD_DIM), lambda m: (0, m // rep_size))
    return pl.pallas_call(
        pack_weights_kernel,
        grid=(members,),
        in_specs=[head_spec(j) for j in range(heads)]
        + [group_spec, group_spec],
        out_specs=[
            pl.BlockSpec((1, depth, heads * HEAD_DIM), lambda m: (m, 0, 0)),
            pl.BlockSpec((1, depth, HEAD_DIM), lambda m: (m, 0, 0)),
        ],
        out_shape=[
            shape_of((members, depth, heads * HEAD_DIM), BF16),
            shape_of((members, depth, HEAD_DIM), BF16),
        ],
        cost_estimate=pl.CostEstimate(flops=1 << 20, bytes_accessed=2 << 20, transcendentals=0),
    )(*([w_query] * heads), key_matrix, value_matrix)


def packet_kernel(rep_size, info, weights, router, routes, priority, documents, moe_gain, query_gain, key_gain, attn_gain, out):
    own = info[2]
    eye = lax.broadcasted_iota(jnp.int32, (LANES, LANES), 0) == lax.broadcasted_iota(
        jnp.int32, (LANES, LANES), 1
    )
    rows = [dot_tn(routes[...].astype(BF16), eye.astype(BF16)), priority[...].astype(F32)]
    rows.append(documents[...].astype(F32))
    for ref, at in ((moe_gain, 0), (query_gain, own), (key_gain, own), (attn_gain, 0)):
        size = ref.shape[1]
        lane = lax.broadcasted_iota(jnp.int32, (size, LANES), 1)
        value = lax.broadcasted_iota(jnp.int32, (size, LANES), 0)
        rows.append(dot(ref[...], (lane == at * size + value).astype(BF16)))
    packet = jnp.concatenate(rows + [jnp.zeros((PACKET_ROWS - 14, LANES), F32)], axis=0).astype(BF16)
    depth, count = weights.shape[1], out.shape[0]
    line = count // weights.shape[0]
    for index in range(count):
        member = index // (line * rep_size) * rep_size + index % rep_size
        out[index, :depth] = weights[member]
        out[index, depth : depth + PACKET_ROWS] = packet
        out[index, depth + PACKET_ROWS :] = router[...]


def gain_row(packet, depth, out):
    for index in range(packet.shape[0]):
        row = packet[index, depth + ATTN_GAIN_ROW : depth + ATTN_GAIN_ROW + 1, :depth]
        out[:, index * depth : (index + 1) * depth] = row.astype(F32)


def normalize_kernel(depth, info, packet, *refs):
    *refs, out, gain = refs
    gain_row(packet, depth, gain)

    def write(row, ref):
        values = ref[...].astype(F32)
        scale = lax.rsqrt(jnp.mean(values * values, axis=-1, keepdims=True) + EPS)
        out[pl.ds(row, ref.shape[0]), :] = (values * scale * gain[...]).astype(BF16)

    place_plane(refs, info[1], write)


def place_weights(refs, info, count, out, groups):
    rows = out.shape[0] // (groups * count)

    def write(index, ref):
        for group in range(groups):
            start = pl.multiple_of((group * count + index) * rows, rows)
            out[pl.ds(start, rows), :] = ref[pl.ds(group * rows, rows), :]

    place_line(refs, info[0], count, write)


def turn(values, cosine, sine):
    return values * cosine + pltpu.roll(values, HEAD_DIM // 2, 1) * sine


def key_value_kernel(info, units, packet, cosine, sine, key_proj, out, weights, gain, query_gain):
    depth = units.shape[1] // packet.shape[0]
    total = jnp.zeros(gain.shape, F32)
    query_total = jnp.zeros(gain.shape, F32)
    for index in range(packet.shape[0]):
        weights[index * depth : (index + 1) * depth] = packet[index, :depth]
        row = depth + KEY_GAIN_ROW
        total = total + packet[index, row : row + 1, :].astype(F32)
        row = depth + QUERY_GAIN_ROW
        query_total = query_total + packet[index, row : row + 1, :].astype(F32)
    gain[...] = total
    query_gain[...] = query_total
    projected = dot(units[...], weights[...])
    key_proj[...] = projected
    scale = lax.rsqrt(jnp.mean(projected * projected, axis=-1, keepdims=True) + EPS)
    keys = projected * scale * total
    groups, rows, _ = out.shape
    for group in range(groups):
        part = slice(group * rows, (group + 1) * rows)
        turned = turn(keys[part], cosine[...], sine[...])
        out[group] = jnp.where(info[3] == 0, turned, projected[part]).astype(BF16)


def query_kernel(count, groups, info, units, *refs):
    *sources, weights, out = refs
    place_weights(sources, info, count, weights, groups)
    out[...] = dot(units[...], weights[...])


def attention_setup(info, sources, qdoc_ref, kdoc_ref, qpos_ref, bias, keys, values):
    key_pos = lax.broadcasted_iota(jnp.int32, bias.shape, 1)
    allowed = (qdoc_ref[0] == kdoc_ref[0]) & (key_pos <= qpos_ref[...])
    bias[...] = jnp.where(allowed, 0.0, BIG_NEG)
    rows, count = bias.shape[0], len(sources) // 2
    for step in range(count):
        part = pl.ds(pl.multiple_of(info[4 + step] * rows, rows), rows)
        mine, other = sources[step][0], sources[count + step][0]
        keys[part, :] = jnp.where(info[3] == 0, mine, other)
        values[part, :] = jnp.where(info[3] == 0, other, mine)


def rotated(projected, gain, cosine, sine):
    scale = lax.rsqrt(jnp.mean(projected * projected, axis=-1, keepdims=True) + EPS)
    unit = projected * scale
    return scale, unit, turn(unit * gain, cosine, sine)


def windows_of(length, rows):
    count = length // rows
    return [max(count * part // 4, 1) * rows for part in (1, 2, 3, 4)]


def in_window(info, qdoc_ref, kdoc_ref, rows, work):
    length = kdoc_ref.shape[2]
    earlier = jnp.sum((kdoc_ref[0] < qdoc_ref[0, 0:1, 0:1]).astype(jnp.int32))
    blocks = info[0] + 1 - lax.div(earlier, rows)
    smaller = 0
    for size in windows_of(length, rows):
        start = pl.multiple_of(jnp.maximum(info[0] + 1 - size // rows, 0) * rows, rows)
        fits = (blocks > smaller) & (blocks <= size // rows)
        pl.when(fits)(functools.partial(work, start, size))
        smaller = size // rows


def head_columns(head):
    return slice(head * HEAD_DIM, (head + 1) * HEAD_DIM)


def forward_kernel(info, q_ref, qdoc_ref, kdoc_ref, qpos_ref, cos_ref, sin_ref, gain_ref, *refs):
    *sources, out_ref, total_ref, bias, keys, values = refs
    attention_setup(info, sources, qdoc_ref, kdoc_ref, qpos_ref, bias, keys, values)
    heads = q_ref.shape[1] // HEAD_DIM

    def work(start, size):
        part = pl.ds(start, size)
        for head in range(heads):
            at = head_columns(head)
            _, _, turned = rotated(q_ref[:, at], gain_ref[...], cos_ref[...], sin_ref[...])
            scores = dot_nt(turned.astype(BF16), keys[part, :]) * (SCALE * LOG2E) + bias[:, part]
            highest = jnp.max(scores, axis=-1, keepdims=True)
            exponent = jnp.exp2(scores - highest)
            total = jnp.sum(exponent, axis=-1, keepdims=True)
            probs = (exponent * (1.0 / total)).astype(BF16)
            out_ref[:, at] = dot(probs, values[part, :]).astype(BF16)
            total_ref[0, head] = highest + jnp.log2(total)

    in_window(info, qdoc_ref, kdoc_ref, bias.shape[0], work)


def backward_kernel(info, q_ref, qdoc_ref, kdoc_ref, qpos_ref, cos_ref, sin_ref, gain_ref, *refs):
    *sources, total_ref, grad_ref, dq_ref, kept_ref, sent_ref, dgain_ref, bias, key_rows, value_rows, dk_sum, dv_sum = refs
    seq = pl.program_id(0)
    attention_setup(info, sources, qdoc_ref, kdoc_ref, qpos_ref, bias, key_rows, value_rows)
    dk_sum[...] = jnp.zeros_like(dk_sum)
    dv_sum[...] = jnp.zeros_like(dv_sum)

    @pl.when(seq == 0)
    def _():
        dgain_ref[...] = jnp.zeros_like(dgain_ref)

    gain, cosine, sine = gain_ref[...], cos_ref[...], sin_ref[...]

    def work(start, size):
        part = pl.ds(start, size)
        keys, values = key_rows[part, :], value_rows[part, :]
        for head in range(q_ref.shape[1] // HEAD_DIM):
            at = head_columns(head)
            scale, unit, turned = rotated(q_ref[:, at], gain, cosine, sine)
            turned = turned.astype(BF16)
            scores = dot_nt(turned, keys) * (SCALE * LOG2E) + bias[:, part]
            probs = jnp.exp2(scores - total_ref[0, head])
            grad = grad_ref[:, at]
            grad_probs = dot_nt(grad, values)
            delta = jnp.sum(probs * grad_probs, axis=-1, keepdims=True)
            grad_scores = (probs * (grad_probs - delta)).astype(BF16)
            dv_sum[part, :] += dot_tn(probs.astype(BF16), grad)
            dk_sum[part, :] += dot_tn(grad_scores, turned)
            grad_turned = dot(grad_scores, keys) * SCALE
            grad_gained = turn(grad_turned, cosine, -sine)
            dgain_ref[...] += jnp.sum(grad_gained * unit, axis=0, keepdims=True)
            weighted = grad_gained * gain
            dq_ref[:, at] = (
                scale * (weighted - unit * jnp.mean(weighted * unit, axis=-1, keepdims=True))
            ).astype(BF16)

    in_window(info, qdoc_ref, kdoc_ref, bias.shape[0], work)
    shape = kept_ref.shape[:1] + kept_ref.shape[2:]
    dk, dv = dk_sum[...] * SCALE, dv_sum[...]
    kept_ref[:, 0] = jnp.where(info[3] == 0, dk, dv).astype(BF16).reshape(shape)
    sent_ref[:, 0] = jnp.where(info[3] == 0, dv, dk).astype(BF16).reshape(shape)


def attention_specs(rows, length, width, sources, first=0):
    specs = [
        pl.BlockSpec(memory_space=pltpu.SMEM),
        pl.BlockSpec((rows, width), lambda s: (first + s, 0)),
        pl.BlockSpec((1, rows, 1), lambda s: (first + s, 0, 0)),
        pl.BlockSpec((1, 1, length), lambda s: (first + s, 0, 0)),
        pl.BlockSpec((rows, 1), lambda s: (0, 0)),
        pl.BlockSpec((rows, HEAD_DIM), lambda s: (0, 0)),
        pl.BlockSpec((rows, HEAD_DIM), lambda s: (0, 0)),
        pl.BlockSpec((1, HEAD_DIM), lambda s: (0, 0)),
    ]
    return specs + [
        pl.BlockSpec((1, rows, HEAD_DIM), lambda s: (first + s, 0, 0)) for _ in sources
    ]


def attention_forward(operands, sources, sequences, heads, rows, length):
    pairs = sequences * heads * rows * length
    return pl.pallas_call(
        forward_kernel,
        grid=(sequences,),
        in_specs=attention_specs(rows, length, heads * HEAD_DIM, sources),
        out_specs=[
            pl.BlockSpec((rows, heads * HEAD_DIM), lambda s: (s, 0)),
            pl.BlockSpec((1, heads, rows, 1), lambda s: (s, 0, 0, 0)),
        ],
        out_shape=[
            shape_of((sequences * rows, heads * HEAD_DIM), BF16),
            shape_of((sequences, heads, rows, 1), F32),
        ],
        scratch_shapes=[
            pltpu.VMEM((rows, length), F32),
            pltpu.VMEM((length, HEAD_DIM), BF16),
            pltpu.VMEM((length, HEAD_DIM), BF16),
        ],
        compiler_params=pltpu.CompilerParams(vmem_limit_bytes=VMEM_LIMIT),
        cost_estimate=pl.CostEstimate(
            flops=1000, bytes_accessed=1000, transcendentals=0
        ),
    )(*operands, *sources)


def attention_backward(
    operands, sources, totals, grads, first, sequences, heads, rows, length, tokens=()
):
    pairs = sequences * heads * rows * length
    parts = length // rows
    key_value_spec = pl.BlockSpec((parts, 1, rows, HEAD_DIM), lambda s: (0, s, 0, 0))
    key_value_shape = shape_of((parts, sequences, rows, HEAD_DIM), BF16)
    count = len(operands) + len(sources) + 2

    def kernel(*refs):
        backward_kernel(*refs[:count], *refs[count + len(tokens) :])

    return pl.pallas_call(
        kernel,
        grid=(sequences,),
        in_specs=attention_specs(rows, length, heads * HEAD_DIM, sources, first)
        + [
            pl.BlockSpec((1, heads, rows, 1), lambda s: (first + s, 0, 0, 0)),
            pl.BlockSpec((rows, heads * HEAD_DIM), lambda s: (first + s, 0)),
        ]
        + [pl.BlockSpec(memory_space=pl.ANY)] * len(tokens),
        out_specs=[
            pl.BlockSpec((rows, heads * HEAD_DIM), lambda s: (s, 0)),
            key_value_spec,
            key_value_spec,
            pl.BlockSpec((1, HEAD_DIM), lambda s: (0, 0)),
        ],
        out_shape=[
            shape_of((sequences * rows, heads * HEAD_DIM), BF16),
            key_value_shape,
            key_value_shape,
            shape_of((1, HEAD_DIM), F32),
        ],
        scratch_shapes=[
            pltpu.VMEM((rows, length), F32),
            pltpu.VMEM((length, HEAD_DIM), BF16),
            pltpu.VMEM((length, HEAD_DIM), BF16),
            pltpu.VMEM((length, HEAD_DIM), F32),
            pltpu.VMEM((length, HEAD_DIM), F32),
        ],
        compiler_params=pltpu.CompilerParams(vmem_limit_bytes=VMEM_LIMIT),
        cost_estimate=pl.CostEstimate(
            flops=1000, bytes_accessed=1000, transcendentals=0
        ),
    )(*operands, *sources, totals, grads, *tokens)


def key_value_back_kernel(groups, info, key_proj, cosine, sine, gain, *refs):
    *terms, out, dgain = refs
    rows = terms[0].shape[1]
    total = jnp.zeros_like(dgain)
    for group in range(groups):
        grad = total_of([term[group] for term in terms])
        part = slice(group * rows, (group + 1) * rows)
        values_grad = grad
        grad = turn(grad, cosine[...], -sine[...])
        keys = key_proj[part]
        scale = lax.rsqrt(jnp.mean(keys * keys, axis=-1, keepdims=True) + EPS)
        unit = keys * scale
        total = total + jnp.sum(grad * unit, axis=0, keepdims=True)
        weighted = grad * gain[...]
        keys_grad = scale * (weighted - unit * jnp.mean(weighted * unit, axis=-1, keepdims=True))
        out[part, :] = jnp.where(info[3] == 0, keys_grad, values_grad).astype(BF16)
    dgain[...] = jnp.where(info[3] == 0, total, 0.0)


def out_sent_kernel(count, info, attended, *refs):
    *sources, sent, weights = refs

    def write(index, ref):
        start = pl.multiple_of(index * HEAD_DIM, HEAD_DIM)
        weights[pl.ds(start, HEAD_DIM), :] = ref[...]

    place_line(sources, info[0], count, write)
    out_parts(info, CORE, attended, weights, sent)


def out_kept_kernel(info, attended, weights, kept):
    out_parts(info, 0, attended, weights, kept)


def rows_for(info, flip, ref, rows):
    return [
        ref[pl.ds(pl.multiple_of((info[1] ^ (bits | flip)) * rows, rows), rows), :] for bits in FLIPS
    ]


def out_parts(info, flip, attended, weights, out):
    rows, width = out.shape[1:]
    left = jnp.concatenate(rows_for(info, flip, attended, rows), axis=0)
    for start in range(0, width, 512):
        part = slice(start, start + 512)
        out[:, :, part] = dot(left, weights[:, part]).astype(BF16).reshape(4, rows, 512)


def normed_grad_kernel(flip, info, query_grad, key_value_grad, query_weights, key_value_weights, units, out, sums):
    rows, width = out.shape[1:]
    left = jnp.concatenate(rows_for(info, flip, query_grad, rows), axis=0)
    other = jnp.concatenate(rows_for(info, flip, key_value_grad, rows), axis=0)
    unit = jnp.concatenate(rows_for(info, flip, units, rows), axis=0)
    for start in range(0, width, 512):
        part = slice(start, start + 512)
        grad = dot_nt(left, query_weights[part]) + dot_nt(other, key_value_weights[part])
        out[:, :, part] = grad.astype(BF16).reshape(4, rows, 512)
        sums[:, part] = jnp.sum(grad * unit[:, part].astype(F32), axis=0, keepdims=True)


def middle_kernel(info, own, across, aside, tokens, gain, middle, routed, scale_out):
    values = own[...] + across[...].astype(F32) + aside[...].astype(F32) + tokens[...].astype(F32)
    scale = lax.rsqrt(jnp.mean(values * values, axis=-1, keepdims=True) + EPS)
    middle[...] = values
    routed[...] = (values * scale * gain[...]).astype(BF16)
    scale_out[...] = scale


def gradient_spread_kernel(info, weights, *refs):
    *blocks, gathered, attended_grad = refs

    def write(row, ref):
        gathered[pl.ds(row, ref.shape[0]), :] = ref[...]

    place_plane(blocks, info[1], write)
    attended_grad[...] = dot_nt(gathered[...], weights[...]).astype(BF16)


def gates_of(token_rows, router, choices):
    logits = jnp.where(choices, dot(token_rows, router), BIG_NEG)
    exponent = jnp.where(choices, jnp.exp(logits - jnp.max(logits, axis=-1, keepdims=True)), 0.0)
    return exponent / jnp.maximum(jnp.sum(exponent, axis=-1, keepdims=True), 1e-30)


def gates_kernel(info, routed, router, picked, gates):
    gates[...] = gates_of(routed[...], router[...], picked[...][:, : gates.shape[1]] > 0.5)


def dispatch_kernel(steps, info, table, *refs):
    *blocks, out = refs
    members = out.shape[0]
    slots = table.shape[2] // members
    for at, step in enumerate(steps):
        block = block_of_step(blocks, info, steps, step)
        rows = dot_tn(table[info[4 + step]], block).astype(BF16)
        out[:, at * slots : (at + 1) * slots, :] = rows.reshape(members, slots, out.shape[2])


def dispatch_with_choices_kernel(steps, info, table, picked, *refs):
    *blocks, out = refs
    members, _, width = out.shape
    slots = table.shape[2] // members
    for at, step in enumerate(steps):
        place = table[info[4 + step]]
        part = slice(at * slots, (at + 1) * slots)
        rows = dot_tn(place, block_of_step(blocks, info, steps, step)).astype(BF16)
        choices = dot_tn(place, picked[info[4 + step]]).astype(BF16)
        model = rows.shape[1]
        out[:, part, :model] = rows.reshape(members, slots, model)
        out[:, part, model:] = choices.reshape(members, slots, width - model)


def combined(table, place, arrived, at):
    members, _, width = arrived.shape
    slots = table.shape[2] // members
    rows = arrived[:, at * slots : (at + 1) * slots, :].reshape(members * slots, width)
    return dot(table[place], rows)


def combine_kernel(first, info, table, arrived, *outs):
    for at, out in enumerate(outs):
        out[...] = combined(table, info[4 + first + at], arrived, at).astype(out.dtype)


def forward_kernel_of_parts(info, part, arrived, out):
    out[...] = (part[...].astype(F32) + arrived[...].astype(F32)).astype(BF16)


def combine_stacked_kernel(first, info, table, arrived, out):
    slots = table.shape[2] // arrived.shape[0]
    steps = arrived.shape[1] // slots
    for step in range(out.shape[0]):
        place = info[4 + step]
        if first <= step < first + steps:
            out[place] = combined(table, place, arrived, step - first).astype(BF16)
        else:
            out[place] = jnp.zeros(out.shape[1:], BF16)


def copy_kernel(info, value, out):
    out[...] = value[...]


def expert_prepare_kernel(info, arrived, down, grad_hidden):
    members, model = arrived.shape[0], down.shape[2]
    slots = grad_hidden.shape[0] // members
    rows = arrived[:, :, :model].reshape(members * slots, model)
    for start in range(0, FFE, 256):
        grad = dot_nt(rows, down[0, start : start + 256, :])
        grad_hidden[:, start : start + 256] = grad


def expert_kernel(experts, info, arrived, grad_hidden, dy_rows, router, weights, act, hidden_out, back):
    members, slots, width = arrived.shape
    rows = members * slots
    inputs = arrived[...].reshape(rows, width)
    chosen = dy_rows[:, :, width:].reshape(rows, -1)[:, :experts] > 0.5
    own = lax.broadcasted_iota(jnp.int32, (rows, experts), 1) == info[2]
    gate = jnp.sum(
        jnp.where(own, gates_of(inputs, router[...], chosen), 0.0), axis=-1, keepdims=True
    )
    grad_gate = jnp.zeros((rows, 1), F32)
    for start in range(0, FFE, 256):
        piece = slice(start, start + 256)
        lower = slice(FFE + start, FFE + start + 256)
        gate_in = dot(inputs, weights[0, :, piece])
        up_in = dot(inputs, weights[0, :, lower])
        grad_in = grad_hidden[:, piece]
        sigmoid = 1.0 / (1.0 + jnp.exp(-gate_in))
        silu = gate_in * sigmoid
        hidden = silu * up_in
        grad_gate = grad_gate + jnp.sum(hidden * grad_in, axis=-1, keepdims=True)
        scaled = grad_in * gate
        act[:, piece] = (scaled * up_in * (sigmoid + silu * (1.0 - sigmoid))).astype(BF16)
        act[:, lower] = (scaled * silu).astype(BF16)
        hidden_out[:, piece] = (hidden * gate).astype(BF16)
    for start in range(0, width, 512):
        piece = slice(start, start + 512)
        grad = dot_nt(act[...], weights[0, piece, :]).astype(BF16)
        back[:, :, piece] = grad.reshape(members, slots, 512)
    extra = back.shape[2] - width
    high = grad_gate.astype(BF16).astype(F32)
    lane = lax.broadcasted_iota(jnp.int32, (rows, extra), 1)
    columns = jnp.where(lane == info[2], high, 0.0)
    columns = columns + jnp.where(lane == info[2] + experts, grad_gate - high, 0.0)
    back[:, :, width:] = columns.astype(BF16).reshape(members, slots, extra)


def results_kernel(info, down, hidden, out):
    members, slots, width = out.shape
    for start in range(0, width, 512):
        piece = slice(start, start + 512)
        rows = dot(hidden[...], down[0, :, piece]).astype(BF16)
        out[:, :, piece] = rows.reshape(members, slots, 512)


def gate_up_grad(rows, acts, tokens):
    count, groups = rows[0].shape[0], len(rows)
    width, columns = rows[0].shape[1], acts[0].shape[1]
    tile = 512

    def kernel(*refs):
        out = refs[-1]
        total = dot_tn(refs[0][...], refs[groups][...])
        for group in range(1, groups):
            total = total + dot_tn(refs[group][...], refs[groups + group][...])
        out[0] = total

    return pl.pallas_call(
        kernel,
        grid=(width // tile,),
        in_specs=[pl.BlockSpec((count, tile), lambda i: (0, i))] * groups
        + [pl.BlockSpec((count, columns), lambda i: (0, 0))] * groups
        + [pl.BlockSpec(memory_space=pl.ANY)] * len(tokens),
        out_specs=pl.BlockSpec((1, tile, columns), lambda i: (0, i, 0)),
        out_shape=shape_of((1, width, columns), F32),
        compiler_params=pltpu.CompilerParams(vmem_limit_bytes=VMEM_LIMIT),
        cost_estimate=pl.CostEstimate(
            flops=1000, bytes_accessed=1000, transcendentals=0
        ),
    )(*rows, *acts, *tokens)


def down_grad(hiddens, arrived, model, tokens):
    groups, tile = len(hiddens), 256
    count = hiddens[0].shape[0]

    def kernel(*refs):
        total = 0.0
        for left, right in zip(refs[:groups], refs[groups : 2 * groups]):
            total = total + dot_tn(left[...], right[:, :, :model].reshape(count, model))
        refs[-1][0] = total

    return pl.pallas_call(
        kernel,
        grid=(FFE // tile,),
        in_specs=[pl.BlockSpec((count, tile), lambda i: (0, i))] * groups
        + [pl.BlockSpec(arrived[0].shape, lambda i: (0, 0, 0))] * groups
        + [pl.BlockSpec(memory_space=pl.ANY)] * len(tokens),
        out_specs=pl.BlockSpec((1, tile, model), lambda i: (0, i, 0)),
        out_shape=shape_of((1, FFE, model), F32),
        compiler_params=pltpu.CompilerParams(vmem_limit_bytes=VMEM_LIMIT),
        cost_estimate=pl.CostEstimate(flops=1000, bytes_accessed=1000, transcendentals=0),
    )(*hiddens, *arrived, *tokens)


def token_back_kernel(info, gates, router, middle, scale, gain, cotangent, routed, *refs):
    *terms, grad_middle, grad_branch, grad_gain, grad_router = refs
    width = middle.shape[1]
    experts = gates.shape[1]
    total = total_of([term[...] for term in terms])
    extra = total[:, width:]
    grad_gates = extra[:, :experts] + extra[:, experts : 2 * experts]
    values = gates[...]
    grad_logits = values * (grad_gates - jnp.sum(values * grad_gates, axis=-1, keepdims=True))
    grad_logits = grad_logits.astype(BF16)
    grad_routed = total[:, :width] + dot_nt(grad_logits, router[...])
    unit = middle[...] * scale[...]
    grad_gain[...] = jnp.sum(grad_routed * unit, axis=0, keepdims=True)
    weighted = grad_routed * gain[...]
    grad = cotangent[...].astype(F32) + scale[...] * (
        weighted - unit * jnp.mean(weighted * unit, axis=-1, keepdims=True)
    )
    grad_middle[...] = grad
    grad_branch[...] = grad.astype(BF16)
    grad_router[...] = dot_tn(routed[...], grad_logits)


def input_grad_kernel(info, own, across, aside, tokens, gain, grad_middle, out):
    weighted = (own[...] + across[...].astype(F32) + aside[...].astype(F32)) * gain[...]
    values = tokens[...].astype(F32)
    scale = lax.rsqrt(jnp.mean(values * values, axis=-1, keepdims=True) + EPS)
    unit = values * scale
    out[...] = grad_middle[...] + scale * (
        weighted - unit * jnp.mean(weighted * unit, axis=-1, keepdims=True)
    )


def mixed_kernel(info, middle, *refs):
    *terms, out = refs
    out[...] = (middle[...] + total_of([term[...] for term in terms])).astype(BF16)


def unpack_weights_kernel(rep_size, info, arrived, queries, keys, values):
    members, _, columns = arrived.shape
    heads = columns // HEAD_DIM - 1
    for member in range(members):
        group, rep = member // rep_size, member % rep_size
        for j in range(heads):
            head = group * heads * rep_size + j * rep_size + rep
            queries[:, head * HEAD_DIM : (head + 1) * HEAD_DIM] = arrived[
                member, :, j * HEAD_DIM : (j + 1) * HEAD_DIM
            ].astype(F32)
        out = values if rep else keys
        out[:, group * HEAD_DIM : (group + 1) * HEAD_DIM] = arrived[
            member, :, heads * HEAD_DIM :
        ].astype(F32)


def body(
    tokens,
    segments,
    routes,
    priority,
    w_query,
    key_matrix,
    value_matrix,
    w_out,
    w_router,
    attn_gain,
    moe_gain,
    query_gain,
    key_norm_weight,
    w_gate_up,
    w_down,
    cotangent,
):
    own_rows, width = tokens.shape[1], tokens.shape[2]
    length = segments.shape[1]
    dp_size, seq_size, rep_size = (lax.axis_size(name) for name in ALL)
    devices = dp_size * seq_size * rep_size
    members = dp_size * rep_size
    dp_at, seq_at, rep_at = (lax.axis_index(name) for name in ALL)
    experts = devices * w_gate_up.shape[0]
    capacity = own_rows * TOPK // experts
    plane_slots = members * capacity
    depth = w_router.shape[0]
    heads = QUERY_HEADS // members
    head_width = heads * HEAD_DIM
    rows = rep_size * own_rows
    plane_rows = members * own_rows
    chunk = members * depth
    extra = -(-2 * experts // LANES) * LANES
    entry = jnp.arange(4 + seq_size, dtype=jnp.int32)
    info = (entry - 4) ^ seq_at if seq_size == 4 else entry - 4
    places = (seq_at, lax.axis_index(PLANE), lax.axis_index(ALL), rep_at)
    for index, place in enumerate(places):
        info = jnp.where(entry == index, place, info)
    own_tokens, own_cotangent = tokens[0], cotangent[0]

    token_blocks = plane_gather(own_tokens)
    query_part, key_value_part = pack_weights(
        w_query, key_matrix, value_matrix, members, rep_size, heads
    )
    cotangent_sources = [lax.all_gather(own_cotangent, "seq")]
    query_part = swap(after(query_part, token_blocks[1], token_blocks[4]), PLANE)
    router_rows = w_router.size // LANES
    own_documents = lax.dynamic_slice_in_dim(segments, (seq_at * rep_size + rep_at) * own_rows, own_rows, 1)
    packet = run(
        functools.partial(packet_kernel, rep_size),
        [shape_of((devices, depth + PACKET_ROWS + router_rows, LANES), BF16)],
        info,
        key_value_part,
        w_router.reshape(router_rows, LANES),
        routes[0],
        priority,
        own_documents,
        moe_gain[None],
        query_gain[None],
        key_norm_weight[None],
        attn_gain[None],
        tokens=(query_part, *token_blocks[5:7]),
    )[0]
    packet = swap(packet, ALL)
    arrival = packet
    router = packet[:, depth + PACKET_ROWS :].reshape(devices, depth, experts)
    router = router.reshape(width, experts)
    packet = packet[:, depth : depth + PACKET_ROWS]
    query_part = after(query_part.reshape(chunk, head_width), arrival, cotangent_sources[0])
    query_sources = [lax.all_gather(query_part, "seq")]

    packet = packet.astype(F32)
    documents = packet[:, DOCUMENT_ROW].reshape(dp_size, length).astype(jnp.int32)
    second_gain = packet[:, MOE_GAIN_ROW, :depth].reshape(1, width)
    meta = packet.reshape(dp_size, seq_size, rep_size, PACKET_ROWS, LANES)
    meta = pick(pick(meta, dp_at), rep_at, 1).astype(jnp.int32)
    choice_ids, priority_rank = meta[:, :TOPK], meta[:, PRIORITY_ROW]
    expert_lanes = -(-experts // LANES) * LANES
    expert_ids = jnp.arange(expert_lanes, dtype=jnp.int32)
    picked = jnp.any(choice_ids[:, :, :, None] == expert_ids, axis=1)
    earlier = (priority_rank[:, None, :] < priority_rank[:, :, None]).astype(BF16)
    plane_picked = pick(
        picked[:, :, :experts].reshape(seq_size, own_rows, dp_size, seq_size, rep_size), seq_at, 3
    ).reshape(seq_size, own_rows, members)
    slot_index = jnp.einsum(
        "bts,bse->bte", earlier, plane_picked.astype(BF16), preferred_element_type=F32
    ).astype(jnp.int32)
    slot_ids = jnp.arange(capacity, dtype=jnp.int32)
    table = plane_picked[..., None] & (slot_index[..., None] == slot_ids)
    table = table.reshape(seq_size, own_rows, plane_slots).astype(BF16)
    picked = picked.astype(BF16)

    units, first_gain = run(
        functools.partial(normalize_kernel, depth),
        [shape_of((plane_rows, width), BF16), shape_of((1, width), F32)],
        info,
        arrival,
        *token_blocks,
    )
    positions = seq_at * rows + jnp.arange(rows, dtype=jnp.int32)
    frequency = THETA ** (-2.0 * jnp.arange(HEAD_DIM // 2, dtype=F32) / HEAD_DIM)
    angles = positions.astype(F32)[:, None] * jnp.concatenate([frequency, frequency])[None, :]
    sign = jnp.where(jnp.arange(HEAD_DIM) < HEAD_DIM // 2, -1.0, 1.0)
    cosine, sine = jnp.cos(angles), jnp.sin(angles) * sign[None, :]
    key_proj, key_value_rows, key_value_weights, key_norm_gain, query_norm_gain = run(
        key_value_kernel,
        [
            shape_of((plane_rows, HEAD_DIM), F32),
            shape_of((dp_size, rows, HEAD_DIM), BF16),
            shape_of((width, HEAD_DIM), BF16),
            shape_of((1, HEAD_DIM), F32),
            shape_of((1, HEAD_DIM), F32),
        ],
        info,
        units,
        arrival,
        cosine,
        sine,
        flops=2 * plane_rows * width * HEAD_DIM,
    )
    mine = line_steps(line_gather(key_value_rows, seq_size))
    other = [plane_move(block, SIDE) for block in mine[:-1]]
    query_weights, query_proj = run(
        functools.partial(query_kernel, seq_size, dp_size),
        [shape_of((width, head_width), BF16), shape_of((plane_rows, head_width), F32)],
        info,
        units,
        *query_sources,
        flops=2 * plane_rows * width * head_width,
    )
    key_values = mine + other + [plane_move(mine[-1], SIDE)]

    whole_heads = w_out.shape[0] == HEAD_DIM
    if whole_heads:
        held_w_out = run(
            copy_kernel, [shape_of(w_out.shape, BF16)], info, w_out, tokens=mine[-1:]
        )[0]
        out_sources = [lax.all_gather(held_w_out, "seq")]
    else:
        group = lax.all_gather(w_out, ("seq", "rep"), axis=0, tiled=True)
        group = group.reshape(heads, rep_size, HEAD_DIM, width)
        out_sources = [pick(group, rep_at, 1)]

    steps = list(range(seq_size))
    groups = [steps[: seq_size // 2], steps[seq_size // 2 :]]
    group_slots = len(groups[0]) * capacity
    group_rows = members * group_slots
    group_rows = members * group_slots
    def send_cotangent(group, held, *late):
        outgoing = run(
            functools.partial(dispatch_with_choices_kernel, group),
            [shape_of((members, group_slots, width + expert_lanes), BF16)],
            info,
            table,
            picked,
            *cotangent_sources,
            tokens=held,
            flops=2 * own_rows * len(group) * plane_slots * width,
        )[0]
        return swap(after(outgoing, *late) if late else outgoing, PLANE)

    dy_rows = [send_cotangent(groups[0], (key_value_rows,))]
    dy_rows.append(
        send_cotangent(groups[1], mine[2:3], dy_rows[0], query_proj, *key_values[seq_size:])
    )
    grad_hidden = [
        run(
            expert_prepare_kernel,
            [shape_of((group_rows, FFE), F32)],
            info,
            rows_,
            w_down,
            filler=True,
        )[0]
        for rows_ in dy_rows
    ]

    query_doc = lax.dynamic_slice_in_dim(documents, seq_at * rows, rows, axis=1)
    operands = (
        info,
        query_proj,
        query_doc[:, :, None],
        documents[:, None, :],
        positions[:, None],
        cosine,
        sine,
        query_norm_gain,
    )
    attended, totals = attention_forward(operands, key_values, dp_size, heads, rows, length)
    parts_shape = shape_of((4, own_rows, width), BF16)
    part_flops = 8 * own_rows * head_width * width
    sent, out_weights = run(
        functools.partial(out_sent_kernel, heads),
        [parts_shape, shape_of((head_width, width), BF16)],
        info,
        attended,
        *out_sources,
        tokens=(dy_rows[1],),
        flops=part_flops,
    )
    kept = run(out_kept_kernel, [parts_shape], info, attended, out_weights, flops=part_flops)[0]
    row_f32, row_bf16 = shape_of((own_rows, width), F32), shape_of((own_rows, width), BF16)
    *plane_terms, _ = plane_reduce(info, sent, kept)
    middle, routed, scale_second = run(
        middle_kernel,
        [row_f32, row_bf16, shape_of((own_rows, 1), F32)],
        info,
        *plane_terms,
        own_tokens,
        second_gain,
    )

    if seq_size == 4:
        half_rows = own_rows // 2
        second = [line_move(routed[:half_rows], 2), line_move(routed[half_rows:], 2)]
        routed_far = second + [line_move(piece, 1) for piece in second]
        routed_near = [routed, line_move(routed, 1)]
        token = second[:1]
    else:
        routed_near = routed_far = line_gather(routed, seq_size)
        token = ()
    own_picked = pick(picked, seq_at)
    gates = run(
        gates_kernel, [shape_of((own_rows, experts), F32)], info, routed, router, own_picked
    )[0]
    arrived = []
    for group, routed_sources in zip(groups, (routed_near, routed_far)):
        outgoing = run(
            functools.partial(dispatch_kernel, group),
            [shape_of((members, group_slots, width), BF16)],
            info,
            table,
            *routed_sources,
            tokens=token,
            flops=2 * own_rows * len(group) * plane_slots * width,
        )[0]
        arrived.append(swap(outgoing, PLANE))
        token = arrived[-1:]
    worked, token = {}, ()
    for at in (1, 0):
        worked[at] = run(
            functools.partial(expert_kernel, experts),
            [
                shape_of((group_rows, 2 * FFE), BF16),
                shape_of((group_rows, FFE), BF16),
                shape_of((members, group_slots, width + extra), BF16),
            ],
            info,
            arrived[at],
            grad_hidden[at],
            dy_rows[at],
            router,
            w_gate_up,
            tokens=token,
            flops=8 * group_rows * width * FFE,
        )
        token = (worked[at][2],)
    acts, hiddens, backs = zip(worked[0], worked[1])

    def combine(at, rows_, columns, held=()):
        group = groups[at]
        return run(
            functools.partial(combine_kernel, group[0]),
            [shape_of((own_rows, columns), BF16)] * len(group),
            info,
            table,
            rows_,
            tokens=held,
            flops=2 * own_rows * len(group) * plane_slots * columns,
        )

    def send_groups(near, far):
        if seq_size != 4:
            return line_reduce(jnp.stack(list(near) + list(far)), seq_at, seq_size)
        return [near[0], line_move(far[0], 2), line_move(near[1], 1)]

    pairs_far, pairs_near = swap(backs[1], PLANE), swap(backs[0], PLANE)
    far_parts = combine(1, pairs_far, width + extra)
    grad_down = down_grad(hiddens, dy_rows, width, far_parts[:1])
    if seq_size == 4:
        far_parts = run(
            forward_kernel_of_parts,
            [shape_of((own_rows, width + extra), BF16)],
            info,
            far_parts[0],
            line_move(far_parts[1], 1),
            tokens=(grad_down,),
        )
    results = [
        run(
            results_kernel,
            [shape_of((members, group_slots, width), BF16)],
            info,
            w_down,
            hidden,
            tokens=far_parts[:1],
            filler=True,
        )[0]
        for hidden in hiddens
    ]
    near_parts = combine(0, pairs_near, width + extra, far_parts[:1])
    pair_terms = send_groups(near_parts, far_parts)
    grad_gate_up = gate_up_grad(
        [rows_.reshape(group_rows, width) for rows_ in arrived], acts, near_parts[:1]
    )
    results_far = swap(results[1], PLANE)
    grad_middle, grad_branch, grad_moe_gain, grad_router = run(
        token_back_kernel,
        [row_f32, row_bf16, shape_of((1, width), F32), shape_of((width, experts), F32)],
        info,
        gates,
        router,
        middle,
        scale_second,
        second_gain,
        own_cotangent,
        routed,
        *pair_terms,
        tokens=(grad_gate_up, results_far, grad_down, results[0]),
    )
    branch_blocks = plane_gather(grad_branch)
    far_stacked = run(
        functools.partial(combine_stacked_kernel, groups[1][0]),
        [shape_of((seq_size, own_rows, width), BF16)],
        info,
        table,
        results_far,
        tokens=(grad_middle,),
        flops=2 * own_rows * len(groups[1]) * plane_slots * width,
    )[0]
    grad_branch, grad_attended = run(
        gradient_spread_kernel,
        [shape_of((plane_rows, width), BF16), shape_of((plane_rows, head_width), BF16)],
        info,
        out_weights,
        *branch_blocks,
        tokens=(far_stacked,),
        flops=2 * plane_rows * head_width * width,
    )
    far_sum = lax.psum_scatter(far_stacked, "seq", scatter_dimension=0, tiled=False)
    results_near = swap(after(results[0], grad_attended), PLANE)
    half = dp_size // 2
    first_call = attention_backward(
        operands, key_values, totals, grad_attended, 0, half, heads, rows, length
    )
    grad_out = dot_tn(after(attended, first_call[0]), grad_branch).astype(BF16)
    second_call = attention_backward(
        operands,
        key_values,
        totals,
        grad_attended,
        half,
        half,
        heads,
        rows,
        length,
        (grad_out,),
    )
    query_grads, kept_grads, sent_grads, gain_grads = zip(first_call, second_call)
    if whole_heads:
        grad_out = grad_out.reshape(heads, HEAD_DIM, width)
        grad_out = lax.psum_scatter(grad_out, "seq", scatter_dimension=0, tiled=False)
    else:
        group = jnp.zeros((heads, rep_size, HEAD_DIM, width), F32)
        group = lax.dynamic_update_index_in_dim(
            group, grad_out.reshape(heads, HEAD_DIM, width).astype(F32), rep_at, 1
        )
        grad_out = lax.psum_scatter(
            group.reshape(heads * rep_size * HEAD_DIM, width),
            ("seq", "rep"),
            scatter_dimension=0,
            tiled=True,
        )
    if seq_size == 4:
        near_terms = near_parts = combine(0, results_near, width, second_call[:1])
        near_terms = [near_terms[0], line_move(near_terms[1], 1)]
    else:
        near_terms = [
            lax.psum_scatter(
                run(
                    functools.partial(combine_stacked_kernel, 0),
                    [shape_of((seq_size, own_rows, width), BF16)],
                    info,
                    table,
                    results_near,
                )[0],
                "seq",
                scatter_dimension=0,
                tiled=False,
            )
        ]
    result_terms = near_terms + [far_sum.reshape(own_rows, width)]
    grad_query_proj = jnp.concatenate(query_grads)
    grad_query_gain = gain_grads[0] + gain_grads[1]
    kept_grads = [
        kept.astype(F32) + plane_move(sent, SIDE).astype(F32)
        for kept, sent in zip(kept_grads, (sent_grads[0], after(sent_grads[1], results_near, far_sum)))
    ]
    grad_key_value = jnp.concatenate(kept_grads, axis=1).astype(BF16)
    key_value_terms = line_reduce(grad_key_value, seq_at, seq_size)
    grad_key_value, grad_key_gain = run(
        functools.partial(key_value_back_kernel, dp_size),
        [shape_of((plane_rows, HEAD_DIM), BF16), shape_of((1, HEAD_DIM), F32)],
        info,
        key_proj,
        cosine,
        sine,
        key_norm_gain,
        *key_value_terms,
        tokens=near_parts[:1],
    )

    def weight_parts(left, grad):
        parts = dot_tn(left, grad).astype(BF16)
        parts = parts.reshape(dp_size, seq_size, rep_size * depth, grad.shape[1])
        return parts.transpose(1, 0, 2, 3)

    query_parts = weight_parts(units, grad_query_proj)

    def normed_grad(flip, held=()):
        return run(
            functools.partial(normed_grad_kernel, flip),
            [parts_shape, shape_of((1, width), F32)],
            info,
            grad_query_proj,
            grad_key_value,
            query_weights,
            key_value_weights,
            units,
            tokens=held,
            flops=8 * own_rows * (head_width + HEAD_DIM) * width,
        )

    sent, sent_sums = normed_grad(CORE, (grad_out,))
    kept, kept_sums = normed_grad(0)
    weights_total = lax.psum_scatter(
        jnp.concatenate([query_parts, weight_parts(units, grad_key_value)], axis=-1),
        "seq",
        scatter_dimension=0,
        tiled=False,
    ).reshape(members, depth, head_width + HEAD_DIM)
    *plane_terms, mark = plane_reduce(info, sent, kept)

    pieces = (grad_router, sent_sums + kept_sums, grad_moe_gain, grad_query_gain, grad_key_gain)
    small = jnp.concatenate([piece.reshape(devices, -1) for piece in pieces], axis=-1)
    small = jnp.sum(swap(small, ALL), axis=0)
    bounds = [0]
    for piece in pieces:
        bounds.append(bounds[-1] + piece.size // devices)
    small = [small[a:b] for a, b in zip(bounds[:-1], bounds[1:])]
    weights_arrived = swap(weights_total, PLANE)
    grad_query, grad_key, grad_value = run(
        functools.partial(unpack_weights_kernel, rep_size),
        [shape_of(w_query.shape, F32)] + [shape_of(key_matrix.shape, F32)] * 2,
        info,
        weights_arrived,
    )
    mixed = run(
        mixed_kernel, [row_bf16], info, middle, *result_terms, tokens=plane_terms[1:]
    )[0]
    input_grad = run(
        input_grad_kernel,
        [row_f32],
        info,
        *plane_terms,
        own_tokens,
        first_gain,
        grad_middle,
    )[0]

    return (
        mixed[None],
        input_grad[None],
        grad_query,
        grad_key,
        grad_value,
        grad_out.astype(F32),
        small[0].reshape(depth, experts),
        small[1] / attn_gain.astype(F32),
        small[2],
        small[3],
        small[4],
        grad_gate_up,
        grad_down,
    )


def solution(mesh):
    tokens_spec = P("dp", ("seq", "rep"), None)
    rows_spec = P(ALL, None)
    vector_spec = P(ALL)
    expert_spec = P(ALL, None, None)
    return jax.shard_map(
        body,
        mesh=mesh,
        in_specs=(
            (tokens_spec, P("dp", None), tokens_spec, P("dp", ("seq", "rep")))
            + (rows_spec,) * 5
            + (vector_spec,) * 4
            + (expert_spec, expert_spec, tokens_spec)
        ),
        out_specs=(
            (tokens_spec, tokens_spec)
            + (rows_spec,) * 5
            + (vector_spec,) * 4
            + (expert_spec, expert_spec)
        ),
        check_vma=False,
    )
```

```python
import functools

import jax
import jax.numpy as jnp
from jax import lax
from jax.experimental import pallas as pl
from jax.experimental.pallas import tpu as pltpu
from jax.sharding import PartitionSpec as P

QUERY_HEADS = 32
KEY_VALUE_HEADS = 4
HEAD_DIM = 128
FFE = 768
TOPK = 8

EPS = 1e-06
THETA = 1000000.0
BIG_NEG = -1e30
LOG2E = 1.4426950408889634
ALL = ("dp", "seq", "rep")
PLANE = ("dp", "rep")
F32 = jnp.float32
BF16 = jnp.bfloat16
VMEM_LIMIT = 56 * 1024 * 1024
SCALE = HEAD_DIM ** (-0.5)
SIDE, CORE, CROSS = 1, 2, 4
FLIPS = (CROSS | SIDE, CROSS, SIDE, 0)
LANES = 128
PRIORITY_ROW, DOCUMENT_ROW, MOE_GAIN_ROW, QUERY_GAIN_ROW, KEY_GAIN_ROW, ATTN_GAIN_ROW, PACKET_ROWS = 8, 9, 10, 11, 12, 13, 16


def dot(a, b):
    return jnp.dot(a, b, preferred_element_type=F32)


def dot_nt(a, b):
    return lax.dot_general(a, b, (((1,), (1,)), ((), ())), preferred_element_type=F32)


def dot_tn(a, b):
    return lax.dot_general(a, b, (((0,), (0,)), ((), ())), preferred_element_type=F32)


def after(value, *earlier):
    return pl.pallas_call(
        lambda *refs: None,
        in_specs=[pl.BlockSpec(memory_space=pl.ANY)] * (1 + len(earlier)),
        out_specs=pl.BlockSpec(memory_space=pl.ANY),
        out_shape=jax.ShapeDtypeStruct(value.shape, value.dtype),
        input_output_aliases={0: 0},
        cost_estimate=pl.CostEstimate(flops=1000, bytes_accessed=1000, transcendentals=0),
    )(value, *earlier)


def swap(blocks, axes):
    return lax.all_to_all(blocks, axes, split_axis=0, concat_axis=0, tiled=True)


def spread(shard, axes, count):
    return swap(jnp.broadcast_to(shard[None], (count,) + shard.shape), axes)


def shape_of(shape, dtype):
    return jax.ShapeDtypeStruct(shape, dtype)


def run(kernel, outs, *operands, tokens=(), flops=0, filler=False):
    in_specs = [pl.BlockSpec(memory_space=pltpu.SMEM)]
    in_specs += [pl.BlockSpec(memory_space=pltpu.VMEM)] * (len(operands) - 1)
    in_specs += [pl.BlockSpec(memory_space=pl.ANY)] * len(tokens)
    touched = sum(o.size * o.dtype.itemsize for o in operands[1:])
    touched += sum(o.size * o.dtype.itemsize for o in outs)
    if filler:
        flops, touched = 1000, 1000

    def body(*refs):
        kernel(*refs[: len(operands)], *refs[len(operands) + len(tokens) :])

    return pl.pallas_call(
        body,
        in_specs=in_specs,
        out_specs=[pl.BlockSpec(memory_space=pltpu.VMEM)] * len(outs),
        out_shape=outs,
        compiler_params=pltpu.CompilerParams(vmem_limit_bytes=VMEM_LIMIT),
        cost_estimate=pl.CostEstimate(
            flops=int(flops), bytes_accessed=int(touched), transcendentals=0
        ),
    )(*operands, *tokens)


def plane_move(block, bits):
    return lax.ppermute(block, PLANE, [(index, index ^ bits) for index in range(8)])


def plane_gather(block):
    half = block.shape[0] // 2
    across, aside, core = (plane_move(block, bits) for bits in (CROSS, SIDE, CORE))
    far = [plane_move(across[:half], SIDE), plane_move(aside[half:], CROSS)]
    across_core, aside_core = plane_move(across, CORE), plane_move(aside, CORE)
    far_core = [plane_move(piece, CORE) for piece in far]
    return [block, aside, core, aside_core, across] + far + [across_core] + far_core


def place_plane(refs, member, write):
    rows = refs[0].shape[0]
    offsets = [(0, 0), (1, 0), (2, 0), (3, 0), (4, 0), (5, 0), (5, rows // 2), (6, 0), (7, 0), (7, rows // 2)]
    for ref, (bits, start) in zip(refs, offsets):
        write(pl.multiple_of((member ^ bits) * rows + start, rows // 2), ref)


def first_sums(_, arrived, kept, far_low, far_high, across, aside, own):
    half = far_low.shape[0]
    sums = [arrived[i].astype(F32) + kept[i].astype(F32) for i in range(4)]
    far_low[...] = sums[0][:half].astype(BF16)
    far_high[...] = sums[0][half:].astype(BF16)
    across[...] = sums[1].astype(BF16)
    aside[...] = sums[2].astype(BF16)
    own[...] = sums[3]


def second_sums(_, across, aside, from_across, from_aside, across_out, aside_out):
    half = from_across.shape[0]
    across_out[:half] = across[:half]
    across_out[half:] = (across[half:].astype(F32) + from_aside[...].astype(F32)).astype(BF16)
    aside_out[:half] = (aside[:half].astype(F32) + from_across[...].astype(F32)).astype(BF16)
    aside_out[half:] = aside[half:]


def plane_reduce(info, sent, kept):
    _, rows, width = sent.shape
    piece, whole = shape_of((rows // 2, width), BF16), shape_of((rows, width), BF16)
    arrived = plane_move(sent, CORE)
    far_low, far_high, across, aside, own = run(
        first_sums, [piece, piece, whole, whole, shape_of((rows, width), F32)], info, arrived, kept
    )
    from_across, from_aside = plane_move(far_low, CROSS), plane_move(far_high, SIDE)
    across, aside = run(
        second_sums, [whole, whole], info, across, aside, from_across, from_aside
    )
    return own, plane_move(across, CROSS), plane_move(aside, SIDE), across


def line_move(block, bits):
    return lax.ppermute(block, "seq", [(place, place ^ bits) for place in range(4)])


def line_gather(block, count):
    if count != 4:
        return [spread(block, "seq", count)]
    near, second = line_move(block, 1), line_move(block, 2)
    return [block, near, second, line_move(after(second, near), 1)]


def line_gather_near(block, count):
    return [block, line_move(block, 1)] if count == 4 else [block]


def place_line(refs, place, count, write):
    for at in range(count):
        if len(refs) == 1:
            write(at, refs[0].at[at])
        else:
            write(place ^ at, refs[at])


def needed(sources, steps):
    return sources if len(sources) == 1 else [sources[step] for step in steps]


def block_of_step(refs, info, steps, step):
    if len(refs) == 1:
        return refs[0][info[4 + step]]
    pieces = len(refs) // len(steps)
    at = steps.index(step) * pieces
    return jnp.concatenate([ref[...] for ref in refs[at : at + pieces]], axis=0)


def line_steps(blocks):
    if len(blocks) == 1:
        return [blocks[0][step] for step in range(blocks[0].shape[0])]
    return blocks


def line_forward(part, crossing):
    return (part.astype(F32) + line_move(crossing, 1).astype(F32)).astype(BF16)


def line_reduce(parts, place, count):
    if count != 4:
        return [jnp.sum(swap(parts, "seq").astype(F32), axis=0)]
    own, near, second, crossing = (pick(parts, place ^ bits) for bits in range(4))
    return [own, line_move(line_forward(second, crossing), 2), line_move(near, 1)]


def total_of(terms):
    return sum(term.astype(F32) for term in terms)


def pick(blocks, index, axis=0):
    return lax.dynamic_index_in_dim(blocks, index, axis, keepdims=False)


def pack_weights_kernel(*refs):
    *query_refs, key_ref, value_ref, query_out, key_value_out = refs
    for j, ref in enumerate(query_refs):
        query_out[0, :, j * HEAD_DIM : (j + 1) * HEAD_DIM] = ref[...]
    takes_keys = lax.rem(pl.program_id(0), 2) == 0
    key_value_out[0] = jnp.where(takes_keys, key_ref[...], value_ref[...])


def pack_weights(w_query, key_matrix, value_matrix, members, rep_size, heads):
    depth = w_query.shape[0]
    group = heads * rep_size

    def head_spec(j):
        return pl.BlockSpec(
            (depth, HEAD_DIM), lambda m: (0, (m // rep_size) * group + j * rep_size + m % rep_size)
        )

    group_spec = pl.BlockSpec((depth, HEAD_DIM), lambda m: (0, m // rep_size))
    return pl.pallas_call(
        pack_weights_kernel,
        grid=(members,),
        in_specs=[head_spec(j) for j in range(heads)]
        + [group_spec, group_spec],
        out_specs=[
            pl.BlockSpec((1, depth, heads * HEAD_DIM), lambda m: (m, 0, 0)),
            pl.BlockSpec((1, depth, HEAD_DIM), lambda m: (m, 0, 0)),
        ],
        out_shape=[
            shape_of((members, depth, heads * HEAD_DIM), BF16),
            shape_of((members, depth, HEAD_DIM), BF16),
        ],
        cost_estimate=pl.CostEstimate(flops=1 << 20, bytes_accessed=2 << 20, transcendentals=0),
    )(*([w_query] * heads), key_matrix, value_matrix)


def packet_kernel(rep_size, info, weights, router, routes, priority, documents, moe_gain, query_gain, key_gain, attn_gain, out):
    own = info[2]
    eye = lax.broadcasted_iota(jnp.int32, (LANES, LANES), 0) == lax.broadcasted_iota(
        jnp.int32, (LANES, LANES), 1
    )
    rows = [dot_tn(routes[...].astype(BF16), eye.astype(BF16)), priority[...].astype(F32)]
    rows.append(documents[...].astype(F32))
    for ref, at in ((moe_gain, 0), (query_gain, own), (key_gain, own), (attn_gain, 0)):
        size = ref.shape[1]
        lane = lax.broadcasted_iota(jnp.int32, (size, LANES), 1)
        value = lax.broadcasted_iota(jnp.int32, (size, LANES), 0)
        rows.append(dot(ref[...], (lane == at * size + value).astype(BF16)))
    packet = jnp.concatenate(rows + [jnp.zeros((PACKET_ROWS - 14, LANES), F32)], axis=0).astype(BF16)
    depth, count = weights.shape[1], out.shape[0]
    line = count // weights.shape[0]
    for index in range(count):
        member = index // (line * rep_size) * rep_size + index % rep_size
        out[index, :depth] = weights[member]
        out[index, depth : depth + PACKET_ROWS] = packet
        out[index, depth + PACKET_ROWS :] = router[...]


def gain_row(packet, depth, out):
    for index in range(packet.shape[0]):
        row = packet[index, depth + ATTN_GAIN_ROW : depth + ATTN_GAIN_ROW + 1, :depth]
        out[:, index * depth : (index + 1) * depth] = row.astype(F32)


def normalize_kernel(depth, info, packet, *refs):
    *refs, out, gain = refs
    gain_row(packet, depth, gain)

    def write(row, ref):
        values = ref[...].astype(F32)
        scale = lax.rsqrt(jnp.mean(values * values, axis=-1, keepdims=True) + EPS)
        out[pl.ds(row, ref.shape[0]), :] = (values * scale * gain[...]).astype(BF16)

    place_plane(refs, info[1], write)


def place_weights(refs, info, count, out, groups):
    rows = out.shape[0] // (groups * count)

    def write(index, ref):
        for group in range(groups):
            start = pl.multiple_of((group * count + index) * rows, rows)
            out[pl.ds(start, rows), :] = ref[pl.ds(group * rows, rows), :]

    place_line(refs, info[0], count, write)


def turn(values, cosine, sine):
    return values * cosine + pltpu.roll(values, HEAD_DIM // 2, 1) * sine


def key_value_kernel(info, units, packet, cosine, sine, key_proj, out, weights, gain, query_gain):
    depth = units.shape[1] // packet.shape[0]
    total = jnp.zeros(gain.shape, F32)
    query_total = jnp.zeros(gain.shape, F32)
    for index in range(packet.shape[0]):
        weights[index * depth : (index + 1) * depth] = packet[index, :depth]
        row = depth + KEY_GAIN_ROW
        total = total + packet[index, row : row + 1, :].astype(F32)
        row = depth + QUERY_GAIN_ROW
        query_total = query_total + packet[index, row : row + 1, :].astype(F32)
    gain[...] = total
    query_gain[...] = query_total
    projected = dot(units[...], weights[...])
    key_proj[...] = projected
    scale = lax.rsqrt(jnp.mean(projected * projected, axis=-1, keepdims=True) + EPS)
    keys = projected * scale * total
    groups, rows, _ = out.shape
    for group in range(groups):
        part = slice(group * rows, (group + 1) * rows)
        turned = turn(keys[part], cosine[...], sine[...])
        out[group] = jnp.where(info[3] == 0, turned, projected[part]).astype(BF16)


def query_kernel(count, groups, info, units, *refs):
    *sources, weights, out = refs
    place_weights(sources, info, count, weights, groups)
    out[...] = dot(units[...], weights[...])


def attention_setup(info, sources, qdoc_ref, kdoc_ref, qpos_ref, bias, keys, values):
    key_pos = lax.broadcasted_iota(jnp.int32, bias.shape, 1)
    allowed = (qdoc_ref[0] == kdoc_ref[0]) & (key_pos <= qpos_ref[...])
    bias[...] = jnp.where(allowed, 0.0, BIG_NEG)
    rows, count = bias.shape[0], len(sources) // 2
    for step in range(count):
        part = pl.ds(pl.multiple_of(info[4 + step] * rows, rows), rows)
        mine, other = sources[step][0], sources[count + step][0]
        keys[part, :] = jnp.where(info[3] == 0, mine, other)
        values[part, :] = jnp.where(info[3] == 0, other, mine)


def rotated(projected, gain, cosine, sine):
    scale = lax.rsqrt(jnp.mean(projected * projected, axis=-1, keepdims=True) + EPS)
    unit = projected * scale
    return scale, unit, turn(unit * gain, cosine, sine)


def windows_of(length, rows):
    count = length // rows
    return [max(count * part // 4, 1) * rows for part in (1, 2, 3, 4)]


def in_window(info, qdoc_ref, kdoc_ref, rows, work):
    length = kdoc_ref.shape[2]
    earlier = jnp.sum((kdoc_ref[0] < qdoc_ref[0, 0:1, 0:1]).astype(jnp.int32))
    blocks = info[0] + 1 - lax.div(earlier, rows)
    smaller = 0
    for size in windows_of(length, rows):
        start = pl.multiple_of(jnp.maximum(info[0] + 1 - size // rows, 0) * rows, rows)
        fits = (blocks > smaller) & (blocks <= size // rows)
        pl.when(fits)(functools.partial(work, start, size))
        smaller = size // rows


def head_columns(head):
    return slice(head * HEAD_DIM, (head + 1) * HEAD_DIM)


def forward_kernel(info, q_ref, qdoc_ref, kdoc_ref, qpos_ref, cos_ref, sin_ref, gain_ref, *refs):
    *sources, out_ref, total_ref, bias, keys, values = refs
    attention_setup(info, sources, qdoc_ref, kdoc_ref, qpos_ref, bias, keys, values)
    heads = q_ref.shape[1] // HEAD_DIM

    def work(start, size):
        part = pl.ds(start, size)
        for head in range(heads):
            at = head_columns(head)
            _, _, turned = rotated(q_ref[:, at], gain_ref[...], cos_ref[...], sin_ref[...])
            scores = dot_nt(turned.astype(BF16), keys[part, :]) * (SCALE * LOG2E) + bias[:, part]
            highest = jnp.max(scores, axis=-1, keepdims=True)
            exponent = jnp.exp2(scores - highest)
            total = jnp.sum(exponent, axis=-1, keepdims=True)
            probs = (exponent * (1.0 / total)).astype(BF16)
            out_ref[:, at] = dot(probs, values[part, :]).astype(BF16)
            total_ref[0, head] = highest + jnp.log2(total)

    in_window(info, qdoc_ref, kdoc_ref, bias.shape[0], work)


def backward_kernel(info, q_ref, qdoc_ref, kdoc_ref, qpos_ref, cos_ref, sin_ref, gain_ref, *refs):
    *sources, total_ref, grad_ref, dq_ref, kept_ref, sent_ref, dgain_ref, bias, key_rows, value_rows, dk_sum, dv_sum = refs
    seq = pl.program_id(0)
    attention_setup(info, sources, qdoc_ref, kdoc_ref, qpos_ref, bias, key_rows, value_rows)
    dk_sum[...] = jnp.zeros_like(dk_sum)
    dv_sum[...] = jnp.zeros_like(dv_sum)

    @pl.when(seq == 0)
    def _():
        dgain_ref[...] = jnp.zeros_like(dgain_ref)

    gain, cosine, sine = gain_ref[...], cos_ref[...], sin_ref[...]

    def work(start, size):
        part = pl.ds(start, size)
        keys, values = key_rows[part, :], value_rows[part, :]
        for head in range(q_ref.shape[1] // HEAD_DIM):
            at = head_columns(head)
            scale, unit, turned = rotated(q_ref[:, at], gain, cosine, sine)
            turned = turned.astype(BF16)
            scores = dot_nt(turned, keys) * (SCALE * LOG2E) + bias[:, part]
            probs = jnp.exp2(scores - total_ref[0, head])
            grad = grad_ref[:, at]
            grad_probs = dot_nt(grad, values)
            delta = jnp.sum(probs * grad_probs, axis=-1, keepdims=True)
            grad_scores = (probs * (grad_probs - delta)).astype(BF16)
            dv_sum[part, :] += dot_tn(probs.astype(BF16), grad)
            dk_sum[part, :] += dot_tn(grad_scores, turned)
            grad_turned = dot(grad_scores, keys) * SCALE
            grad_gained = turn(grad_turned, cosine, -sine)
            dgain_ref[...] += jnp.sum(grad_gained * unit, axis=0, keepdims=True)
            weighted = grad_gained * gain
            dq_ref[:, at] = (
                scale * (weighted - unit * jnp.mean(weighted * unit, axis=-1, keepdims=True))
            ).astype(BF16)

    in_window(info, qdoc_ref, kdoc_ref, bias.shape[0], work)
    shape = kept_ref.shape[:1] + kept_ref.shape[2:]
    dk, dv = dk_sum[...] * SCALE, dv_sum[...]
    kept_ref[:, 0] = jnp.where(info[3] == 0, dk, dv).astype(BF16).reshape(shape)
    sent_ref[:, 0] = jnp.where(info[3] == 0, dv, dk).astype(BF16).reshape(shape)


def attention_specs(rows, length, width, sources, first=0):
    specs = [
        pl.BlockSpec(memory_space=pltpu.SMEM),
        pl.BlockSpec((rows, width), lambda s: (first + s, 0)),
        pl.BlockSpec((1, rows, 1), lambda s: (first + s, 0, 0)),
        pl.BlockSpec((1, 1, length), lambda s: (first + s, 0, 0)),
        pl.BlockSpec((rows, 1), lambda s: (0, 0)),
        pl.BlockSpec((rows, HEAD_DIM), lambda s: (0, 0)),
        pl.BlockSpec((rows, HEAD_DIM), lambda s: (0, 0)),
        pl.BlockSpec((1, HEAD_DIM), lambda s: (0, 0)),
    ]
    return specs + [
        pl.BlockSpec((1, rows, HEAD_DIM), lambda s: (first + s, 0, 0)) for _ in sources
    ]


def attention_forward(operands, sources, sequences, heads, rows, length):
    pairs = sequences * heads * rows * length
    return pl.pallas_call(
        forward_kernel,
        grid=(sequences,),
        in_specs=attention_specs(rows, length, heads * HEAD_DIM, sources),
        out_specs=[
            pl.BlockSpec((rows, heads * HEAD_DIM), lambda s: (s, 0)),
            pl.BlockSpec((1, heads, rows, 1), lambda s: (s, 0, 0, 0)),
        ],
        out_shape=[
            shape_of((sequences * rows, heads * HEAD_DIM), BF16),
            shape_of((sequences, heads, rows, 1), F32),
        ],
        scratch_shapes=[
            pltpu.VMEM((rows, length), F32),
            pltpu.VMEM((length, HEAD_DIM), BF16),
            pltpu.VMEM((length, HEAD_DIM), BF16),
        ],
        compiler_params=pltpu.CompilerParams(vmem_limit_bytes=VMEM_LIMIT),
        cost_estimate=pl.CostEstimate(
            flops=1000, bytes_accessed=1000, transcendentals=0
        ),
    )(*operands, *sources)


def attention_backward(
    operands, sources, totals, grads, first, sequences, heads, rows, length, tokens=()
):
    pairs = sequences * heads * rows * length
    parts = length // rows
    key_value_spec = pl.BlockSpec((parts, 1, rows, HEAD_DIM), lambda s: (0, s, 0, 0))
    key_value_shape = shape_of((parts, sequences, rows, HEAD_DIM), BF16)
    count = len(operands) + len(sources) + 2

    def kernel(*refs):
        backward_kernel(*refs[:count], *refs[count + len(tokens) :])

    return pl.pallas_call(
        kernel,
        grid=(sequences,),
        in_specs=attention_specs(rows, length, heads * HEAD_DIM, sources, first)
        + [
            pl.BlockSpec((1, heads, rows, 1), lambda s: (first + s, 0, 0, 0)),
            pl.BlockSpec((rows, heads * HEAD_DIM), lambda s: (first + s, 0)),
        ]
        + [pl.BlockSpec(memory_space=pl.ANY)] * len(tokens),
        out_specs=[
            pl.BlockSpec((rows, heads * HEAD_DIM), lambda s: (s, 0)),
            key_value_spec,
            key_value_spec,
            pl.BlockSpec((1, HEAD_DIM), lambda s: (0, 0)),
        ],
        out_shape=[
            shape_of((sequences * rows, heads * HEAD_DIM), BF16),
            key_value_shape,
            key_value_shape,
            shape_of((1, HEAD_DIM), F32),
        ],
        scratch_shapes=[
            pltpu.VMEM((rows, length), F32),
            pltpu.VMEM((length, HEAD_DIM), BF16),
            pltpu.VMEM((length, HEAD_DIM), BF16),
            pltpu.VMEM((length, HEAD_DIM), F32),
            pltpu.VMEM((length, HEAD_DIM), F32),
        ],
        compiler_params=pltpu.CompilerParams(vmem_limit_bytes=VMEM_LIMIT),
        cost_estimate=pl.CostEstimate(
            flops=1000, bytes_accessed=1000, transcendentals=0
        ),
    )(*operands, *sources, totals, grads, *tokens)


def key_value_back_kernel(groups, info, key_proj, cosine, sine, gain, *refs):
    *terms, out, dgain = refs
    rows = terms[0].shape[1]
    total = jnp.zeros_like(dgain)
    for group in range(groups):
        grad = total_of([term[group] for term in terms])
        part = slice(group * rows, (group + 1) * rows)
        values_grad = grad
        grad = turn(grad, cosine[...], -sine[...])
        keys = key_proj[part]
        scale = lax.rsqrt(jnp.mean(keys * keys, axis=-1, keepdims=True) + EPS)
        unit = keys * scale
        total = total + jnp.sum(grad * unit, axis=0, keepdims=True)
        weighted = grad * gain[...]
        keys_grad = scale * (weighted - unit * jnp.mean(weighted * unit, axis=-1, keepdims=True))
        out[part, :] = jnp.where(info[3] == 0, keys_grad, values_grad).astype(BF16)
    dgain[...] = jnp.where(info[3] == 0, total, 0.0)


def out_sent_kernel(count, info, attended, *refs):
    *sources, sent, weights = refs

    def write(index, ref):
        start = pl.multiple_of(index * HEAD_DIM, HEAD_DIM)
        weights[pl.ds(start, HEAD_DIM), :] = ref[...]

    place_line(sources, info[0], count, write)
    out_parts(info, CORE, attended, weights, sent)


def out_kept_kernel(info, attended, weights, kept):
    out_parts(info, 0, attended, weights, kept)


def rows_for(info, flip, ref, rows):
    return [
        ref[pl.ds(pl.multiple_of((info[1] ^ (bits | flip)) * rows, rows), rows), :] for bits in FLIPS
    ]


def out_parts(info, flip, attended, weights, out):
    rows, width = out.shape[1:]
    left = jnp.concatenate(rows_for(info, flip, attended, rows), axis=0)
    for start in range(0, width, 512):
        part = slice(start, start + 512)
        out[:, :, part] = dot(left, weights[:, part]).astype(BF16).reshape(4, rows, 512)


def normed_grad_kernel(flip, info, query_grad, key_value_grad, query_weights, key_value_weights, units, out, sums):
    rows, width = out.shape[1:]
    left = jnp.concatenate(rows_for(info, flip, query_grad, rows), axis=0)
    other = jnp.concatenate(rows_for(info, flip, key_value_grad, rows), axis=0)
    unit = jnp.concatenate(rows_for(info, flip, units, rows), axis=0)
    for start in range(0, width, 512):
        part = slice(start, start + 512)
        grad = dot_nt(left, query_weights[part]) + dot_nt(other, key_value_weights[part])
        out[:, :, part] = grad.astype(BF16).reshape(4, rows, 512)
        sums[:, part] = jnp.sum(grad * unit[:, part].astype(F32), axis=0, keepdims=True)


def middle_kernel(info, own, across, aside, tokens, gain, middle, routed, scale_out):
    values = own[...] + across[...].astype(F32) + aside[...].astype(F32) + tokens[...].astype(F32)
    scale = lax.rsqrt(jnp.mean(values * values, axis=-1, keepdims=True) + EPS)
    middle[...] = values
    routed[...] = (values * scale * gain[...]).astype(BF16)
    scale_out[...] = scale


def gradient_spread_kernel(info, weights, *refs):
    *blocks, gathered, attended_grad = refs

    def write(row, ref):
        gathered[pl.ds(row, ref.shape[0]), :] = ref[...]

    place_plane(blocks, info[1], write)
    attended_grad[...] = dot_nt(gathered[...], weights[...]).astype(BF16)


def gates_of(token_rows, router, choices):
    logits = jnp.where(choices, dot(token_rows, router), BIG_NEG)
    exponent = jnp.where(choices, jnp.exp(logits - jnp.max(logits, axis=-1, keepdims=True)), 0.0)
    return exponent / jnp.maximum(jnp.sum(exponent, axis=-1, keepdims=True), 1e-30)


def gates_kernel(info, routed, router, picked, gates):
    gates[...] = gates_of(routed[...], router[...], picked[...][:, : gates.shape[1]] > 0.5)


def dispatch_kernel(steps, info, table, *refs):
    *blocks, out = refs
    members = out.shape[0]
    slots = table.shape[2] // members
    for at, step in enumerate(steps):
        block = block_of_step(blocks, info, steps, step)
        rows = dot_tn(table[info[4 + step]], block).astype(BF16)
        out[:, at * slots : (at + 1) * slots, :] = rows.reshape(members, slots, out.shape[2])


def dispatch_with_choices_kernel(steps, info, table, picked, *refs):
    *blocks, out = refs
    members, _, width = out.shape
    slots = table.shape[2] // members
    for at, step in enumerate(steps):
        place = table[info[4 + step]]
        part = slice(at * slots, (at + 1) * slots)
        rows = dot_tn(place, block_of_step(blocks, info, steps, step)).astype(BF16)
        choices = dot_tn(place, picked[info[4 + step]]).astype(BF16)
        model = rows.shape[1]
        out[:, part, :model] = rows.reshape(members, slots, model)
        out[:, part, model:] = choices.reshape(members, slots, width - model)


def combined(table, place, arrived, at):
    members, _, width = arrived.shape
    slots = table.shape[2] // members
    rows = arrived[:, at * slots : (at + 1) * slots, :].reshape(members * slots, width)
    return dot(table[place], rows)


def combine_kernel(first, info, table, arrived, *outs):
    for at, out in enumerate(outs):
        out[...] = combined(table, info[4 + first + at], arrived, at).astype(out.dtype)


def forward_kernel_of_parts(info, part, arrived, out):
    out[...] = (part[...].astype(F32) + arrived[...].astype(F32)).astype(BF16)


def combine_stacked_kernel(first, info, table, arrived, out):
    slots = table.shape[2] // arrived.shape[0]
    steps = arrived.shape[1] // slots
    for step in range(out.shape[0]):
        place = info[4 + step]
        if first <= step < first + steps:
            out[place] = combined(table, place, arrived, step - first).astype(BF16)
        else:
            out[place] = jnp.zeros(out.shape[1:], BF16)


def copy_kernel(info, value, out):
    out[...] = value[...]


def expert_prepare_kernel(info, arrived, down, grad_hidden):
    members, model = arrived.shape[0], down.shape[2]
    slots = grad_hidden.shape[0] // members
    rows = arrived[:, :, :model].reshape(members * slots, model)
    for start in range(0, FFE, 256):
        grad = dot_nt(rows, down[0, start : start + 256, :])
        grad_hidden[:, start : start + 256] = grad


def expert_kernel(experts, info, arrived, grad_hidden, dy_rows, router, weights, act, hidden_out, back):
    members, slots, width = arrived.shape
    rows = members * slots
    inputs = arrived[...].reshape(rows, width)
    chosen = dy_rows[:, :, width:].reshape(rows, -1)[:, :experts] > 0.5
    own = lax.broadcasted_iota(jnp.int32, (rows, experts), 1) == info[2]
    gate = jnp.sum(
        jnp.where(own, gates_of(inputs, router[...], chosen), 0.0), axis=-1, keepdims=True
    )
    grad_gate = jnp.zeros((rows, 1), F32)
    for start in range(0, FFE, 256):
        piece = slice(start, start + 256)
        lower = slice(FFE + start, FFE + start + 256)
        gate_in = dot(inputs, weights[0, :, piece])
        up_in = dot(inputs, weights[0, :, lower])
        grad_in = grad_hidden[:, piece]
        sigmoid = 1.0 / (1.0 + jnp.exp(-gate_in))
        silu = gate_in * sigmoid
        hidden = silu * up_in
        grad_gate = grad_gate + jnp.sum(hidden * grad_in, axis=-1, keepdims=True)
        scaled = grad_in * gate
        act[:, piece] = (scaled * up_in * (sigmoid + silu * (1.0 - sigmoid))).astype(BF16)
        act[:, lower] = (scaled * silu).astype(BF16)
        hidden_out[:, piece] = (hidden * gate).astype(BF16)
    for start in range(0, width, 512):
        piece = slice(start, start + 512)
        grad = dot_nt(act[...], weights[0, piece, :]).astype(BF16)
        back[:, :, piece] = grad.reshape(members, slots, 512)
    extra = back.shape[2] - width
    high = grad_gate.astype(BF16).astype(F32)
    lane = lax.broadcasted_iota(jnp.int32, (rows, extra), 1)
    columns = jnp.where(lane == info[2], high, 0.0)
    columns = columns + jnp.where(lane == info[2] + experts, grad_gate - high, 0.0)
    back[:, :, width:] = columns.astype(BF16).reshape(members, slots, extra)


def results_kernel(info, down, hidden, out):
    members, slots, width = out.shape
    for start in range(0, width, 512):
        piece = slice(start, start + 512)
        rows = dot(hidden[...], down[0, :, piece]).astype(BF16)
        out[:, :, piece] = rows.reshape(members, slots, 512)


def gate_up_grad(rows, acts, tokens):
    count, groups = rows[0].shape[0], len(rows)
    width, columns = rows[0].shape[1], acts[0].shape[1]
    tile = 512

    def kernel(*refs):
        out = refs[-1]
        total = dot_tn(refs[0][...], refs[groups][...])
        for group in range(1, groups):
            total = total + dot_tn(refs[group][...], refs[groups + group][...])
        out[0] = total

    return pl.pallas_call(
        kernel,
        grid=(width // tile,),
        in_specs=[pl.BlockSpec((count, tile), lambda i: (0, i))] * groups
        + [pl.BlockSpec((count, columns), lambda i: (0, 0))] * groups
        + [pl.BlockSpec(memory_space=pl.ANY)] * len(tokens),
        out_specs=pl.BlockSpec((1, tile, columns), lambda i: (0, i, 0)),
        out_shape=shape_of((1, width, columns), F32),
        compiler_params=pltpu.CompilerParams(vmem_limit_bytes=VMEM_LIMIT),
        cost_estimate=pl.CostEstimate(
            flops=1000, bytes_accessed=1000, transcendentals=0
        ),
    )(*rows, *acts, *tokens)


def down_grad(hiddens, arrived, model, tokens):
    groups, tile = len(hiddens), 256
    count = hiddens[0].shape[0]

    def kernel(*refs):
        total = 0.0
        for left, right in zip(refs[:groups], refs[groups : 2 * groups]):
            total = total + dot_tn(left[...], right[:, :, :model].reshape(count, model))
        refs[-1][0] = total

    return pl.pallas_call(
        kernel,
        grid=(FFE // tile,),
        in_specs=[pl.BlockSpec((count, tile), lambda i: (0, i))] * groups
        + [pl.BlockSpec(arrived[0].shape, lambda i: (0, 0, 0))] * groups
        + [pl.BlockSpec(memory_space=pl.ANY)] * len(tokens),
        out_specs=pl.BlockSpec((1, tile, model), lambda i: (0, i, 0)),
        out_shape=shape_of((1, FFE, model), F32),
        compiler_params=pltpu.CompilerParams(vmem_limit_bytes=VMEM_LIMIT),
        cost_estimate=pl.CostEstimate(flops=1000, bytes_accessed=1000, transcendentals=0),
    )(*hiddens, *arrived, *tokens)


def token_back_kernel(info, gates, router, middle, scale, gain, cotangent, routed, *refs):
    *terms, grad_middle, grad_branch, grad_gain, grad_router = refs
    width = middle.shape[1]
    experts = gates.shape[1]
    total = total_of([term[...] for term in terms])
    extra = total[:, width:]
    grad_gates = extra[:, :experts] + extra[:, experts : 2 * experts]
    values = gates[...]
    grad_logits = values * (grad_gates - jnp.sum(values * grad_gates, axis=-1, keepdims=True))
    grad_logits = grad_logits.astype(BF16)
    grad_routed = total[:, :width] + dot_nt(grad_logits, router[...])
    unit = middle[...] * scale[...]
    grad_gain[...] = jnp.sum(grad_routed * unit, axis=0, keepdims=True)
    weighted = grad_routed * gain[...]
    grad = cotangent[...].astype(F32) + scale[...] * (
        weighted - unit * jnp.mean(weighted * unit, axis=-1, keepdims=True)
    )
    grad_middle[...] = grad
    grad_branch[...] = grad.astype(BF16)
    grad_router[...] = dot_tn(routed[...], grad_logits)


def input_grad_kernel(info, own, across, aside, tokens, gain, grad_middle, out):
    weighted = (own[...] + across[...].astype(F32) + aside[...].astype(F32)) * gain[...]
    values = tokens[...].astype(F32)
    scale = lax.rsqrt(jnp.mean(values * values, axis=-1, keepdims=True) + EPS)
    unit = values * scale
    out[...] = grad_middle[...] + scale * (
        weighted - unit * jnp.mean(weighted * unit, axis=-1, keepdims=True)
    )


def mixed_kernel(info, middle, *refs):
    *terms, out = refs
    out[...] = (middle[...] + total_of([term[...] for term in terms])).astype(BF16)


def unpack_weights_kernel(rep_size, info, arrived, queries, keys, values):
    members, _, columns = arrived.shape
    heads = columns // HEAD_DIM - 1
    for member in range(members):
        group, rep = member // rep_size, member % rep_size
        for j in range(heads):
            head = group * heads * rep_size + j * rep_size + rep
            queries[:, head * HEAD_DIM : (head + 1) * HEAD_DIM] = arrived[
                member, :, j * HEAD_DIM : (j + 1) * HEAD_DIM
            ].astype(F32)
        out = values if rep else keys
        out[:, group * HEAD_DIM : (group + 1) * HEAD_DIM] = arrived[
            member, :, heads * HEAD_DIM :
        ].astype(F32)


def body(
    tokens,
    segments,
    routes,
    priority,
    w_query,
    key_matrix,
    value_matrix,
    w_out,
    w_router,
    attn_gain,
    moe_gain,
    query_gain,
    key_norm_weight,
    w_gate_up,
    w_down,
    cotangent,
):
    own_rows, width = tokens.shape[1], tokens.shape[2]
    length = segments.shape[1]
    dp_size, seq_size, rep_size = (lax.axis_size(name) for name in ALL)
    devices = dp_size * seq_size * rep_size
    members = dp_size * rep_size
    dp_at, seq_at, rep_at = (lax.axis_index(name) for name in ALL)
    experts = devices * w_gate_up.shape[0]
    capacity = own_rows * TOPK // experts
    plane_slots = members * capacity
    depth = w_router.shape[0]
    heads = QUERY_HEADS // members
    head_width = heads * HEAD_DIM
    rows = rep_size * own_rows
    plane_rows = members * own_rows
    chunk = members * depth
    extra = -(-2 * experts // LANES) * LANES
    entry = jnp.arange(4 + seq_size, dtype=jnp.int32)
    info = (entry - 4) ^ seq_at if seq_size == 4 else entry - 4
    places = (seq_at, lax.axis_index(PLANE), lax.axis_index(ALL), rep_at)
    for index, place in enumerate(places):
        info = jnp.where(entry == index, place, info)
    own_tokens, own_cotangent = tokens[0], cotangent[0]

    token_blocks = plane_gather(own_tokens)
    query_part, key_value_part = pack_weights(
        w_query, key_matrix, value_matrix, members, rep_size, heads
    )
    cotangent_sources = [lax.all_gather(own_cotangent, "seq")]
    query_part = swap(after(query_part, token_blocks[1], token_blocks[4]), PLANE)
    router_rows = w_router.size // LANES
    own_documents = lax.dynamic_slice_in_dim(segments, (seq_at * rep_size + rep_at) * own_rows, own_rows, 1)
    packet = run(
        functools.partial(packet_kernel, rep_size),
        [shape_of((devices, depth + PACKET_ROWS + router_rows, LANES), BF16)],
        info,
        key_value_part,
        w_router.reshape(router_rows, LANES),
        routes[0],
        priority,
        own_documents,
        moe_gain[None],
        query_gain[None],
        key_norm_weight[None],
        attn_gain[None],
        tokens=(query_part, *token_blocks[5:7]),
    )[0]
    packet = swap(packet, ALL)
    arrival = packet
    router = packet[:, depth + PACKET_ROWS :].reshape(devices, depth, experts)
    router = router.reshape(width, experts)
    packet = packet[:, depth : depth + PACKET_ROWS]
    query_part = after(query_part.reshape(chunk, head_width), arrival, cotangent_sources[0])
    query_sources = [lax.all_gather(query_part, "seq")]

    packet = packet.astype(F32)
    documents = packet[:, DOCUMENT_ROW].reshape(dp_size, length).astype(jnp.int32)
    second_gain = packet[:, MOE_GAIN_ROW, :depth].reshape(1, width)
    meta = packet.reshape(dp_size, seq_size, rep_size, PACKET_ROWS, LANES)
    meta = pick(pick(meta, dp_at), rep_at, 1).astype(jnp.int32)
    choice_ids, priority_rank = meta[:, :TOPK], meta[:, PRIORITY_ROW]
    expert_lanes = -(-experts // LANES) * LANES
    expert_ids = jnp.arange(expert_lanes, dtype=jnp.int32)
    picked = jnp.any(choice_ids[:, :, :, None] == expert_ids, axis=1)
    earlier = (priority_rank[:, None, :] < priority_rank[:, :, None]).astype(BF16)
    plane_picked = pick(
        picked[:, :, :experts].reshape(seq_size, own_rows, dp_size, seq_size, rep_size), seq_at, 3
    ).reshape(seq_size, own_rows, members)
    slot_index = jnp.einsum(
        "bts,bse->bte", earlier, plane_picked.astype(BF16), preferred_element_type=F32
    ).astype(jnp.int32)
    slot_ids = jnp.arange(capacity, dtype=jnp.int32)
    table = plane_picked[..., None] & (slot_index[..., None] == slot_ids)
    table = table.reshape(seq_size, own_rows, plane_slots).astype(BF16)
    picked = picked.astype(BF16)

    units, first_gain = run(
        functools.partial(normalize_kernel, depth),
        [shape_of((plane_rows, width), BF16), shape_of((1, width), F32)],
        info,
        arrival,
        *token_blocks,
    )
    positions = seq_at * rows + jnp.arange(rows, dtype=jnp.int32)
    frequency = THETA ** (-2.0 * jnp.arange(HEAD_DIM // 2, dtype=F32) / HEAD_DIM)
    angles = positions.astype(F32)[:, None] * jnp.concatenate([frequency, frequency])[None, :]
    sign = jnp.where(jnp.arange(HEAD_DIM) < HEAD_DIM // 2, -1.0, 1.0)
    cosine, sine = jnp.cos(angles), jnp.sin(angles) * sign[None, :]
    key_proj, key_value_rows, key_value_weights, key_norm_gain, query_norm_gain = run(
        key_value_kernel,
        [
            shape_of((plane_rows, HEAD_DIM), F32),
            shape_of((dp_size, rows, HEAD_DIM), BF16),
            shape_of((width, HEAD_DIM), BF16),
            shape_of((1, HEAD_DIM), F32),
            shape_of((1, HEAD_DIM), F32),
        ],
        info,
        units,
        arrival,
        cosine,
        sine,
        flops=2 * plane_rows * width * HEAD_DIM,
    )
    mine = line_steps(line_gather(key_value_rows, seq_size))
    other = [plane_move(block, SIDE) for block in mine[:-1]]
    query_weights, query_proj = run(
        functools.partial(query_kernel, seq_size, dp_size),
        [shape_of((width, head_width), BF16), shape_of((plane_rows, head_width), F32)],
        info,
        units,
        *query_sources,
        flops=2 * plane_rows * width * head_width,
    )
    key_values = mine + other + [plane_move(mine[-1], SIDE)]

    whole_heads = w_out.shape[0] == HEAD_DIM
    if whole_heads:
        held_w_out = run(
            copy_kernel, [shape_of(w_out.shape, BF16)], info, w_out, tokens=mine[-1:]
        )[0]
        out_sources = [lax.all_gather(held_w_out, "seq")]
    else:
        group = lax.all_gather(w_out, ("seq", "rep"), axis=0, tiled=True)
        group = group.reshape(heads, rep_size, HEAD_DIM, width)
        out_sources = [pick(group, rep_at, 1)]

    steps = list(range(seq_size))
    groups = [steps[: seq_size // 2], steps[seq_size // 2 :]]
    group_slots = len(groups[0]) * capacity
    group_rows = members * group_slots
    group_rows = members * group_slots
    def send_cotangent(group, held, *late):
        outgoing = run(
            functools.partial(dispatch_with_choices_kernel, group),
            [shape_of((members, group_slots, width + expert_lanes), BF16)],
            info,
            table,
            picked,
            *cotangent_sources,
            tokens=held,
            flops=2 * own_rows * len(group) * plane_slots * width,
        )[0]
        return swap(after(outgoing, *late) if late else outgoing, PLANE)

    dy_rows = [send_cotangent(groups[0], (key_value_rows,))]
    dy_rows.append(
        send_cotangent(groups[1], mine[2:3], dy_rows[0], query_proj, *key_values[seq_size:])
    )
    grad_hidden = [
        run(
            expert_prepare_kernel,
            [shape_of((group_rows, FFE), F32)],
            info,
            rows_,
            w_down,
            filler=True,
        )[0]
        for rows_ in dy_rows
    ]

    query_doc = lax.dynamic_slice_in_dim(documents, seq_at * rows, rows, axis=1)
    operands = (
        info,
        query_proj,
        query_doc[:, :, None],
        documents[:, None, :],
        positions[:, None],
        cosine,
        sine,
        query_norm_gain,
    )
    attended, totals = attention_forward(operands, key_values, dp_size, heads, rows, length)
    parts_shape = shape_of((4, own_rows, width), BF16)
    part_flops = 8 * own_rows * head_width * width
    sent, out_weights = run(
        functools.partial(out_sent_kernel, heads),
        [parts_shape, shape_of((head_width, width), BF16)],
        info,
        attended,
        *out_sources,
        tokens=(dy_rows[1],),
        flops=part_flops,
    )
    kept = run(out_kept_kernel, [parts_shape], info, attended, out_weights, flops=part_flops)[0]
    row_f32, row_bf16 = shape_of((own_rows, width), F32), shape_of((own_rows, width), BF16)
    *plane_terms, _ = plane_reduce(info, sent, kept)
    middle, routed, scale_second = run(
        middle_kernel,
        [row_f32, row_bf16, shape_of((own_rows, 1), F32)],
        info,
        *plane_terms,
        own_tokens,
        second_gain,
    )

    if seq_size == 4:
        half_rows = own_rows // 2
        second = [line_move(routed[:half_rows], 2), line_move(routed[half_rows:], 2)]
        routed_far = second + [line_move(piece, 1) for piece in second]
        routed_near = [routed, line_move(routed, 1)]
        token = second[:1]
    else:
        routed_near = routed_far = line_gather(routed, seq_size)
        token = ()
    own_picked = pick(picked, seq_at)
    gates = run(
        gates_kernel, [shape_of((own_rows, experts), F32)], info, routed, router, own_picked
    )[0]
    arrived = []
    for group, routed_sources in zip(groups, (routed_near, routed_far)):
        outgoing = run(
            functools.partial(dispatch_kernel, group),
            [shape_of((members, group_slots, width), BF16)],
            info,
            table,
            *routed_sources,
            tokens=token,
            flops=2 * own_rows * len(group) * plane_slots * width,
        )[0]
        arrived.append(swap(outgoing, PLANE))
        token = arrived[-1:]
    worked, token = {}, ()
    for at in (1, 0):
        worked[at] = run(
            functools.partial(expert_kernel, experts),
            [
                shape_of((group_rows, 2 * FFE), BF16),
                shape_of((group_rows, FFE), BF16),
                shape_of((members, group_slots, width + extra), BF16),
            ],
            info,
            arrived[at],
            grad_hidden[at],
            dy_rows[at],
            router,
            w_gate_up,
            tokens=token,
            flops=8 * group_rows * width * FFE,
        )
        token = (worked[at][2],)
    acts, hiddens, backs = zip(worked[0], worked[1])

    def combine(at, rows_, columns, held=()):
        group = groups[at]
        return run(
            functools.partial(combine_kernel, group[0]),
            [shape_of((own_rows, columns), BF16)] * len(group),
            info,
            table,
            rows_,
            tokens=held,
            flops=2 * own_rows * len(group) * plane_slots * columns,
        )

    def send_groups(near, far):
        if seq_size != 4:
            return line_reduce(jnp.stack(list(near) + list(far)), seq_at, seq_size)
        return [near[0], line_move(far[0], 2), line_move(near[1], 1)]

    pairs_far, pairs_near = swap(backs[1], PLANE), swap(backs[0], PLANE)
    far_parts = combine(1, pairs_far, width + extra)
    grad_down = down_grad(hiddens, dy_rows, width, far_parts[:1])
    if seq_size == 4:
        far_parts = run(
            forward_kernel_of_parts,
            [shape_of((own_rows, width + extra), BF16)],
            info,
            far_parts[0],
            line_move(far_parts[1], 1),
            tokens=(grad_down,),
        )
    results = [
        run(
            results_kernel,
            [shape_of((members, group_slots, width), BF16)],
            info,
            w_down,
            hidden,
            tokens=far_parts[:1],
            filler=True,
        )[0]
        for hidden in hiddens
    ]
    near_parts = combine(0, pairs_near, width + extra, far_parts[:1])
    pair_terms = send_groups(near_parts, far_parts)
    grad_gate_up = gate_up_grad(
        [rows_.reshape(group_rows, width) for rows_ in arrived], acts, near_parts[:1]
    )
    results_far = swap(results[1], PLANE)
    grad_middle, grad_branch, grad_moe_gain, grad_router = run(
        token_back_kernel,
        [row_f32, row_bf16, shape_of((1, width), F32), shape_of((width, experts), F32)],
        info,
        gates,
        router,
        middle,
        scale_second,
        second_gain,
        own_cotangent,
        routed,
        *pair_terms,
        tokens=(grad_gate_up, results_far, grad_down, results[0]),
    )
    branch_blocks = plane_gather(grad_branch)
    far_stacked = run(
        functools.partial(combine_stacked_kernel, groups[1][0]),
        [shape_of((seq_size, own_rows, width), BF16)],
        info,
        table,
        results_far,
        tokens=(grad_middle,),
        flops=2 * own_rows * len(groups[1]) * plane_slots * width,
    )[0]
    grad_branch, grad_attended = run(
        gradient_spread_kernel,
        [shape_of((plane_rows, width), BF16), shape_of((plane_rows, head_width), BF16)],
        info,
        out_weights,
        *branch_blocks,
        tokens=(far_stacked,),
        flops=2 * plane_rows * head_width * width,
    )
    far_sum = lax.psum_scatter(far_stacked, "seq", scatter_dimension=0, tiled=False)
    results_near = swap(after(results[0], grad_attended), PLANE)
    half = dp_size // 2
    first_call = attention_backward(
        operands, key_values, totals, grad_attended, 0, half, heads, rows, length
    )
    grad_out = dot_tn(after(attended, first_call[0]), grad_branch).astype(BF16)
    second_call = attention_backward(
        operands,
        key_values,
        totals,
        grad_attended,
        half,
        half,
        heads,
        rows,
        length,
        (grad_out,),
    )
    query_grads, kept_grads, sent_grads, gain_grads = zip(first_call, second_call)
    if whole_heads:
        grad_out = grad_out.reshape(heads, HEAD_DIM, width)
        grad_out = lax.psum_scatter(grad_out, "seq", scatter_dimension=0, tiled=False)
    else:
        group = jnp.zeros((heads, rep_size, HEAD_DIM, width), F32)
        group = lax.dynamic_update_index_in_dim(
            group, grad_out.reshape(heads, HEAD_DIM, width).astype(F32), rep_at, 1
        )
        grad_out = lax.psum_scatter(
            group.reshape(heads * rep_size * HEAD_DIM, width),
            ("seq", "rep"),
            scatter_dimension=0,
            tiled=True,
        )
    if seq_size == 4:
        near_terms = near_parts = combine(0, results_near, width, second_call[:1])
    else:
        near_terms = [
            lax.psum_scatter(
                run(
                    functools.partial(combine_stacked_kernel, 0),
                    [shape_of((seq_size, own_rows, width), BF16)],
                    info,
                    table,
                    results_near,
                )[0],
                "seq",
                scatter_dimension=0,
                tiled=False,
            )
        ]
    grad_query_proj = jnp.concatenate(query_grads)
    grad_query_gain = gain_grads[0] + gain_grads[1]
    kept_grads = [
        kept.astype(F32) + plane_move(sent, SIDE).astype(F32)
        for kept, sent in zip(kept_grads, (sent_grads[0], after(sent_grads[1], results_near, far_sum)))
    ]
    grad_key_value = jnp.concatenate(kept_grads, axis=1).astype(BF16)
    key_value_terms = line_reduce(grad_key_value, seq_at, seq_size)
    grad_key_value, grad_key_gain = run(
        functools.partial(key_value_back_kernel, dp_size),
        [shape_of((plane_rows, HEAD_DIM), BF16), shape_of((1, HEAD_DIM), F32)],
        info,
        key_proj,
        cosine,
        sine,
        key_norm_gain,
        *key_value_terms,
        tokens=near_parts[:1],
    )

    def weight_parts(left, grad):
        parts = dot_tn(left, grad).astype(BF16)
        parts = parts.reshape(dp_size, seq_size, rep_size * depth, grad.shape[1])
        return parts.transpose(1, 0, 2, 3)

    query_parts = weight_parts(units, grad_query_proj)

    def normed_grad(flip, held=()):
        return run(
            functools.partial(normed_grad_kernel, flip),
            [parts_shape, shape_of((1, width), F32)],
            info,
            grad_query_proj,
            grad_key_value,
            query_weights,
            key_value_weights,
            units,
            tokens=held,
            flops=8 * own_rows * (head_width + HEAD_DIM) * width,
        )

    sent, sent_sums = normed_grad(CORE, (grad_out,))
    kept, kept_sums = normed_grad(0)
    weights_total = lax.psum_scatter(
        jnp.concatenate([query_parts, weight_parts(units, grad_key_value)], axis=-1),
        "seq",
        scatter_dimension=0,
        tiled=False,
    ).reshape(members, depth, head_width + HEAD_DIM)
    *plane_terms, mark = plane_reduce(info, sent, kept)

    pieces = (grad_router, sent_sums + kept_sums, grad_moe_gain, grad_query_gain, grad_key_gain)
    small = jnp.concatenate([piece.reshape(devices, -1) for piece in pieces], axis=-1)
    small = jnp.sum(swap(small, ALL), axis=0)
    bounds = [0]
    for piece in pieces:
        bounds.append(bounds[-1] + piece.size // devices)
    small = [small[a:b] for a, b in zip(bounds[:-1], bounds[1:])]
    weights_arrived = swap(weights_total, PLANE)
    grad_query, grad_key, grad_value = run(
        functools.partial(unpack_weights_kernel, rep_size),
        [shape_of(w_query.shape, F32)] + [shape_of(key_matrix.shape, F32)] * 2,
        info,
        weights_arrived,
    )
    if seq_size == 4:
        near_terms = [near_terms[0], line_move(after(near_terms[1], weights_total), 1)]
    result_terms = near_terms + [far_sum.reshape(own_rows, width)]
    mixed = run(
        mixed_kernel, [row_bf16], info, middle, *result_terms, tokens=plane_terms[1:]
    )[0]
    input_grad = run(
        input_grad_kernel,
        [row_f32],
        info,
        *plane_terms,
        own_tokens,
        first_gain,
        grad_middle,
    )[0]

    return (
        mixed[None],
        input_grad[None],
        grad_query,
        grad_key,
        grad_value,
        grad_out.astype(F32),
        small[0].reshape(depth, experts),
        small[1] / attn_gain.astype(F32),
        small[2],
        small[3],
        small[4],
        grad_gate_up,
        grad_down,
    )


def solution(mesh):
    tokens_spec = P("dp", ("seq", "rep"), None)
    rows_spec = P(ALL, None)
    vector_spec = P(ALL)
    expert_spec = P(ALL, None, None)
    return jax.shard_map(
        body,
        mesh=mesh,
        in_specs=(
            (tokens_spec, P("dp", None), tokens_spec, P("dp", ("seq", "rep")))
            + (rows_spec,) * 5
            + (vector_spec,) * 4
            + (expert_spec, expert_spec, tokens_spec)
        ),
        out_specs=(
            (tokens_spec, tokens_spec)
            + (rows_spec,) * 5
            + (vector_spec,) * 4
            + (expert_spec, expert_spec)
        ),
        check_vma=False,
    )
```
